32 devices in a mesh: seq: 16 (over z, y, x), head: 2 (over core).
Axes of the slice: x: 2, y: 2, z: 4, core: 2. Of those that a mesh axis runs over, the one named last changes fastest.
Arguments:
- hidden_in: bfloat16 [16384, 768], P('seq'), may hold values from -6 to 6
- norm_gain: float32 [768], replicated, may hold values from 0.5 to 1.5
- gate_proj: bfloat16 [768, 1536], P(None, 'head'), may hold values from -0.21875 to 0.21875
- value_proj: bfloat16 [768, 1536], P(None, 'head'), may hold values from -0.21875 to 0.21875
- state_proj: bfloat16 [768, 256], replicated, may hold values from -0.21875 to 0.21875
- step_proj: bfloat16 [2, 768, 24], P(None, None, 'head'), may hold values from -0.21875 to 0.21875
- conv_value: float32 [4, 1536], P(None, 'head'), may hold values from -3 to 3
- conv_state: float32 [4, 256], replicated, may hold values from -3 to 3
- step_bias: float32 [2, 24], P(None, 'head'), may hold values from -4 to -3
- decay_log: float32 [24], P('head'), may hold values from -12 to 0
- skip_scale: float32 [24], P('head'), may hold values from 0.5 to 2
- gate_gain: float32 [1536], P('head'), may hold values from 0.5 to 1.5
- out_proj: bfloat16 [1536, 768], P('head'), may hold values from -0.15625 to 0.15625
- lengths: int32 [9], replicated, may hold values from 1024 to 4096, as said below
- cotangent: bfloat16 [16384, 768], P('seq'), may hold values from -6 to 6
Outputs:
- block_out: bfloat16 [16384, 768], P('seq')
- grad_hidden: float32 [16384, 768], P('seq')
- grad_norm_gain: float32 [768], replicated
- grad_gate_proj: float32 [768, 1536], P(None, 'head')
- grad_value_proj: float32 [768, 1536], P(None, 'head')
- grad_state_proj: float32 [768, 256], replicated
- grad_step_proj: float32 [2, 768, 24], P(None, None, 'head')
- grad_conv_value: float32 [4, 1536], P(None, 'head')
- grad_conv_state: float32 [4, 256], replicated
- grad_step_bias: float32 [2, 24], P(None, 'head')
- grad_decay_log: float32 [24], P('head')
- grad_skip_scale: float32 [24], P('head')
- grad_gate_gain: float32 [1536], P('head')
- grad_out_proj: float32 [1536, 768], P('head')
The draws below stay inside these ranges and needn't reach their ends.
Inputs may be any that keep to these rules, and one draw needn't show every extreme that they name: 9 lengths that sum to 16384; exactly one of them is 4096.
All inputs are finite; a program needn't handle non-finite values.
Results may differ from the reference program's by a relative error of at most 0.012.
The reference program's roundings to bfloat16 on the way count: a program that leaves them out, or rounds other values in their place, can miss the bound.
Values may be sent and summed in bfloat16 or wider, within the bound.
A program may use at most 320 MiB of HBM per device.

```python
import math
import jax
import jax.numpy as jnp
from jax import lax

D = 768
INNER = 1536
HDIM = 64
NS = 64
HEADS = 24
GROUP = 256
LEN_MID = 1536
LEN_MOST = 4096
TOKENS = 16384
NSEQ = 9


def draw_lengths(key, part):
    key = jax.random.fold_in(key, 11)
    jitter_key = jax.random.fold_in(key, 1)
    long_key = jax.random.fold_in(key, 2)
    spread = LEN_MID // 6
    places = jnp.arange(NSEQ, dtype=jnp.int32)
    long_index = jax.random.randint(long_key, (), 0, NSEQ - 1).astype(jnp.int32)
    jitter = jax.random.randint(jitter_key, (NSEQ,), -spread, spread + 1).astype(jnp.int32)
    jitter = jnp.where(places == 0, 0, jitter).astype(jnp.int32)
    jitter_long = jnp.sum(jnp.where(places == long_index, jitter, 0)).astype(jnp.int32)
    jitter = jnp.where(places == long_index + 1, jitter_long, jitter).astype(jnp.int32)
    starts = places * LEN_MID + jitter + (LEN_MOST - LEN_MID) * (places > long_index).astype(jnp.int32)
    ends = jnp.concatenate([starts[1:], jnp.full((1,), TOKENS, jnp.int32)])
    return (ends - starts).astype(jnp.int32)


def draw_decay_log(key, part):
    key = jax.random.fold_in(key, 7)
    uniform_draw = jax.random.uniform(key, (HEADS,), jnp.float32)
    lowest = math.log(1.0 / LEN_MOST)
    highest = math.log(0.8)
    return (lowest + (highest - lowest) * uniform_draw).astype(jnp.float32)


def level_of(rng, shape, pieces, low, largest):
    loudness, own = 1.0, jax.random.fold_in(rng, 6)
    for position, blocks in pieces:
        heights = jnp.exp(jax.random.uniform(jax.random.fold_in(own, position), (blocks,), jnp.float32, low / len(pieces), largest / len(pieces)))
        loudness = loudness * jnp.repeat(heights, shape[position] // blocks).reshape([-1 if axis == position else 1 for axis in range(len(shape))])
    return loudness


def bell_draw(stream_key, extent, scale, bound, shards=(), kind=jnp.bfloat16):
    level = level_of(stream_key, extent, shards, -0.22, 0.18) if shards else 1.0
    values = jax.random.normal(stream_key, extent, jnp.float32) * scale * level
    return jnp.minimum(jnp.maximum(values, -bound), bound).astype(kind)


def setup_inputs(seed: int = 0) -> dict:
    seeds = jax.random.split(jax.random.key(seed), 16)
    hidden_in = bell_draw(seeds[0], (TOKENS, D), 1.0, 6.0, ((0, 16),))
    norm_gain = jnp.clip(1.0 + 0.1 * jax.random.normal(seeds[1], (D,), jnp.float32), 0.5, 1.5)
    gate_proj = bell_draw(seeds[2], (D, INNER), D ** -0.5, 0.21875, ((1, 2),))
    value_proj = bell_draw(seeds[3], (D, INNER), D ** -0.5, 0.21875, ((1, 2),))
    state_proj = bell_draw(seeds[4], (D, 4 * NS), D ** -0.5, 0.21875)
    step_proj = bell_draw(seeds[5], (2, D, HEADS), D ** -0.5, 0.21875, ((2, 2),))
    conv_value = bell_draw(seeds[6], (4, INNER), 0.5, 3.0, ((1, 2),), jnp.float32)
    conv_state = bell_draw(seeds[7], (4, 4 * NS), 0.5, 3.0, (), jnp.float32)
    step_bias = jnp.clip(-4.0 + 1.0 * jax.random.uniform(seeds[8], (2, HEADS), jnp.float32) ** level_of(seeds[8], (2, HEADS), ((1, 2),), -0.2, 0.2), -4.0, -3.0)
    decay_log = draw_decay_log(jax.random.fold_in(seeds[15], 71), 0)
    skip_scale = jnp.clip(0.5 + 1.5 * jax.random.uniform(seeds[10], (HEADS,), jnp.float32) ** level_of(seeds[10], (HEADS,), ((0, 2),), -0.2, 0.2), 0.5, 2.0)
    gate_gain = jnp.clip(1.0 + 0.1 * jax.random.normal(seeds[11], (INNER,), jnp.float32), 0.5, 1.5)
    out_proj = bell_draw(seeds[12], (INNER, D), INNER ** -0.5, 0.15625, ((0, 2),))
    lengths = draw_lengths(jax.random.fold_in(seeds[15], 71), 0)
    cotangent = bell_draw(seeds[14], (TOKENS, D), 1.0, 6.0, ((0, 16),))
    return {"hidden_in": hidden_in, "norm_gain": norm_gain, "gate_proj": gate_proj, "value_proj": value_proj, "state_proj": state_proj, "step_proj": step_proj, "conv_value": conv_value, "conv_state": conv_state, "step_bias": step_bias, "decay_log": decay_log, "skip_scale": skip_scale, "gate_gain": gate_gain, "out_proj": out_proj, "lengths": lengths, "cotangent": cotangent}


HIGHEST = lax.Precision.HIGHEST
EPSILON = 1e-05

@jax.custom_vjp
def low(v):
    return lax.optimization_barrier(v.astype(jnp.bfloat16)).astype(jnp.float32)

@jax.custom_vjp
def low_back(v):
    return v

def low_keep(v):
    return (low(v), None)

def low_pass(kept, grad):
    return (grad,)

def back_keep(v):
    return (v, None)

def back_low(kept, grad):
    return (low(grad),)
low.defvjp(low_keep, low_pass)
low_back.defvjp(back_keep, back_low)

def group_step(carry_in, block_data):
    carried, seg_prev = carry_in
    values, step_size, log_decay, entry_map, read_map, segment = block_data
    running = jnp.cumsum(log_decay, axis=0)
    before = running - log_decay
    length = segment.shape[0]
    positions = jnp.arange(length)
    same_seq = (segment[:, None] == segment[None, :]) & (positions[:, None] > positions[None, :])
    chosen = same_seq[:, :, None]
    decay_matrix = jnp.where(chosen, jnp.exp(jnp.where(chosen, before[:, None, :] - running[None, :, :], 0.0)), 0.0)
    scores = jnp.dot(read_map, entry_map.T, precision=HIGHEST)
    weight = decay_matrix * scores[:, :, None] * step_size[None, :, :]
    inner_y = jnp.einsum('tsh,shp->thp', weight, values, precision=HIGHEST)
    keep_rows = (segment == seg_prev).astype(jnp.float32)
    from_state = jnp.einsum('tn,hpn->thp', read_map, carried, precision=HIGHEST)
    output = inner_y + (keep_rows[:, None] * jnp.exp(before))[:, :, None] * from_state
    last_seg = segment[-1]
    tail_weight = jnp.where((segment == last_seg)[:, None], jnp.exp(running[-1][None, :] - running), 0.0) * step_size
    passed = jnp.where(last_seg == seg_prev, jnp.exp(running[-1]), 0.0)
    new_state = passed[:, None, None] * carried + jnp.einsum('sh,shp,sn->hpn', tail_weight, values, entry_map, precision=HIGHEST)
    return ((new_state, last_seg), output)

def scan_ssd(values, step_size, log_decay, entry_map, read_map, segment):
    total_rows = values.shape[0]
    num_blocks = total_rows // GROUP

    def to_blocks(array):
        return array.reshape((num_blocks, GROUP) + array.shape[1:])
    start_state = (jnp.zeros((HEADS, HDIM, NS), jnp.float32), jnp.int32(-1))
    carry_out, outputs = lax.scan(jax.checkpoint(group_step), start_state, (to_blocks(values), to_blocks(step_size), to_blocks(log_decay), to_blocks(entry_map), to_blocks(read_map), to_blocks(segment)))
    return outputs.reshape(total_rows, HEADS, HDIM)

def reference(hidden_in, norm_gain, gate_proj, value_proj, state_proj, step_proj, conv_value, conv_state, step_bias, decay_log, skip_scale, gate_gain, out_proj, lengths, cotangent):
    total_rows = hidden_in.shape[0]
    seq_ends = jnp.cumsum(lengths).astype(jnp.int32)
    starts = (seq_ends - lengths).astype(jnp.int32)
    positions = jnp.arange(total_rows, dtype=jnp.int32)
    segment = lax.optimization_barrier(jnp.sum((positions[:, None] >= seq_ends[None, :]).astype(jnp.int32), axis=1)).astype(jnp.int32)
    seq_start = lax.optimization_barrier(jnp.max(jnp.where(positions[:, None] >= starts[None, :], starts[None, :], 0), axis=1))
    offset = positions - seq_start

    def forward(hidden, gain_in, gate_w, value_w, state_w, step_w, conv_v, conv_s, bias_step, decay_w, skip_w, gain_gate, out_w):
        scale_in = lax.rsqrt(lax.optimization_barrier(jnp.mean(hidden * hidden, axis=1)) + EPSILON)
        normed = low(hidden * scale_in[:, None] * gain_in)
        gate_pre = low_back(jnp.dot(normed, gate_w, precision=HIGHEST))
        value_pre = low_back(low(jnp.dot(normed, value_w, precision=HIGHEST)))
        state_pre = low_back(low(jnp.dot(normed, state_w, precision=HIGHEST)))
        step_pre = low_back(jnp.einsum('td,kdh->tkh', normed, step_w, precision=HIGHEST))
        joined = jnp.concatenate([value_pre, state_pre], axis=1)
        padded_rows = jnp.concatenate([jnp.zeros((3, joined.shape[1]), jnp.float32), joined], axis=0)
        tap_weights = jnp.concatenate([conv_v, conv_s], axis=1)
        conv_total = jnp.zeros_like(joined)
        for shift_tap in range(4):
            valid_rows = (offset >= 3 - shift_tap).astype(jnp.float32)
            conv_total = conv_total + padded_rows[shift_tap:shift_tap + total_rows] * tap_weights[shift_tap] * valid_rows[:, None]
        rounded = low(jax.nn.silu(conv_total))
        values = rounded[:, :INNER].reshape(total_rows, HEADS, HDIM)
        state_maps = rounded[:, INNER:]
        entry_fwd = state_maps[:, :NS]
        read_fwd = state_maps[:, NS:2 * NS]
        entry_rev = state_maps[:, 2 * NS:3 * NS]
        read_rev = state_maps[:, 3 * NS:]
        step_size = jax.nn.softplus(step_pre + bias_step[None])
        log_decay = -jnp.exp(decay_w)[None, None, :] * step_size
        y_fwd = scan_ssd(values, step_size[:, 0], log_decay[:, 0], entry_fwd, read_fwd, segment)
        y_rev = scan_ssd(values[::-1], step_size[::-1, 1], log_decay[::-1, 1], entry_rev[::-1], read_rev[::-1], segment[::-1])[::-1]
        mixed_heads = y_fwd + y_rev + skip_w[None, :, None] * values
        gated = mixed_heads.reshape(total_rows, INNER) * jax.nn.silu(gate_pre)
        scale_gate = lax.rsqrt(lax.optimization_barrier(jnp.mean(gated * gated, axis=1)) + EPSILON)
        normed_gate = low(gated * scale_gate[:, None] * gain_gate)
        return hidden + jnp.dot(normed_gate, out_w, precision=HIGHEST)
    inputs = (hidden_in, norm_gain, gate_proj, value_proj, state_proj, step_proj, conv_value, conv_state, step_bias, decay_log, skip_scale, gate_gain, out_proj)
    inputs = tuple((item.astype(jnp.float32) for item in inputs))
    result, pullback = jax.vjp(forward, *inputs)
    gradients = pullback(cotangent.astype(jnp.float32))
    return (result.astype(jnp.bfloat16), gradients[0], gradients[1], gradients[2], gradients[3], gradients[4], gradients[5], gradients[6], gradients[7], gradients[8], gradients[9], gradients[10], gradients[11], gradients[12])
```

```python
from functools import partial

import jax
import jax.numpy as jnp
from jax import lax
from jax.experimental import pallas as pl
from jax.experimental.pallas import tpu as pltpu
from jax.sharding import PartitionSpec as P

EPSILON = 1e-05
LEN_MOST = 4096
Q = 128
TB = 256
HP = 16
MIB = 1024 * 1024
HIGHEST = lax.Precision.HIGHEST
F32 = jnp.float32
BF16 = jnp.bfloat16
MESH = pl.DeviceIdType.MESH


def nn(a, b, precision=None):
    return jnp.dot(a, b, preferred_element_type=F32, precision=precision)


def nt(a, b, precision=None):
    return lax.dot_general(a, b, (((1,), (1,)), ((), ())), preferred_element_type=F32, precision=precision)


def tn(a, b, precision=None):
    return lax.dot_general(a, b, (((0,), (0,)), ((), ())), preferred_element_type=F32, precision=precision)


def iota(shape, axis):
    return lax.broadcasted_iota(jnp.int32, shape, axis)


def spread_matrix(width, hdim):
    return (iota((HP, width), 1) // hdim == iota((HP, width), 0)).astype(F32)


def split(x):
    hi = x.astype(BF16)
    return hi, (x - hi.astype(F32)).astype(BF16)


def widen(rows, spread2):
    hi, lo = split(rows.T)
    return nn(jnp.concatenate([hi, lo], axis=1), spread2)


def widen_col(col, spread):
    return tn(jnp.broadcast_to(col, (HP, 8)), spread, HIGHEST)[0:1]


def silu(x):
    return x * jax.nn.sigmoid(x)


def softplus(x):
    return jnp.maximum(x, 0.0) + jnp.log1p(jnp.exp(-jnp.abs(x)))


def step_parts(step, bias, dlog):
    dt = softplus(step + bias)
    ld = -jnp.exp(dlog) * dt
    upto = (iota((Q, Q), 0) <= iota((Q, Q), 1)).astype(F32)
    run = nn(ld, upto, HIGHEST)
    return dt, ld, run, run - ld


def state_factors(dt, run, bef, t0, b):
    t1 = t0 + Q
    tok = iota((1, Q), 1) + t0
    ef = jnp.where((tok < b) | (t0 > b), jnp.exp(bef[:HP]), 0.0)
    er = jnp.where((tok >= b) | (t1 < b), jnp.exp(run[HP:, Q - 1 : Q] - run[HP:]), 0.0)
    tf = jnp.where((tok >= b) | (t1 <= b), jnp.exp(run[:HP, Q - 1 : Q] - run[:HP]), 0.0) * dt[:HP]
    tr = jnp.where((tok < b) | (t0 >= b), jnp.exp(bef[HP:]), 0.0) * dt[HP:]
    return ef, er, tf, tr


def conv_mask(tok, shift, b, off0):
    lost = ((tok < b) & (tok + off0 < shift)) | ((tok >= b) & (tok < b + shift))
    return jnp.where(lost, 0.0, 1.0)


def put_message(ref, state, passed):
    hi, lo = split(passed)
    ref[0:64, :] = state.astype(BF16)
    row = iota((16, state.shape[1]), 0)
    tail = jnp.where(row == 0, hi.astype(F32), jnp.where(row == 1, lo.astype(F32), 0.0))
    ref[64:80, :] = tail.astype(BF16)


def chain(ref):
    total = ref[0, 0:64, :].astype(F32)
    passed = None
    for k in range(1, ref.shape[0]):
        tail = ref[k - 1, 64:80, :].astype(F32)
        here = tail[0:1] + tail[1:2]
        passed = here if passed is None else passed * here
        total = total + passed * ref[k, 0:64, :].astype(F32)
    return total


def front_kernel(len_ref, hid_ref, halo_ref, gain_ref, wg_ref, wv_ref, ws_ref, wstep_ref, tapv_ref, taps_ref,
                 bias_ref, dlog_ref,
                 meta_ref, normt_ref, gate_ref, joined_ref, jhalo_ref, act_ref, step_ref, inc_ref, pexp_ref,
                 msgf_ref, msgr_ref,
                 ext, sumf, sumr, prod):
    blk = pl.program_id(0)
    nblk = pl.num_programs(0)
    inner = wv_ref.shape[1]
    both = inner + ws_ref.shape[1]
    base = lax.axis_index("seq") * (TB * nblk)
    length = TB * nblk

    @pl.when(blk == 0)
    def _():
        def one(j, carry):
            start, b, off0, after = carry
            end = start + len_ref[j]
            b = jnp.where((start > base) & (start < base + length), start - base, b)
            off0 = jnp.where((start <= base) & (base < end), base - start, off0)
            after = jnp.where(end == base + length, 0, after)
            return end, b, off0, after

        _, b, off0, after = lax.fori_loop(
            0, len_ref.shape[0], one, (jnp.int32(0), jnp.int32(length + 1), jnp.int32(0), jnp.int32(1)))
        meta_ref[0] = b
        meta_ref[1] = off0
        meta_ref[2] = jnp.where(off0 > 0, 1, 0).astype(jnp.int32)
        meta_ref[3] = after

    b = meta_ref[0]
    off0 = meta_ref[1]

    def norm(x):
        x = x.astype(F32)
        scale = lax.rsqrt(jnp.mean(x * x, axis=1, keepdims=True) + EPSILON)
        return (x * scale * gain_ref[...]).astype(BF16)

    @pl.when(blk == 0)
    def _():
        nh = norm(halo_ref[...])
        pre = jnp.concatenate([nn(nh, wv_ref[...]), nn(nh, ws_ref[...])], axis=1).astype(BF16)
        jhalo_ref[...] = pre
        ext[0:8, :] = pre.astype(F32)[8:16]
        sumf[...] = jnp.zeros_like(sumf)
        sumr[...] = jnp.zeros_like(sumr)
        prod[...] = jnp.ones_like(prod)

    @pl.when(blk > 0)
    def _():
        ext[0:8, :] = ext[TB : TB + 8, :]

    x = hid_ref[...].astype(F32)
    scale = lax.rsqrt(jnp.mean(x * x, axis=1, keepdims=True) + EPSILON)
    normed32 = x * scale * gain_ref[...]
    normed = normed32.astype(BF16)
    normt_ref[...] = normed.T
    gate_ref[...] = nn(normed, wg_ref[...])
    jv = nn(normed, wv_ref[...]).astype(BF16)
    js = nn(normed, ws_ref[...]).astype(BF16)
    joined_ref[:, :inner] = jv
    joined_ref[:, inner:] = js
    ext[8 : 8 + TB, :inner] = jv.astype(F32)
    ext[8 : 8 + TB, inner:] = js.astype(F32)
    step_all = nt(wstep_ref[...], normed)
    step_ref[...] = step_all
    tok = iota((TB, 1), 0) + blk * TB
    masks = [conv_mask(tok, m, b, off0) for m in range(4)]
    for j in range(both // 128):
        cols = slice(j * 128, (j + 1) * 128)
        tap = tapv_ref[:, cols] if j * 128 < inner else taps_ref[:, j * 128 - inner : (j + 1) * 128 - inner]
        total = ext[8 : 8 + TB, cols] * tap[3:4]
        for m in range(1, 4):
            total = total + ext[8 - m : 8 - m + TB, cols] * tap[3 - m : 4 - m] * masks[m]
        act_ref[:, cols] = silu(total).astype(BF16)
    spread = spread_matrix(inner, 64)
    spread2 = jnp.concatenate([spread, spread], axis=0).astype(BF16)
    for q in range(TB // Q):
        rows = slice(q * Q, (q + 1) * Q)
        t0 = blk * TB + q * Q
        dt, ld, run, bef = step_parts(step_all[:, rows], bias_ref[...], dlog_ref[...])
        _, _, tf, tr = state_factors(dt, run, bef, t0, b)
        values = act_ref[rows, :inner].astype(F32)
        maps_t = act_ref[rows, inner:].astype(F32).T.astype(BF16)
        incf = nn(maps_t[0:64], (values * widen(tf, spread2)).astype(BF16))
        incr = nn(maps_t[128:192], (values * widen(tr, spread2)).astype(BF16))
        inc_ref[q, 0:64, :] = incf
        inc_ref[q, 64:128, :] = incr
        gone = jnp.exp(run[:, Q - 1 : Q])
        passf = jnp.where((t0 <= b) & (b < t0 + Q), 0.0, 1.0)
        passr = jnp.where((t0 < b) & (b <= t0 + Q), 0.0, 1.0)
        pf = widen_col(gone[:HP], spread) * passf
        pr = widen_col(gone[HP:], spread) * passr
        pexp_ref[q, 0:1, :] = pf
        pexp_ref[q, 1:2, :] = pr
        sumf[...] = pf * sumf[...] + incf
        sumr[...] = sumr[...] + prod[1:2, :] * incr
        prod[0:1, :] = prod[0:1, :] * pf
        prod[1:2, :] = prod[1:2, :] * pr

    @pl.when(blk == nblk - 1)
    def _():
        put_message(msgf_ref, sumf[...], prod[0:1, :] * meta_ref[2].astype(F32))
        put_message(msgr_ref, sumr[...], prod[1:2, :] * meta_ref[3].astype(F32))


def swap_kernel(reach, up_ref, down_ref, from_low, from_high, up_send, up_recv, down_send, down_recv):
    me = lax.axis_index("seq")
    core = lax.axis_index("head")
    count = lax.axis_size("seq")
    barrier = pltpu.get_barrier_semaphore()
    for k in range(1, reach + 1):
        @pl.when(me + k < count)
        def _():
            pl.semaphore_signal(barrier, inc=1, device_id=(me + k, core), device_id_type=MESH)

        @pl.when(me >= k)
        def _():
            pl.semaphore_signal(barrier, inc=1, device_id=(me - k, core), device_id_type=MESH)

    pl.semaphore_wait(barrier, jnp.minimum(me, reach) + jnp.minimum(count - 1 - me, reach))

    def up(k):
        return pltpu.make_async_remote_copy(
            src_ref=up_ref, dst_ref=from_low.at[k - 1], send_sem=up_send.at[k - 1], recv_sem=up_recv.at[k - 1],
            device_id=(me + k, core), device_id_type=MESH)

    def down(k):
        return pltpu.make_async_remote_copy(
            src_ref=down_ref, dst_ref=from_high.at[k - 1], send_sem=down_send.at[k - 1],
            recv_sem=down_recv.at[k - 1], device_id=(me - k, core), device_id_type=MESH)

    for k in range(1, reach + 1):
        @pl.when(me + k < count)
        def _():
            up(k).start()

        @pl.when(me >= k)
        def _():
            down(k).start()

    for k in range(1, reach + 1):
        @pl.when(me < k)
        def _():
            from_low[k - 1] = jnp.zeros_like(from_low[k - 1])

        @pl.when(me + k >= count)
        def _():
            from_high[k - 1] = jnp.zeros_like(from_high[k - 1])

    for k in range(1, reach + 1):
        @pl.when(me + k < count)
        def _():
            up(k).wait_send()
            down(k).wait_recv()

        @pl.when(me >= k)
        def _():
            down(k).wait_send()
            up(k).wait_recv()


def swap(up, down, reach, ident):
    shape = jax.ShapeDtypeStruct((reach,) + up.shape, up.dtype)
    vm = pl.BlockSpec(memory_space=pltpu.VMEM)
    return pl.pallas_call(
        partial(swap_kernel, reach),
        out_shape=(shape, shape),
        in_specs=[vm, vm],
        out_specs=(vm, vm),
        scratch_shapes=[pltpu.SemaphoreType.DMA((reach,))] * 4,
        compiler_params=pltpu.CompilerParams(
            collective_id=ident, has_side_effects=True, vmem_limit_bytes=16 * MIB),
    )(up, down)


def core_swap_kernel(count, *refs):
    ins, outs, (send, recv) = refs[:count], refs[count : 2 * count], refs[2 * count :]
    me = lax.axis_index("seq")
    other = 1 - lax.axis_index("head")
    barrier = pltpu.get_barrier_semaphore()
    pl.semaphore_signal(barrier, inc=1, device_id=(me, other), device_id_type=MESH)
    pl.semaphore_wait(barrier, 1)
    copies = [
        pltpu.make_async_remote_copy(
            src_ref=ins[i], dst_ref=outs[i], send_sem=send.at[i], recv_sem=recv.at[i],
            device_id=(me, other), device_id_type=MESH)
        for i in range(count)
    ]
    for copy in copies:
        copy.start()
    for copy in copies:
        copy.wait()


def core_swap(arrays, ident):
    count = len(arrays)
    vm = pl.BlockSpec(memory_space=pltpu.VMEM)
    return pl.pallas_call(
        partial(core_swap_kernel, count),
        out_shape=tuple(jax.ShapeDtypeStruct(a.shape, a.dtype) for a in arrays),
        in_specs=[vm] * count,
        out_specs=(vm,) * count,
        scratch_shapes=[pltpu.SemaphoreType.DMA((count,))] * 2,
        compiler_params=pltpu.CompilerParams(
            collective_id=ident, has_side_effects=True, vmem_limit_bytes=32 * MIB),
    )(*arrays)


def chunk_scores(maps, t0, b):
    tr, tc = iota((Q, Q), 0), iota((Q, Q), 1)
    same = (tr + t0 < b) == (tc + t0 < b)
    fwd = nt(maps[:, 64:128], maps[:, 0:64])
    rev = nt(maps[:, 192:256], maps[:, 128:192])
    return jnp.where((tr > tc) & same, fwd, jnp.where((tr < tc) & same, rev, 0.0))


def halves(x):
    left = iota(x.shape, 1) < 64
    zero = jnp.zeros_like(x)
    return jnp.concatenate([jnp.where(left, x, zero), jnp.where(left, zero, x)], axis=0)


def mix_kernel(meta_ref, act_ref, step_ref, bias_ref, dlog_ref, gate_ref, cot_ref, wo_ref, ggain_ref, skip_ref,
               inc_ref, pexp_ref, low_ref, high_ref,
               mixed_ref, state_ref, sums_ref):
    blk = pl.program_id(0)
    inner = wo_ref.shape[0]
    nchunk = inc_ref.shape[0]
    b = meta_ref[0]

    @pl.when(blk == 0)
    def _():
        hf = chain(low_ref) * meta_ref[2].astype(F32)
        hr = chain(high_ref) * meta_ref[3].astype(F32)
        for c in range(nchunk):
            state_ref[c, 0:64, :] = hf.astype(BF16)
            hf = pexp_ref[c, 0:1, :] * hf + inc_ref[c, 0:64, :]
            d = nchunk - 1 - c
            state_ref[d, 64:128, :] = hr.astype(BF16)
            hr = pexp_ref[d, 1:2, :] * hr + inc_ref[d, 64:128, :]

    spread = spread_matrix(inner, 64)
    spread2 = jnp.concatenate([spread, spread], axis=0).astype(BF16)
    skip = widen_col(skip_ref[...], spread)
    lower = iota((Q, Q), 0) > iota((Q, Q), 1)
    u_all = nt(cot_ref[...], wo_ref[...])
    lane = iota((Q, 128), 1)
    for q in range(TB // Q):
        rows = slice(q * Q, (q + 1) * Q)
        t0 = blk * TB + q * Q
        chunk = blk * (TB // Q) + q
        dt, ld, run, bef = step_parts(step_ref[:, rows], bias_ref[...], dlog_ref[...])
        ef, er, _, _ = state_factors(dt, run, bef, t0, b)
        ldt = jnp.log(jnp.maximum(dt, 1e-37))
        rowf = ldt[:HP] - run[:HP]
        rowr = ldt[HP:] + bef[HP:]
        cols = jnp.concatenate([bef[:HP], -run[HP:]], axis=0).T
        maps = act_ref[rows, inner:]
        scores = chunk_scores(maps, t0, b)
        efe, ere = widen(ef, spread2), widen(er, spread2)
        state = state_ref[chunk]
        ys = nn(maps[:, 64:128], state[0:64]) * efe + nn(maps[:, 192:256], state[64:128]) * ere
        square = jnp.zeros((Q, 1), F32)
        cross = jnp.zeros((Q, 1), F32)
        for j in range(inner // 128):
            lanes = slice(j * 128, (j + 1) * 128)
            weights = []
            for h in (2 * j, 2 * j + 1):
                e = jnp.where(lower, cols[:, h : h + 1] + rowf[h : h + 1],
                              cols[:, HP + h : HP + h + 1] + rowr[h : h + 1])
                weights.append((jnp.exp(jnp.minimum(e, 60.0)) * scores).astype(BF16))
            vp = act_ref[rows, lanes]
            y = nn(jnp.concatenate(weights, axis=1), halves(vp))
            y = y + ys[:, lanes] + skip[:, lanes] * vp.astype(F32)
            mixed_ref[rows, lanes] = y
            gated = y * silu(gate_ref[rows, lanes])
            square = square + jnp.sum(gated * gated, axis=1, keepdims=True)
            cross = cross + jnp.sum(gated * (u_all[rows, lanes] * ggain_ref[:, lanes]), axis=1, keepdims=True)
        both = jnp.where(lane == 0, square, jnp.where(lane == 1, cross, 0.0))
        sums_ref[:, rows] = both.T[0:8]


def gate_kernel(meta_ref, mine_ref, other_ref, mixed_ref, gate_ref, cot_ref, wo_ref, ggain_ref, act_ref, step_ref,
                bias_ref, dlog_ref, pexp_ref, normt_ref,
                out_ref, ggate_ref, dy_ref, dhy_ref, msgf_ref, msgr_ref, small_ref, ggw_ref, ngt,
                gsum_f, gsum_r, prod):
    blk = pl.program_id(0)
    nblk = pl.num_programs(0)
    inner = wo_ref.shape[0]
    whole = inner * 2
    b = meta_ref[0]

    @pl.when(blk == 0)
    def _():
        gsum_f[...] = jnp.zeros_like(gsum_f)
        gsum_r[...] = jnp.zeros_like(gsum_r)
        prod[...] = jnp.ones_like(prod)
        small_ref[...] = jnp.zeros_like(small_ref)

    sums = mine_ref[...] + other_ref[...]
    sums = jnp.concatenate([sums, jnp.zeros((120, TB), F32)], axis=0).T
    scale = lax.rsqrt(sums[:, 0:1] / whole + EPSILON)
    back = scale * scale * scale * sums[:, 1:2] / whole
    gng = nt(cot_ref[...], wo_ref[...])
    for j in range(inner // 128):
        lanes = slice(j * 128, (j + 1) * 128)
        mixed = mixed_ref[:, lanes]
        pre = gate_ref[:, lanes]
        sig = jax.nn.sigmoid(pre)
        gated = mixed * (pre * sig)
        ng = gated * scale
        gain = ggain_ref[:, lanes]
        ng_low = (ng * gain).astype(BF16)
        ngt[blk, :, lanes] = ng_low
        g = gng[:, lanes]
        small_ref[0:1, lanes] += jnp.sum(g * ng, axis=0, keepdims=True)
        grad_gated = scale * (g * gain) - gated * back
        dy = grad_gated * (pre * sig)
        small_ref[1:2, lanes] += jnp.sum(dy * act_ref[:, lanes].astype(F32), axis=0, keepdims=True)
        dy_ref[:, lanes] = dy
        ggate_ref[pl.ds(blk * TB, TB), lanes] = (
            grad_gated * mixed * (sig * (1.0 + pre * (1.0 - sig)))).astype(BF16)
    out_ref[...] = nn(ngt[blk], wo_ref[...]).astype(BF16)
    spread = spread_matrix(inner, 64)
    spread2 = jnp.concatenate([spread, spread], axis=0).astype(BF16)
    for q in range(TB // Q):
        rows = slice(q * Q, (q + 1) * Q)
        t0 = blk * TB + q * Q
        chunk = blk * (TB // Q) + q
        dt, ld, run, bef = step_parts(step_ref[:, rows], bias_ref[...], dlog_ref[...])
        ef, er, _, _ = state_factors(dt, run, bef, t0, b)
        maps_t = act_ref[rows, inner:].astype(F32).T.astype(BF16)
        dy = dy_ref[rows, :]
        df = nn(maps_t[64:128], (dy * widen(ef, spread2)).astype(BF16))
        dr = nn(maps_t[192:256], (dy * widen(er, spread2)).astype(BF16))
        dhy_ref[q, 0:64, :] = df
        dhy_ref[q, 64:128, :] = dr
        pf, pr = pexp_ref[chunk, 0:1, :], pexp_ref[chunk, 1:2, :]
        gsum_f[...] = gsum_f[...] + prod[0:1, :] * df
        gsum_r[...] = pr * gsum_r[...] + dr
        prod[0:1, :] = prod[0:1, :] * pf
        prod[1:2, :] = prod[1:2, :] * pr

    @pl.when(blk == nblk - 1)
    def _():
        before = meta_ref[2].astype(F32)
        after = meta_ref[3].astype(F32)
        put_message(msgf_ref, gsum_f[...] * before, prod[0:1, :] * before)
        put_message(msgr_ref, gsum_r[...] * after, prod[1:2, :] * after)
        ggw_ref[...] = nn(normt_ref[...], ggate_ref[...]).astype(BF16)


def outgrad_kernel(ng_ref, cot_ref, gow_ref):
    gow_ref[...] = tn(ng_ref[...], cot_ref[...]).astype(BF16)


def back_kernel(meta_ref, act_ref, step_ref, bias_ref, dlog_ref, dy_ref, skip_ref, state_ref, dhy_ref, pexp_ref,
                low_ref, high_ref, joined_ref, jprev_ref, jhalo_ref, tapv_ref, taps_ref,
                gv_ref, gs_ref, gstep_ref, lent_ref, convg_ref, heads_ref,
                dstate, ext, jext, rowbuf, dact):
    step_no = pl.program_id(0)
    nblk = pl.num_programs(0)
    blk = nblk - 1 - step_no
    inner = tapv_ref.shape[1]
    both = act_ref.shape[1]
    nchunk = state_ref.shape[0]
    b = meta_ref[0]
    off0 = meta_ref[1]

    @pl.when(step_no == 0)
    def _():
        df = chain(high_ref)
        dr = chain(low_ref)
        for c in range(nchunk):
            d = nchunk - 1 - c
            dstate[d, 0:64, :] = df.astype(BF16)
            df = pexp_ref[d, 0:1, :] * df + dhy_ref[d, 0:64, :]
            dstate[c, 64:128, :] = dr.astype(BF16)
            dr = pexp_ref[c, 1:2, :] * dr + dhy_ref[c, 64:128, :]
        ext[TB : TB + 8, :] = jnp.zeros((8, both), F32)
        convg_ref[...] = jnp.zeros_like(convg_ref)
        heads_ref[...] = jnp.zeros_like(heads_ref)
        rowbuf[...] = jnp.zeros_like(rowbuf)

    @pl.when(step_no > 0)
    def _():
        ext[TB : TB + 8, :] = ext[0:8, :]

    spread = spread_matrix(inner, 64)
    spread_low = spread.astype(BF16)
    spread2 = jnp.concatenate([spread_low, spread_low], axis=0)
    skip = widen_col(skip_ref[...], spread)
    i0, i1 = iota((Q, Q), 0), iota((Q, Q), 1)
    after, before = (i0 > i1), (i0 < i1)
    diag = i0 == i1
    sums_low = jnp.concatenate([after, before], axis=1).astype(BF16)
    after32, before32 = after.astype(F32), before.astype(F32)
    for q in reversed(range(TB // Q)):
        rows = slice(q * Q, (q + 1) * Q)
        t0 = blk * TB + q * Q
        chunk = blk * (TB // Q) + q
        dt, ld, run, bef = step_parts(step_ref[:, rows], bias_ref[...], dlog_ref[...])
        ef, er, tf, tr = state_factors(dt, run, bef, t0, b)
        ldt = jnp.log(jnp.maximum(dt, 1e-37))
        cols = jnp.concatenate([ldt[:HP] - run[:HP], ldt[HP:] + bef[HP:]], axis=0).T
        rowf, rowr = bef[:HP], -run[HP:]
        maps = act_ref[rows, inner:]
        entf, readf, entr, readr = maps[:, 0:64], maps[:, 64:128], maps[:, 128:192], maps[:, 192:256]
        same = (i0 + t0 < b) == (i1 + t0 < b)
        okf, okr = before & same, after & same
        scores = jnp.where(okf, nt(entf, readf), jnp.where(okr, nt(entr, readr), 0.0))
        state = state_ref[chunk]
        grad_state = dstate[chunk]
        dscore = jnp.zeros((Q, Q), F32)
        efe, ere = widen(ef, spread2), widen(er, spread2)
        tfe, tre = widen(tf, spread2), widen(tr, spread2)
        dy = dy_ref[rows, :]
        values = act_ref[rows, :inner].astype(F32)
        dyf, dyr = dy * efe, dy * ere
        dyf_low, dyr_low = dyf.astype(BF16), dyr.astype(BF16)
        dreadf = nt(dyf_low, state[0:64])
        dreadr = nt(dyr_low, state[64:128])
        qf = nt(spread_low, (nn(readf, state[0:64]) * dyf).astype(BF16))
        qr = nt(spread_low, (nn(readr, state[64:128]) * dyr).astype(BF16))
        dvf = nn(entf, grad_state[0:64]) * tfe
        dvr = nn(entr, grad_state[64:128]) * tre
        wf = nt(spread_low, (values * dvf).astype(BF16))
        wr = nt(spread_low, (values * dvr).astype(BF16))
        dentf = nt((values * tfe).astype(BF16), grad_state[0:64])
        dentr = nt((values * tre).astype(BF16), grad_state[64:128])
        through = state.astype(F32) * grad_state.astype(F32)
        zf = jnp.sum(through[0:64], axis=0, keepdims=True) * pexp_ref[chunk, 0:1, :]
        zr = jnp.sum(through[64:128], axis=0, keepdims=True) * pexp_ref[chunk, 1:2, :]
        zf = nt(spread, jnp.broadcast_to(zf, (8, inner)), HIGHEST)[:, 0:1]
        zr = nt(spread, jnp.broadcast_to(zr, (8, inner)), HIGHEST)[:, 0:1]
        for j in range(inner // 128):
            lanes = slice(j * 128, (j + 1) * 128)
            vp = act_ref[rows, lanes]
            dyp = dy_ref[rows, lanes].astype(BF16)
            dw = nt(halves(vp), dyp)
            weights = []
            for i, h in enumerate((2 * j, 2 * j + 1)):
                e = jnp.where(before, cols[:, h : h + 1] + rowf[h : h + 1],
                              cols[:, HP + h : HP + h + 1] + rowr[h : h + 1])
                x = jnp.exp(jnp.minimum(e, 60.0))
                weights.append((x * scores).astype(BF16))
                dwx = dw[i * Q : (i + 1) * Q] * x
                dscore = dscore + dwx
                sums = nn((dwx * scores).astype(BF16), sums_low)
                pf, pr = sums[:, :Q], sums[:, Q:]
                rowbuf[h : h + 1, :] = jnp.sum(jnp.where(before, pf, 0.0), axis=0, keepdims=True)
                rowbuf[HP + h : HP + h + 1, :] = jnp.sum(jnp.where(after, pr, 0.0), axis=0, keepdims=True)
                rowbuf[2 * HP + h : 2 * HP + h + 1, :] = jnp.sum(jnp.where(diag, pf, 0.0), axis=0, keepdims=True)
                rowbuf[3 * HP + h : 3 * HP + h + 1, :] = jnp.sum(jnp.where(diag, pr, 0.0), axis=0, keepdims=True)
            dv = nn(jnp.concatenate(weights, axis=1), halves(dyp))
            dact[rows, lanes] = dv + dvf[:, lanes] + dvr[:, lanes] + dy[:, lanes] * skip[:, lanes]
        dsf = jnp.where(okf, dscore, 0.0)
        dsr = jnp.where(okr, dscore, 0.0)
        dsf_low, dsr_low = dsf.astype(BF16), dsr.astype(BF16)
        dentf = dentf + nn(dsf_low, readf)
        dentr = dentr + nn(dsr_low, readr)
        dreadf = dreadf + nn(dsf.T.astype(BF16), entf)
        dreadr = dreadr + nn(dsr.T.astype(BF16), entr)
        dact[rows, inner:] = jnp.concatenate([dentf, dreadf, dentr, dreadr], axis=1)
        late = nn(jnp.concatenate([qf, wr], axis=0), after32, HIGHEST)
        early = nn(jnp.concatenate([wf, qr], axis=0), before32, HIGHEST)
        dld = jnp.concatenate(
            [rowbuf[0:HP] + late[:HP] + early[:HP] + zf, rowbuf[HP : 2 * HP] + late[HP:] + early[HP:] + zr], axis=0)
        dldt = rowbuf[2 * HP : 4 * HP] + jnp.concatenate([wf, wr], axis=0)
        sig = jax.nn.sigmoid(step_ref[:, rows] + bias_ref[...])
        ratio = jnp.where(dt < 1e-30, 1.0, sig / jnp.maximum(dt, 1e-30))
        graw = dldt * ratio - jnp.exp(dlog_ref[...]) * sig * dld
        gstep_ref[:, rows] = graw.astype(BF16)
        heads_ref[:, 0:1] += jnp.sum(graw, axis=1, keepdims=True)
        heads_ref[:, 1:2] += jnp.sum(dld * ld, axis=1, keepdims=True)

    prev = jnp.where(blk == 0, jhalo_ref[...], jprev_ref[...])
    jext[0:16, :] = prev.astype(F32)
    jext[16 : 16 + TB, :] = joined_ref[...].astype(F32)
    tok = iota((TB, 1), 0) + blk * TB
    masks = [conv_mask(tok, m, b, off0) for m in range(4)]
    later_masks = [conv_mask(tok + m, m, b, off0) for m in range(4)]
    edge_masks = [conv_mask(iota((8, 1), 0) - 8 + m, m, b, off0) for m in range(4)]
    for j in range(both // 128):
        cols = slice(j * 128, (j + 1) * 128)
        tap = tapv_ref[:, cols] if j * 128 < inner else taps_ref[:, j * 128 - inner : (j + 1) * 128 - inner]
        shifted = [jext[16 : 16 + TB, cols]]
        total = shifted[0] * tap[3:4]
        for m in range(1, 4):
            shifted.append(jext[16 - m : 16 - m + TB, cols] * masks[m])
            total = total + shifted[m] * tap[3 - m : 4 - m]
        sig = jax.nn.sigmoid(total)
        dconv = dact[:, cols] * (sig * (1.0 + total * (1.0 - sig)))
        ext[0:TB, cols] = dconv
        for m in range(4):
            convg_ref[3 - m : 4 - m, cols] += jnp.sum(dconv * shifted[m], axis=0, keepdims=True)
        grad = dconv * tap[3:4]
        for m in range(1, 4):
            grad = grad + ext[m : m + TB, cols] * later_masks[m] * tap[3 - m : 4 - m]
        if j * 128 < inner:
            gv_ref[:, cols] = grad
        else:
            gs_ref[:, j * 128 - inner : (j + 1) * 128 - inner] = grad

    @pl.when(step_no == nblk - 1)
    def _():
        first = jnp.concatenate([jnp.zeros((8, both), F32), ext[0:8, :]], axis=0)
        tap = jnp.concatenate([tapv_ref[...], taps_ref[...]], axis=1)
        lent = jnp.zeros((8, both), F32)
        for m in range(1, 4):
            lent = lent + first[m : m + 8] * edge_masks[m] * tap[3 - m : 4 - m]
        lent_ref[...] = lent


def down_kernel(gv_ref, gs_ref, next_ref, gstep_ref, ggate_ref, normt_ref, wg_ref, wv_ref, wstep_ref,
                gn_ref, gso_ref, gvw_ref, gstepw_ref,
                gvl):
    blk = pl.program_id(0)
    nblk = pl.num_programs(0)
    inner = wg_ref.shape[1]
    last = (blk == nblk - 1).astype(F32)
    gvl[pl.ds(blk * TB, TB), :] = gv_ref[...].astype(BF16)

    tail = gv_ref[TB - 16 : TB, :] + jnp.concatenate(
        [jnp.zeros((8, inner), F32), next_ref[:, :inner] * last], axis=0)
    gvl[pl.ds(blk * TB + TB - 16, 16), :] = tail.astype(BF16)
    gso_ref[...] = gs_ref[...].astype(BF16)
    tail = gs_ref[TB - 16 : TB, :] + jnp.concatenate(
        [jnp.zeros((8, gs_ref.shape[1]), F32), next_ref[:, inner:] * last], axis=0)
    gso_ref[TB - 16 : TB, :] = tail.astype(BF16)
    gn = nt(ggate_ref[...], wg_ref[...]) + nt(gvl[pl.ds(blk * TB, TB), :], wv_ref[...])
    gn = gn + tn(gstep_ref[:, pl.ds(blk * TB, TB)], wstep_ref[...])
    gn_ref[...] = gn.astype(BF16)

    @pl.when(blk == nblk - 1)
    def _():
        gvw_ref[...] = nn(normt_ref[...], gvl[...]).astype(BF16)
        gstepw_ref[...] = nt(gstep_ref[...], normt_ref[...])


def end_kernel(mine_ref, other_ref, smine_ref, sother_ref, hid_ref, cot_ref, gain_ref, ws_ref, normt_ref,
               omine_ref, oother_ref,
               gh_ref, ngain_ref, gsw_ref, out_ref,
               gsl):
    blk = pl.program_id(0)
    nblk = pl.num_programs(0)

    @pl.when(blk == 0)
    def _():
        ngain_ref[...] = jnp.zeros_like(ngain_ref)

    grad_state = (smine_ref[...].astype(F32) + sother_ref[...].astype(F32)).astype(BF16)
    gsl[pl.ds(blk * TB, TB), :] = grad_state
    gn = mine_ref[...].astype(F32) + other_ref[...].astype(F32) + nt(grad_state, ws_ref[...])
    x = hid_ref[...].astype(F32)
    scale = lax.rsqrt(jnp.mean(x * x, axis=1, keepdims=True) + EPSILON)
    ngain_ref[0:1, :] += jnp.sum(gn * x * scale, axis=0, keepdims=True)
    v = gn * gain_ref[...]
    inner = jnp.mean(x * v, axis=1, keepdims=True)
    gh_ref[...] = cot_ref[...].astype(F32) + scale * v - x * (scale * scale * scale * inner)
    out_ref[...] = (x + (omine_ref[...].astype(F32) + oother_ref[...].astype(F32))).astype(BF16)

    @pl.when(blk == nblk - 1)
    def _():
        gsw_ref[...] = nn(normt_ref[...], gsl[...]).astype(BF16)


def whole_spec(array):
    zeros = (0,) * array.ndim
    return pl.BlockSpec(array.shape, lambda i: zeros)


def rows_spec(array, rows=TB, flip=0):
    rest = (0,) * (array.ndim - 1)
    if flip:
        return pl.BlockSpec((rows,) + array.shape[1:], lambda i: (flip - 1 - i,) + rest)
    return pl.BlockSpec((rows,) + array.shape[1:], lambda i: (i,) + rest)


def cols_spec(array, flip=0):
    if flip:
        return pl.BlockSpec((array.shape[0], TB), lambda i: (0, flip - 1 - i))
    return pl.BlockSpec((array.shape[0], TB), lambda i: (0, i))


SMEM_SPEC = pl.BlockSpec(memory_space=pltpu.SMEM)


def call(kernel, grid, ins, outs, scratch, vmem, flops):
    arrays = [a for a, _ in ins]
    return pl.pallas_call(
        kernel,
        grid=(grid,),
        in_specs=[s for _, s in ins],
        out_specs=[s for _, s in outs],
        out_shape=[jax.ShapeDtypeStruct(a.shape, a.dtype) for a, _ in outs],
        scratch_shapes=scratch,
        compiler_params=pltpu.CompilerParams(
            dimension_semantics=("arbitrary",), vmem_limit_bytes=vmem * MIB),
        cost_estimate=pl.CostEstimate(
            flops=int(flops), transcendentals=0,
            bytes_accessed=sum(a.size * a.dtype.itemsize for a in arrays)
            + sum(a.size * a.dtype.itemsize for a, _ in outs)),
    )(*arrays)


def padded(x, axis):
    pads = [(0, 0)] * x.ndim
    pads[axis] = (0, HP - x.shape[axis])
    return jnp.pad(x, pads)


def shape(dims, dtype):
    return jax.ShapeDtypeStruct(dims, dtype)


def body(
    hidden_in, norm_gain, gate_proj, value_proj, state_proj, step_proj, conv_value, conv_state,
    step_bias, decay_log, skip_scale, gate_gain, out_proj, lengths, cotangent,
):
    length, width = hidden_in.shape
    inner = gate_proj.shape[1]
    heads = decay_log.shape[0]
    maps = state_proj.shape[1]
    both = inner + maps
    nblk = length // TB
    nchunk = length // Q
    count = lax.axis_size("seq")
    reach = min(1 + (LEN_MOST - 2) // length, count - 1)
    mib = MIB

    halo = lax.ppermute(hidden_in[length - 16 :], "seq", [(i, i + 1) for i in range(count - 1)])
    wstep = padded(step_proj.transpose(0, 2, 1), 1).reshape(2 * HP, width)
    bias = padded(step_bias, 1).reshape(2 * HP, 1)
    dlog = padded(decay_log, 0)
    dlog = jnp.concatenate([dlog, dlog]).reshape(2 * HP, 1)
    skip = padded(skip_scale, 0).reshape(HP, 1)
    gain_in = norm_gain.reshape(1, width)
    gain_gate = gate_gain.reshape(1, inner)

    normt = shape((width, length), BF16)
    gate = shape((length, inner), F32)
    joined = shape((length, both), BF16)
    jhalo = shape((16, both), BF16)
    act = shape((length, both), BF16)
    step = shape((2 * HP, length), F32)
    inc = shape((nchunk, 128, inner), F32)
    pexp = shape((nchunk, 2, inner), F32)
    msg = shape((80, inner), BF16)
    meta = shape((8,), jnp.int32)
    cq = TB // Q
    meta, normt, gate, joined, jhalo, act, step, inc, pexp, msgf, msgr = call(
        front_kernel, nblk,
        [(lengths, SMEM_SPEC), (hidden_in, rows_spec(hidden_in)), (halo, whole_spec(halo)),
         (gain_in, whole_spec(gain_in)), (gate_proj, whole_spec(gate_proj)), (value_proj, whole_spec(value_proj)),
         (state_proj, whole_spec(state_proj)), (wstep, whole_spec(wstep)), (conv_value, whole_spec(conv_value)),
         (conv_state, whole_spec(conv_state)), (bias, whole_spec(bias)), (dlog, whole_spec(dlog))],
        [(meta, SMEM_SPEC), (normt, cols_spec(normt)), (gate, rows_spec(gate)), (joined, rows_spec(joined)),
         (jhalo, whole_spec(jhalo)), (act, rows_spec(act)), (step, cols_spec(step)), (inc, rows_spec(inc, cq)),
         (pexp, rows_spec(pexp, cq)), (msg, whole_spec(msg)), (msg, whole_spec(msg))],
        [pltpu.VMEM((TB + 8, both), F32), pltpu.VMEM((64, inner), F32), pltpu.VMEM((64, inner), F32),
         pltpu.VMEM((8, inner), F32)],
        48, 2 * length * width * (2 * inner + maps))
    low, high = swap(msgf, msgr, reach, 1)

    mixed = shape((length, inner), F32)
    state = shape((nchunk, 128, inner), BF16)
    sums = shape((8, length), F32)
    mixed, state, sums = call(
        mix_kernel, nblk,
        [(meta, SMEM_SPEC), (act, rows_spec(act)), (step, cols_spec(step)), (bias, whole_spec(bias)),
         (dlog, whole_spec(dlog)), (gate, rows_spec(gate)), (cotangent, rows_spec(cotangent)),
         (out_proj, whole_spec(out_proj)), (gain_gate, whole_spec(gain_gate)), (skip, whole_spec(skip)),
         (inc, whole_spec(inc)), (pexp, whole_spec(pexp)), (low, whole_spec(low)), (high, whole_spec(high))],
        [(mixed, rows_spec(mixed)), (state, whole_spec(state)), (sums, cols_spec(sums))],
        [], 48, 2 * length * width * inner * 2)
    (sums_other,) = core_swap([sums], 2)

    out_part = shape((length, width), BF16)
    ggate = shape((length, inner), BF16)
    dy = shape((length, inner), F32)
    dhy = shape((nchunk, 128, inner), F32)
    small = shape((8, inner), F32)
    ggw = shape((width, inner), BF16)
    ng = shape((nblk, TB, inner), BF16)
    out_part, ggate, dy, dhy, msgf, msgr, small, ggw, ng = call(
        gate_kernel, nblk,
        [(meta, SMEM_SPEC), (sums, cols_spec(sums)), (sums_other, cols_spec(sums_other)), (mixed, rows_spec(mixed)),
         (gate, rows_spec(gate)), (cotangent, rows_spec(cotangent)), (out_proj, whole_spec(out_proj)),
         (gain_gate, whole_spec(gain_gate)), (act, rows_spec(act)), (step, cols_spec(step)),
         (bias, whole_spec(bias)), (dlog, whole_spec(dlog)), (pexp, whole_spec(pexp)), (normt, whole_spec(normt))],
        [(out_part, rows_spec(out_part)), (ggate, whole_spec(ggate)), (dy, rows_spec(dy)),
         (dhy, rows_spec(dhy, cq)), (msg, whole_spec(msg)), (msg, whole_spec(msg)), (small, whole_spec(small)),
         (ggw, whole_spec(ggw)), (ng, whole_spec(ng))],
        [pltpu.VMEM((64, inner), F32), pltpu.VMEM((64, inner), F32), pltpu.VMEM((8, inner), F32)],
        48, 2 * length * width * inner * 4)
    low, high = swap(msgr, msgf, reach, 3)

    ng = ng.reshape(length, inner)
    gow = shape((inner, width), BF16)
    (gow,) = call(
        outgrad_kernel, 1, [(ng, whole_spec(ng)), (cotangent, whole_spec(cotangent))], [(gow, whole_spec(gow))],
        [], 32, 2 * length * width * inner)
    ggw, gow = lax.psum((ggw, gow), "seq")

    gv = shape((length, inner), F32)
    gs = shape((length, maps), F32)
    gstep = shape((2 * HP, length), BF16)
    lent = shape((8, both), F32)
    convg = shape((8, both), F32)
    hsum = shape((2 * HP, 128), F32)
    prev_spec = pl.BlockSpec((16, both), lambda i: (jnp.maximum((nblk - 1 - i) * (TB // 16) - 1, 0), 0))
    gv, gs, gstep, lent, convg, hsum = call(
        back_kernel, nblk,
        [(meta, SMEM_SPEC), (act, rows_spec(act, TB, nblk)), (step, cols_spec(step, nblk)), (bias, whole_spec(bias)),
         (dlog, whole_spec(dlog)), (dy, rows_spec(dy, TB, nblk)), (skip, whole_spec(skip)),
         (state, whole_spec(state)), (dhy, whole_spec(dhy)), (pexp, whole_spec(pexp)), (low, whole_spec(low)),
         (high, whole_spec(high)), (joined, rows_spec(joined, TB, nblk)), (joined, prev_spec),
         (jhalo, whole_spec(jhalo)), (conv_value, whole_spec(conv_value)), (conv_state, whole_spec(conv_state))],
        [(gv, rows_spec(gv, TB, nblk)), (gs, rows_spec(gs, TB, nblk)), (gstep, cols_spec(gstep, nblk)),
         (lent, whole_spec(lent)), (convg, whole_spec(convg)), (hsum, whole_spec(hsum))],
        [pltpu.VMEM((nchunk, 128, inner), BF16), pltpu.VMEM((TB + 8, both), F32), pltpu.VMEM((TB + 16, both), F32),
         pltpu.VMEM((4 * HP, Q), F32), pltpu.VMEM((TB, both), F32)],
        56, 2 * length * width * inner * 4)
    from_next = lax.ppermute(lent, "seq", [(i + 1, i) for i in range(count - 1)])

    gn = shape((length, width), BF16)
    gso = shape((length, maps), BF16)
    gvw = shape((width, inner), BF16)
    gstepw = shape((2 * HP, width), F32)
    gn, gso, gvw, gstepw = call(
        down_kernel, nblk,
        [(gv, rows_spec(gv)), (gs, rows_spec(gs)), (from_next, whole_spec(from_next)), (gstep, whole_spec(gstep)),
         (ggate, rows_spec(ggate)), (normt, whole_spec(normt)), (gate_proj, whole_spec(gate_proj)),
         (value_proj, whole_spec(value_proj)), (wstep, whole_spec(wstep))],
        [(gn, rows_spec(gn)), (gso, rows_spec(gso)), (gvw, whole_spec(gvw)), (gstepw, whole_spec(gstepw))],
        [pltpu.VMEM((length, inner), BF16)],
        48, 2 * length * width * inner * 3)
    gn_other, gso_other, out_other = core_swap([gn, gso, out_part], 4)

    gh = shape((length, width), F32)
    ngain = shape((8, width), F32)
    gsw = shape((width, maps), BF16)
    out = shape((length, width), BF16)
    gh, ngain, gsw, out = call(
        end_kernel, nblk,
        [(gn, rows_spec(gn)), (gn_other, rows_spec(gn_other)), (gso, rows_spec(gso)),
         (gso_other, rows_spec(gso_other)), (hidden_in, rows_spec(hidden_in)), (cotangent, rows_spec(cotangent)),
         (gain_in, whole_spec(gain_in)), (state_proj, whole_spec(state_proj)), (normt, whole_spec(normt)),
         (out_part, rows_spec(out_part)), (out_other, rows_spec(out_other))],
        [(gh, rows_spec(gh)), (ngain, whole_spec(ngain)), (gsw, whole_spec(gsw)), (out, rows_spec(out))],
        [pltpu.VMEM((length, maps), BF16)],
        48, 2 * length * width * maps * 2)

    gvw, gsw, gstepw = lax.psum((gvw, gsw, gstepw), "seq")
    small, convg, hsum, ngain = lax.psum((small[0:2], convg[0:4], hsum[:, 0:2], ngain[0]), "seq")
    conv_state_grad = lax.psum(convg[:, inner:], "head")
    gstepw = gstepw.reshape(2, HP, width)[:, :heads].transpose(0, 2, 1)
    hsum = hsum.reshape(2, HP, 2)[:, :heads]
    return (
        out,
        gh,
        ngain,
        ggw.astype(F32),
        gvw.astype(F32),
        gsw.astype(F32),
        gstepw,
        convg[:, :inner],
        conv_state_grad,
        hsum[:, :, 0],
        hsum[0, :, 1] + hsum[1, :, 1],
        jnp.sum(small[1].reshape(heads, inner // heads), axis=1),
        small[0],
        gow.astype(F32),
    )


def solution(mesh):
    in_specs = (
        P("seq", None),
        P(),
        P(None, "head"),
        P(None, "head"),
        P(),
        P(None, None, "head"),
        P(None, "head"),
        P(),
        P(None, "head"),
        P("head"),
        P("head"),
        P("head"),
        P("head", None),
        P(),
        P("seq", None),
    )
    out_specs = (
        P("seq", None),
        P("seq", None),
        P(),
        P(None, "head"),
        P(None, "head"),
        P(),
        P(None, None, "head"),
        P(None, "head"),
        P(),
        P(None, "head"),
        P("head"),
        P("head"),
        P("head"),
        P("head", None),
    )
    return jax.shard_map(body, mesh=mesh, in_specs=in_specs, out_specs=out_specs, check_vma=False)
```

```python
from functools import partial

import jax
import jax.numpy as jnp
from jax import lax
from jax.experimental import pallas as pl
from jax.experimental.pallas import tpu as pltpu
from jax.sharding import PartitionSpec as P

EPSILON = 1e-05
LEN_MOST = 4096
Q = 128
TB = 256
HP = 16
MIB = 1024 * 1024
HIGHEST = lax.Precision.HIGHEST
F32 = jnp.float32
BF16 = jnp.bfloat16
MESH = pl.DeviceIdType.MESH


def nn(a, b, precision=None):
    return jnp.dot(a, b, preferred_element_type=F32, precision=precision)


def nt(a, b, precision=None):
    return lax.dot_general(a, b, (((1,), (1,)), ((), ())), preferred_element_type=F32, precision=precision)


def tn(a, b, precision=None):
    return lax.dot_general(a, b, (((0,), (0,)), ((), ())), preferred_element_type=F32, precision=precision)


def iota(shape, axis):
    return lax.broadcasted_iota(jnp.int32, shape, axis)


def spread_matrix(width, hdim):
    return (iota((HP, width), 1) // hdim == iota((HP, width), 0)).astype(F32)


def split(x):
    hi = x.astype(BF16)
    return hi, (x - hi.astype(F32)).astype(BF16)


def widen(rows, spread2):
    hi, lo = split(rows.T)
    return nn(jnp.concatenate([hi, lo], axis=1), spread2)


def widen_col(col, spread):
    return tn(jnp.broadcast_to(col, (HP, 8)), spread, HIGHEST)[0:1]


def silu(x):
    return x * jax.nn.sigmoid(x)


def softplus(x):
    return jnp.maximum(x, 0.0) + jnp.log1p(jnp.exp(-jnp.abs(x)))


def step_parts(step, bias, dlog):
    dt = softplus(step + bias)
    ld = -jnp.exp(dlog) * dt
    upto = (iota((Q, Q), 0) <= iota((Q, Q), 1)).astype(F32)
    run = nn(ld, upto, HIGHEST)
    return dt, ld, run, run - ld


def state_factors(dt, run, bef, t0, b):
    t1 = t0 + Q
    tok = iota((1, Q), 1) + t0
    ef = jnp.where((tok < b) | (t0 > b), jnp.exp(bef[:HP]), 0.0)
    er = jnp.where((tok >= b) | (t1 < b), jnp.exp(run[HP:, Q - 1 : Q] - run[HP:]), 0.0)
    tf = jnp.where((tok >= b) | (t1 <= b), jnp.exp(run[:HP, Q - 1 : Q] - run[:HP]), 0.0) * dt[:HP]
    tr = jnp.where((tok < b) | (t0 >= b), jnp.exp(bef[HP:]), 0.0) * dt[HP:]
    return ef, er, tf, tr


def conv_mask(tok, shift, b, off0):
    lost = ((tok < b) & (tok + off0 < shift)) | ((tok >= b) & (tok < b + shift))
    return jnp.where(lost, 0.0, 1.0)


def put_message(ref, state, passed):
    hi, lo = split(passed)
    ref[0:64, :] = state.astype(BF16)
    row = iota((16, state.shape[1]), 0)
    tail = jnp.where(row == 0, hi.astype(F32), jnp.where(row == 1, lo.astype(F32), 0.0))
    ref[64:80, :] = tail.astype(BF16)


def chain(ref):
    total = ref[0, 0:64, :].astype(F32)
    passed = None
    for k in range(1, ref.shape[0]):
        tail = ref[k - 1, 64:80, :].astype(F32)
        here = tail[0:1] + tail[1:2]
        passed = here if passed is None else passed * here
        total = total + passed * ref[k, 0:64, :].astype(F32)
    return total


def front_kernel(len_ref, hid_ref, halo_ref, gain_ref, wg_ref, wv_ref, ws_ref, wstep_ref, tapv_ref, taps_ref,
                 bias_ref, dlog_ref,
                 meta_ref, normt_ref, gate_ref, joined_ref, jhalo_ref, act_ref, step_ref, inc_ref, pexp_ref,
                 msgf_ref, msgr_ref,
                 ext, sumf, sumr, prod):
    blk = pl.program_id(0)
    nblk = pl.num_programs(0)
    inner = wv_ref.shape[1]
    both = inner + ws_ref.shape[1]
    base = lax.axis_index("seq") * (TB * nblk)
    length = TB * nblk

    @pl.when(blk == 0)
    def _():
        def one(j, carry):
            start, b, off0, after = carry
            end = start + len_ref[j]
            b = jnp.where((start > base) & (start < base + length), start - base, b)
            off0 = jnp.where((start <= base) & (base < end), base - start, off0)
            after = jnp.where(end == base + length, 0, after)
            return end, b, off0, after

        _, b, off0, after = lax.fori_loop(
            0, len_ref.shape[0], one, (jnp.int32(0), jnp.int32(length + 1), jnp.int32(0), jnp.int32(1)))
        meta_ref[0] = b
        meta_ref[1] = off0
        meta_ref[2] = jnp.where(off0 > 0, 1, 0).astype(jnp.int32)
        meta_ref[3] = after

    b = meta_ref[0]
    off0 = meta_ref[1]

    def norm(x):
        x = x.astype(F32)
        scale = lax.rsqrt(jnp.mean(x * x, axis=1, keepdims=True) + EPSILON)
        return (x * scale * gain_ref[...]).astype(BF16)

    @pl.when(blk == 0)
    def _():
        nh = norm(halo_ref[...])
        pre = jnp.concatenate([nn(nh, wv_ref[...]), nn(nh, ws_ref[...])], axis=1).astype(BF16)
        jhalo_ref[...] = pre
        ext[0:8, :] = pre.astype(F32)[8:16]
        sumf[...] = jnp.zeros_like(sumf)
        sumr[...] = jnp.zeros_like(sumr)
        prod[...] = jnp.ones_like(prod)

    @pl.when(blk > 0)
    def _():
        ext[0:8, :] = ext[TB : TB + 8, :]

    x = hid_ref[...].astype(F32)
    scale = lax.rsqrt(jnp.mean(x * x, axis=1, keepdims=True) + EPSILON)
    normed32 = x * scale * gain_ref[...]
    normed = normed32.astype(BF16)
    normt_ref[...] = normed.T
    gate_ref[...] = nn(normed, wg_ref[...])
    jv = nn(normed, wv_ref[...]).astype(BF16)
    js = nn(normed, ws_ref[...]).astype(BF16)
    joined_ref[:, :inner] = jv
    joined_ref[:, inner:] = js
    ext[8 : 8 + TB, :inner] = jv.astype(F32)
    ext[8 : 8 + TB, inner:] = js.astype(F32)
    step_all = nt(wstep_ref[...], normed)
    step_ref[...] = step_all
    tok = iota((TB, 1), 0) + blk * TB
    masks = [conv_mask(tok, m, b, off0) for m in range(4)]
    for j in range(both // 128):
        cols = slice(j * 128, (j + 1) * 128)
        tap = tapv_ref[:, cols] if j * 128 < inner else taps_ref[:, j * 128 - inner : (j + 1) * 128 - inner]
        total = ext[8 : 8 + TB, cols] * tap[3:4]
        for m in range(1, 4):
            total = total + ext[8 - m : 8 - m + TB, cols] * tap[3 - m : 4 - m] * masks[m]
        act_ref[:, cols] = silu(total).astype(BF16)
    spread = spread_matrix(inner, 64)
    spread2 = jnp.concatenate([spread, spread], axis=0).astype(BF16)
    for q in range(TB // Q):
        rows = slice(q * Q, (q + 1) * Q)
        t0 = blk * TB + q * Q
        dt, ld, run, bef = step_parts(step_all[:, rows], bias_ref[...], dlog_ref[...])
        _, _, tf, tr = state_factors(dt, run, bef, t0, b)
        values = act_ref[rows, :inner].astype(F32)
        maps_t = act_ref[rows, inner:].astype(F32).T.astype(BF16)
        incf = nn(maps_t[0:64], (values * widen(tf, spread2)).astype(BF16))
        incr = nn(maps_t[128:192], (values * widen(tr, spread2)).astype(BF16))
        inc_ref[q, 0:64, :] = incf
        inc_ref[q, 64:128, :] = incr
        gone = jnp.exp(run[:, Q - 1 : Q])
        passf = jnp.where((t0 <= b) & (b < t0 + Q), 0.0, 1.0)
        passr = jnp.where((t0 < b) & (b <= t0 + Q), 0.0, 1.0)
        pf = widen_col(gone[:HP], spread) * passf
        pr = widen_col(gone[HP:], spread) * passr
        pexp_ref[q, 0:1, :] = pf
        pexp_ref[q, 1:2, :] = pr
        sumf[...] = pf * sumf[...] + incf
        sumr[...] = sumr[...] + prod[1:2, :] * incr
        prod[0:1, :] = prod[0:1, :] * pf
        prod[1:2, :] = prod[1:2, :] * pr

    @pl.when(blk == nblk - 1)
    def _():
        put_message(msgf_ref, sumf[...], prod[0:1, :] * meta_ref[2].astype(F32))
        put_message(msgr_ref, sumr[...], prod[1:2, :] * meta_ref[3].astype(F32))


def swap_kernel(reach, up_ref, down_ref, from_low, from_high, up_send, up_recv, down_send, down_recv):
    me = lax.axis_index("seq")
    core = lax.axis_index("head")
    count = lax.axis_size("seq")
    barrier = pltpu.get_barrier_semaphore()
    for k in range(1, reach + 1):
        @pl.when(me + k < count)
        def _():
            pl.semaphore_signal(barrier, inc=1, device_id=(me + k, core), device_id_type=MESH)

        @pl.when(me >= k)
        def _():
            pl.semaphore_signal(barrier, inc=1, device_id=(me - k, core), device_id_type=MESH)

    pl.semaphore_wait(barrier, jnp.minimum(me, reach) + jnp.minimum(count - 1 - me, reach))

    def up(k):
        return pltpu.make_async_remote_copy(
            src_ref=up_ref, dst_ref=from_low.at[k - 1], send_sem=up_send.at[k - 1], recv_sem=up_recv.at[k - 1],
            device_id=(me + k, core), device_id_type=MESH)

    def down(k):
        return pltpu.make_async_remote_copy(
            src_ref=down_ref, dst_ref=from_high.at[k - 1], send_sem=down_send.at[k - 1],
            recv_sem=down_recv.at[k - 1], device_id=(me - k, core), device_id_type=MESH)

    for k in range(1, reach + 1):
        @pl.when(me + k < count)
        def _():
            up(k).start()

        @pl.when(me >= k)
        def _():
            down(k).start()

    for k in range(1, reach + 1):
        @pl.when(me < k)
        def _():
            from_low[k - 1] = jnp.zeros_like(from_low[k - 1])

        @pl.when(me + k >= count)
        def _():
            from_high[k - 1] = jnp.zeros_like(from_high[k - 1])

    for k in range(1, reach + 1):
        @pl.when(me + k < count)
        def _():
            up(k).wait_send()
            down(k).wait_recv()

        @pl.when(me >= k)
        def _():
            down(k).wait_send()
            up(k).wait_recv()


def swap(up, down, reach, ident):
    shape = jax.ShapeDtypeStruct((reach,) + up.shape, up.dtype)
    vm = pl.BlockSpec(memory_space=pltpu.VMEM)
    return pl.pallas_call(
        partial(swap_kernel, reach),
        out_shape=(shape, shape),
        in_specs=[vm, vm],
        out_specs=(vm, vm),
        scratch_shapes=[pltpu.SemaphoreType.DMA((reach,))] * 4,
        compiler_params=pltpu.CompilerParams(
            collective_id=ident, has_side_effects=True, vmem_limit_bytes=16 * MIB),
    )(up, down)


def core_swap_kernel(count, *refs):
    ins, outs, (send, recv) = refs[:count], refs[count : 2 * count], refs[2 * count :]
    me = lax.axis_index("seq")
    other = 1 - lax.axis_index("head")
    barrier = pltpu.get_barrier_semaphore()
    pl.semaphore_signal(barrier, inc=1, device_id=(me, other), device_id_type=MESH)
    pl.semaphore_wait(barrier, 1)
    copies = [
        pltpu.make_async_remote_copy(
            src_ref=ins[i], dst_ref=outs[i], send_sem=send.at[i], recv_sem=recv.at[i],
            device_id=(me, other), device_id_type=MESH)
        for i in range(count)
    ]
    for copy in copies:
        copy.start()
    for copy in copies:
        copy.wait()


def core_swap(arrays, ident):
    count = len(arrays)
    vm = pl.BlockSpec(memory_space=pltpu.VMEM)
    return pl.pallas_call(
        partial(core_swap_kernel, count),
        out_shape=tuple(jax.ShapeDtypeStruct(a.shape, a.dtype) for a in arrays),
        in_specs=[vm] * count,
        out_specs=(vm,) * count,
        scratch_shapes=[pltpu.SemaphoreType.DMA((count,))] * 2,
        compiler_params=pltpu.CompilerParams(
            collective_id=ident, has_side_effects=True, vmem_limit_bytes=32 * MIB),
    )(*arrays)


def pieces_of(arrays, bits):
    found = []
    for a, array in enumerate(arrays):
        rows, cols = array.shape
        halvings = 0
        while halvings < bits and (rows >> halvings) % 32 == 0:
            halvings += 1
        parts = 2 if rows * cols >= 512 * 512 else 1
        for p in range(parts):
            order = list(range(bits))
            if len(found) % 2 and bits > 1:
                order[0], order[1] = order[1], order[0]
            found.append((a, p * (cols // parts), cols // parts, order, halvings))
    return found


def reduce_kernel(count, bits, *refs):
    ins, tiny_ref = refs[:count], refs[count]
    outs, tiny_out = refs[count + 1 : 2 * count + 1], refs[2 * count + 1]
    works, recvs = refs[2 * count + 2 : 3 * count + 2], refs[3 * count + 2 : 4 * count + 2]
    tiny_work, tiny_recv, rs_send, rs_recv, ag_send, ag_recv, t_send, t_recv = refs[4 * count + 2 :]
    me = lax.axis_index("seq")
    core = lax.axis_index("head")
    bit = [lax.rem(me // (1 << k), 2) for k in range(bits)]
    partner = [me + (1 - 2 * bit[k]) * (1 << k) for k in range(bits)]
    pieces = pieces_of(ins, bits)

    barrier = pltpu.get_barrier_semaphore()
    for k in range(bits):
        pl.semaphore_signal(barrier, inc=1, device_id=(partner[k], core), device_id_type=MESH)
    pl.semaphore_wait(barrier, bits)

    def remote(src, dst, send, recv, k):
        return pltpu.make_async_remote_copy(
            src_ref=src, dst_ref=dst, send_sem=send, recv_sem=recv, device_id=(partner[k], core),
            device_id_type=MESH)

    state = []
    for p, (a, c0, cols, order, halvings) in enumerate(pieces):
        state.append({"off": jnp.int32(0), "size": ins[a].shape[0], "slot": 0, "copy": None})

    def rs_start(p, s):
        a, c0, cols, order, halvings = pieces[p]
        st = state[p]
        k = order[s]
        src = ins[a] if s == 0 else works[a]
        half = st["size"] // 2 if s < halvings else st["size"]
        if s < halvings:
            st["keep"] = pl.multiple_of(st["off"] + bit[k] * half, 16)
            st["give"] = pl.multiple_of(st["off"] + (1 - bit[k]) * half, 16)
        else:
            st["keep"] = st["give"] = st["off"]
        st["half"] = half
        st["copy"] = remote(
            src.at[pl.ds(st["give"], half), pl.ds(c0, cols)],
            recvs[a].at[pl.ds(st["slot"], half), pl.ds(c0, cols)],
            rs_send.at[p, s], rs_recv.at[p, s], k)
        st["copy"].start()

    def rs_finish(p, s):
        a, c0, cols, order, halvings = pieces[p]
        st = state[p]
        half, keep, slot = st["half"], st["keep"], st["slot"]
        if s < halvings:
            st["copy"].wait_recv()
            st.setdefault("sends", []).append(st["copy"])
        else:
            st["copy"].wait()
        src = ins[a] if s == 0 else works[a]
        dst = outs[a] if s == bits - 1 else works[a]
        step = 48 if half % 48 == 0 else 16

        def add(i, _):
            r = pl.multiple_of(keep + i * step, 16)
            q = pl.multiple_of(slot + i * step, 16)
            total = src[pl.ds(r, step), pl.ds(c0, cols)].astype(F32) + recvs[a][pl.ds(q, step), pl.ds(c0, cols)].astype(F32)
            dst[pl.ds(r, step), pl.ds(c0, cols)] = total.astype(BF16)
            return 0

        lax.fori_loop(0, half // step, add, 0)
        st["off"], st["size"], st["slot"] = keep, half, slot + half

    def ag_start(p, s):
        a, c0, cols, order, halvings = pieces[p]
        st = state[p]
        k = order[s]
        where = outs[a].at[pl.ds(st["off"], st["size"]), pl.ds(c0, cols)]
        st["copy"] = remote(where, where, ag_send.at[p, s], ag_recv.at[p, s], k)
        st["copy"].start()

    def ag_finish(p, s):
        a, c0, cols, order, halvings = pieces[p]
        st = state[p]
        st["copy"].wait_recv()
        st["sends"].append(st["copy"])
        st["off"] = pl.multiple_of(st["off"] - bit[order[s]] * st["size"], 16)
        st["size"] = 2 * st["size"]

    def tiny_copy(s):
        src = tiny_ref if s == 0 else tiny_work.at[s - 1]
        return remote(src, tiny_recv.at[s], t_send.at[s], t_recv.at[s], s)

    every = range(len(pieces))
    for p in every:
        rs_start(p, 0)
    tiny_copy(0).start()
    for s in range(bits):
        for p in every:
            rs_finish(p, s)
            if s + 1 < bits:
                rs_start(p, s + 1)
            elif pieces[p][4]:
                ag_start(p, pieces[p][4] - 1)
        tiny_copy(s).wait()
        total = (tiny_ref[...] if s == 0 else tiny_work[s - 1]) + tiny_recv[s]
        if s + 1 < bits:
            tiny_work[s] = total
            tiny_copy(s + 1).start()
        else:
            tiny_out[...] = total
    for back in range(bits):
        for p in every:
            s = pieces[p][4] - 1 - back
            if s >= 0:
                ag_finish(p, s)
                if s > 0:
                    ag_start(p, s - 1)
    for p in every:
        for copy in state[p].get("sends", []):
            copy.wait_send()


def reduce_all(arrays, tiny, devices, ident):
    count = len(arrays)
    bits = devices.bit_length() - 1
    assert devices == 1 << bits
    npieces = len(pieces_of(arrays, bits))
    vm = pl.BlockSpec(memory_space=pltpu.VMEM)
    received = []
    for array in arrays:
        rows, halvings = array.shape[0], pieces_of([array], bits)[0][4]
        total = 0
        for s in range(bits):
            rows = rows // 2 if s < halvings else rows
            total += rows
        received.append(total)
    outs = pl.pallas_call(
        partial(reduce_kernel, count, bits),
        out_shape=[jax.ShapeDtypeStruct(a.shape, a.dtype) for a in arrays + [tiny]],
        in_specs=[vm] * (count + 1),
        out_specs=[vm] * (count + 1),
        scratch_shapes=[pltpu.VMEM(a.shape, a.dtype) for a in arrays]
        + [pltpu.VMEM((r, a.shape[1]), a.dtype) for r, a in zip(received, arrays)]
        + [pltpu.VMEM((bits,) + tiny.shape, F32), pltpu.VMEM((bits,) + tiny.shape, F32)]
        + [pltpu.SemaphoreType.DMA((npieces, bits))] * 4
        + [pltpu.SemaphoreType.DMA((bits,))] * 2,
        compiler_params=pltpu.CompilerParams(
            collective_id=ident, has_side_effects=True, vmem_limit_bytes=48 * MIB),
    )(*arrays, tiny)
    return outs[:count], outs[count]


def chunk_scores(maps, t0, b):
    tr, tc = iota((Q, Q), 0), iota((Q, Q), 1)
    same = (tr + t0 < b) == (tc + t0 < b)
    fwd = nt(maps[:, 64:128], maps[:, 0:64])
    rev = nt(maps[:, 192:256], maps[:, 128:192])
    return jnp.where((tr > tc) & same, fwd, jnp.where((tr < tc) & same, rev, 0.0))


def halves(x):
    left = iota(x.shape, 1) < 64
    zero = jnp.zeros_like(x)
    return jnp.concatenate([jnp.where(left, x, zero), jnp.where(left, zero, x)], axis=0)


def mix_kernel(meta_ref, act_ref, step_ref, bias_ref, dlog_ref, gate_ref, cot_ref, wo_ref, ggain_ref, skip_ref,
               inc_ref, pexp_ref, low_ref, high_ref,
               mixed_ref, state_ref, sums_ref):
    blk = pl.program_id(0)
    inner = wo_ref.shape[0]
    nchunk = inc_ref.shape[0]
    b = meta_ref[0]

    @pl.when(blk == 0)
    def _():
        hf = chain(low_ref) * meta_ref[2].astype(F32)
        hr = chain(high_ref) * meta_ref[3].astype(F32)
        for c in range(nchunk):
            state_ref[c, 0:64, :] = hf.astype(BF16)
            hf = pexp_ref[c, 0:1, :] * hf + inc_ref[c, 0:64, :]
            d = nchunk - 1 - c
            state_ref[d, 64:128, :] = hr.astype(BF16)
            hr = pexp_ref[d, 1:2, :] * hr + inc_ref[d, 64:128, :]

    spread = spread_matrix(inner, 64)
    spread2 = jnp.concatenate([spread, spread], axis=0).astype(BF16)
    skip = widen_col(skip_ref[...], spread)
    lower = iota((Q, Q), 0) > iota((Q, Q), 1)
    u_all = nt(cot_ref[...], wo_ref[...])
    lane = iota((Q, 128), 1)
    for q in range(TB // Q):
        rows = slice(q * Q, (q + 1) * Q)
        t0 = blk * TB + q * Q
        chunk = blk * (TB // Q) + q
        dt, ld, run, bef = step_parts(step_ref[:, rows], bias_ref[...], dlog_ref[...])
        ef, er, _, _ = state_factors(dt, run, bef, t0, b)
        ldt = jnp.log(jnp.maximum(dt, 1e-37))
        rowf = ldt[:HP] - run[:HP]
        rowr = ldt[HP:] + bef[HP:]
        cols = jnp.concatenate([bef[:HP], -run[HP:]], axis=0).T
        maps = act_ref[rows, inner:]
        scores = chunk_scores(maps, t0, b)
        efe, ere = widen(ef, spread2), widen(er, spread2)
        state = state_ref[chunk]
        ys = nn(maps[:, 64:128], state[0:64]) * efe + nn(maps[:, 192:256], state[64:128]) * ere
        square = jnp.zeros((Q, 1), F32)
        cross = jnp.zeros((Q, 1), F32)
        for j in range(inner // 128):
            lanes = slice(j * 128, (j + 1) * 128)
            weights = []
            for h in (2 * j, 2 * j + 1):
                e = jnp.where(lower, cols[:, h : h + 1] + rowf[h : h + 1],
                              cols[:, HP + h : HP + h + 1] + rowr[h : h + 1])
                weights.append((jnp.exp(jnp.minimum(e, 60.0)) * scores).astype(BF16))
            vp = act_ref[rows, lanes]
            y = nn(jnp.concatenate(weights, axis=1), halves(vp))
            y = y + ys[:, lanes] + skip[:, lanes] * vp.astype(F32)
            mixed_ref[rows, lanes] = y
            gated = y * silu(gate_ref[rows, lanes])
            square = square + jnp.sum(gated * gated, axis=1, keepdims=True)
            cross = cross + jnp.sum(gated * (u_all[rows, lanes] * ggain_ref[:, lanes]), axis=1, keepdims=True)
        both = jnp.where(lane == 0, square, jnp.where(lane == 1, cross, 0.0))
        sums_ref[:, rows] = both.T[0:8]


def gate_kernel(meta_ref, mine_ref, other_ref, mixed_ref, gate_ref, cot_ref, wo_ref, ggain_ref, act_ref, step_ref,
                bias_ref, dlog_ref, pexp_ref, normt_ref,
                out_ref, ggate_ref, dy_ref, dhy_ref, msgf_ref, msgr_ref, small_ref, ggw_ref, ngt,
                gsum_f, gsum_r, prod):
    blk = pl.program_id(0)
    nblk = pl.num_programs(0)
    inner = wo_ref.shape[0]
    whole = inner * 2
    b = meta_ref[0]

    @pl.when(blk == 0)
    def _():
        gsum_f[...] = jnp.zeros_like(gsum_f)
        gsum_r[...] = jnp.zeros_like(gsum_r)
        prod[...] = jnp.ones_like(prod)
        small_ref[...] = jnp.zeros_like(small_ref)

    sums = mine_ref[...] + other_ref[...]
    sums = jnp.concatenate([sums, jnp.zeros((120, TB), F32)], axis=0).T
    scale = lax.rsqrt(sums[:, 0:1] / whole + EPSILON)
    back = scale * scale * scale * sums[:, 1:2] / whole
    gng = nt(cot_ref[...], wo_ref[...])
    for j in range(inner // 128):
        lanes = slice(j * 128, (j + 1) * 128)
        mixed = mixed_ref[:, lanes]
        pre = gate_ref[:, lanes]
        sig = jax.nn.sigmoid(pre)
        gated = mixed * (pre * sig)
        ng = gated * scale
        gain = ggain_ref[:, lanes]
        ng_low = (ng * gain).astype(BF16)
        ngt[blk, :, lanes] = ng_low
        g = gng[:, lanes]
        small_ref[0:1, lanes] += jnp.sum(g * ng, axis=0, keepdims=True)
        grad_gated = scale * (g * gain) - gated * back
        dy = grad_gated * (pre * sig)
        small_ref[1:2, lanes] += jnp.sum(dy * act_ref[:, lanes].astype(F32), axis=0, keepdims=True)
        dy_ref[:, lanes] = dy
        ggate_ref[pl.ds(blk * TB, TB), lanes] = (
            grad_gated * mixed * (sig * (1.0 + pre * (1.0 - sig)))).astype(BF16)
    out_ref[...] = nn(ngt[blk], wo_ref[...]).astype(BF16)
    spread = spread_matrix(inner, 64)
    spread2 = jnp.concatenate([spread, spread], axis=0).astype(BF16)
    for q in range(TB // Q):
        rows = slice(q * Q, (q + 1) * Q)
        t0 = blk * TB + q * Q
        chunk = blk * (TB // Q) + q
        dt, ld, run, bef = step_parts(step_ref[:, rows], bias_ref[...], dlog_ref[...])
        ef, er, _, _ = state_factors(dt, run, bef, t0, b)
        maps_t = act_ref[rows, inner:].astype(F32).T.astype(BF16)
        dy = dy_ref[rows, :]
        df = nn(maps_t[64:128], (dy * widen(ef, spread2)).astype(BF16))
        dr = nn(maps_t[192:256], (dy * widen(er, spread2)).astype(BF16))
        dhy_ref[q, 0:64, :] = df
        dhy_ref[q, 64:128, :] = dr
        pf, pr = pexp_ref[chunk, 0:1, :], pexp_ref[chunk, 1:2, :]
        gsum_f[...] = gsum_f[...] + prod[0:1, :] * df
        gsum_r[...] = pr * gsum_r[...] + dr
        prod[0:1, :] = prod[0:1, :] * pf
        prod[1:2, :] = prod[1:2, :] * pr

    @pl.when(blk == nblk - 1)
    def _():
        before = meta_ref[2].astype(F32)
        after = meta_ref[3].astype(F32)
        put_message(msgf_ref, gsum_f[...] * before, prod[0:1, :] * before)
        put_message(msgr_ref, gsum_r[...] * after, prod[1:2, :] * after)
        ggw_ref[...] = nn(normt_ref[...], ggate_ref[...]).astype(BF16)


def outgrad_kernel(ng_ref, cot_ref, gow_ref):
    gow_ref[...] = tn(ng_ref[...], cot_ref[...]).astype(BF16)


def back_kernel(meta_ref, act_ref, step_ref, bias_ref, dlog_ref, dy_ref, skip_ref, state_ref, dhy_ref, pexp_ref,
                low_ref, high_ref, joined_ref, jprev_ref, jhalo_ref, tapv_ref, taps_ref,
                gv_ref, gs_ref, gstep_ref, lent_ref, convg_ref, heads_ref,
                dstate, ext, jext, rowbuf, dact):
    step_no = pl.program_id(0)
    nblk = pl.num_programs(0)
    blk = nblk - 1 - step_no
    inner = tapv_ref.shape[1]
    both = act_ref.shape[1]
    nchunk = state_ref.shape[0]
    b = meta_ref[0]
    off0 = meta_ref[1]

    @pl.when(step_no == 0)
    def _():
        df = chain(high_ref)
        dr = chain(low_ref)
        for c in range(nchunk):
            d = nchunk - 1 - c
            dstate[d, 0:64, :] = df.astype(BF16)
            df = pexp_ref[d, 0:1, :] * df + dhy_ref[d, 0:64, :]
            dstate[c, 64:128, :] = dr.astype(BF16)
            dr = pexp_ref[c, 1:2, :] * dr + dhy_ref[c, 64:128, :]
        ext[TB : TB + 8, :] = jnp.zeros((8, both), F32)
        convg_ref[...] = jnp.zeros_like(convg_ref)
        heads_ref[...] = jnp.zeros_like(heads_ref)
        rowbuf[...] = jnp.zeros_like(rowbuf)

    @pl.when(step_no > 0)
    def _():
        ext[TB : TB + 8, :] = ext[0:8, :]

    spread = spread_matrix(inner, 64)
    spread_low = spread.astype(BF16)
    spread2 = jnp.concatenate([spread_low, spread_low], axis=0)
    skip = widen_col(skip_ref[...], spread)
    i0, i1 = iota((Q, Q), 0), iota((Q, Q), 1)
    after, before = (i0 > i1), (i0 < i1)
    diag = i0 == i1
    sums_low = jnp.concatenate([after, before], axis=1).astype(BF16)
    after32, before32 = after.astype(F32), before.astype(F32)
    for q in reversed(range(TB // Q)):
        rows = slice(q * Q, (q + 1) * Q)
        t0 = blk * TB + q * Q
        chunk = blk * (TB // Q) + q
        dt, ld, run, bef = step_parts(step_ref[:, rows], bias_ref[...], dlog_ref[...])
        ef, er, tf, tr = state_factors(dt, run, bef, t0, b)
        ldt = jnp.log(jnp.maximum(dt, 1e-37))
        cols = jnp.concatenate([ldt[:HP] - run[:HP], ldt[HP:] + bef[HP:]], axis=0).T
        rowf, rowr = bef[:HP], -run[HP:]
        maps = act_ref[rows, inner:]
        entf, readf, entr, readr = maps[:, 0:64], maps[:, 64:128], maps[:, 128:192], maps[:, 192:256]
        same = (i0 + t0 < b) == (i1 + t0 < b)
        okf, okr = before & same, after & same
        scores = jnp.where(okf, nt(entf, readf), jnp.where(okr, nt(entr, readr), 0.0))
        state = state_ref[chunk]
        grad_state = dstate[chunk]
        dscore = jnp.zeros((Q, Q), F32)
        efe, ere = widen(ef, spread2), widen(er, spread2)
        tfe, tre = widen(tf, spread2), widen(tr, spread2)
        dy = dy_ref[rows, :]
        values = act_ref[rows, :inner].astype(F32)
        dyf, dyr = dy * efe, dy * ere
        dyf_low, dyr_low = dyf.astype(BF16), dyr.astype(BF16)
        dreadf = nt(dyf_low, state[0:64])
        dreadr = nt(dyr_low, state[64:128])
        qf = nt(spread_low, (nn(readf, state[0:64]) * dyf).astype(BF16))
        qr = nt(spread_low, (nn(readr, state[64:128]) * dyr).astype(BF16))
        dvf = nn(entf, grad_state[0:64]) * tfe
        dvr = nn(entr, grad_state[64:128]) * tre
        wf = nt(spread_low, (values * dvf).astype(BF16))
        wr = nt(spread_low, (values * dvr).astype(BF16))
        dentf = nt((values * tfe).astype(BF16), grad_state[0:64])
        dentr = nt((values * tre).astype(BF16), grad_state[64:128])
        through = state.astype(F32) * grad_state.astype(F32)
        zf = jnp.sum(through[0:64], axis=0, keepdims=True) * pexp_ref[chunk, 0:1, :]
        zr = jnp.sum(through[64:128], axis=0, keepdims=True) * pexp_ref[chunk, 1:2, :]
        zf = nt(spread, jnp.broadcast_to(zf, (8, inner)), HIGHEST)[:, 0:1]
        zr = nt(spread, jnp.broadcast_to(zr, (8, inner)), HIGHEST)[:, 0:1]
        for j in range(inner // 128):
            lanes = slice(j * 128, (j + 1) * 128)
            vp = act_ref[rows, lanes]
            dyp = dy_ref[rows, lanes].astype(BF16)
            dw = nt(halves(vp), dyp)
            weights = []
            for i, h in enumerate((2 * j, 2 * j + 1)):
                e = jnp.where(before, cols[:, h : h + 1] + rowf[h : h + 1],
                              cols[:, HP + h : HP + h + 1] + rowr[h : h + 1])
                x = jnp.exp(jnp.minimum(e, 60.0))
                weights.append((x * scores).astype(BF16))
                dwx = dw[i * Q : (i + 1) * Q] * x
                dscore = dscore + dwx
                sums = nn((dwx * scores).astype(BF16), sums_low)
                pf, pr = sums[:, :Q], sums[:, Q:]
                rowbuf[h : h + 1, :] = jnp.sum(jnp.where(before, pf, 0.0), axis=0, keepdims=True)
                rowbuf[HP + h : HP + h + 1, :] = jnp.sum(jnp.where(after, pr, 0.0), axis=0, keepdims=True)
                rowbuf[2 * HP + h : 2 * HP + h + 1, :] = jnp.sum(jnp.where(diag, pf, 0.0), axis=0, keepdims=True)
                rowbuf[3 * HP + h : 3 * HP + h + 1, :] = jnp.sum(jnp.where(diag, pr, 0.0), axis=0, keepdims=True)
            dv = nn(jnp.concatenate(weights, axis=1), halves(dyp))
            dact[rows, lanes] = dv + dvf[:, lanes] + dvr[:, lanes] + dy[:, lanes] * skip[:, lanes]
        dsf = jnp.where(okf, dscore, 0.0)
        dsr = jnp.where(okr, dscore, 0.0)
        dsf_low, dsr_low = dsf.astype(BF16), dsr.astype(BF16)
        dentf = dentf + nn(dsf_low, readf)
        dentr = dentr + nn(dsr_low, readr)
        dreadf = dreadf + nn(dsf.T.astype(BF16), entf)
        dreadr = dreadr + nn(dsr.T.astype(BF16), entr)
        dact[rows, inner:] = jnp.concatenate([dentf, dreadf, dentr, dreadr], axis=1)
        late = nn(jnp.concatenate([qf, wr], axis=0), after32, HIGHEST)
        early = nn(jnp.concatenate([wf, qr], axis=0), before32, HIGHEST)
        dld = jnp.concatenate(
            [rowbuf[0:HP] + late[:HP] + early[:HP] + zf, rowbuf[HP : 2 * HP] + late[HP:] + early[HP:] + zr], axis=0)
        dldt = rowbuf[2 * HP : 4 * HP] + jnp.concatenate([wf, wr], axis=0)
        sig = jax.nn.sigmoid(step_ref[:, rows] + bias_ref[...])
        ratio = jnp.where(dt < 1e-30, 1.0, sig / jnp.maximum(dt, 1e-30))
        graw = dldt * ratio - jnp.exp(dlog_ref[...]) * sig * dld
        gstep_ref[:, rows] = graw.astype(BF16)
        heads_ref[:, 0:1] += jnp.sum(graw, axis=1, keepdims=True)
        heads_ref[:, 1:2] += jnp.sum(dld * ld, axis=1, keepdims=True)

    prev = jnp.where(blk == 0, jhalo_ref[...], jprev_ref[...])
    jext[0:16, :] = prev.astype(F32)
    jext[16 : 16 + TB, :] = joined_ref[...].astype(F32)
    tok = iota((TB, 1), 0) + blk * TB
    masks = [conv_mask(tok, m, b, off0) for m in range(4)]
    later_masks = [conv_mask(tok + m, m, b, off0) for m in range(4)]
    edge_masks = [conv_mask(iota((8, 1), 0) - 8 + m, m, b, off0) for m in range(4)]
    for j in range(both // 128):
        cols = slice(j * 128, (j + 1) * 128)
        tap = tapv_ref[:, cols] if j * 128 < inner else taps_ref[:, j * 128 - inner : (j + 1) * 128 - inner]
        shifted = [jext[16 : 16 + TB, cols]]
        total = shifted[0] * tap[3:4]
        for m in range(1, 4):
            shifted.append(jext[16 - m : 16 - m + TB, cols] * masks[m])
            total = total + shifted[m] * tap[3 - m : 4 - m]
        sig = jax.nn.sigmoid(total)
        dconv = dact[:, cols] * (sig * (1.0 + total * (1.0 - sig)))
        ext[0:TB, cols] = dconv
        for m in range(4):
            convg_ref[3 - m : 4 - m, cols] += jnp.sum(dconv * shifted[m], axis=0, keepdims=True)
        grad = dconv * tap[3:4]
        for m in range(1, 4):
            grad = grad + ext[m : m + TB, cols] * later_masks[m] * tap[3 - m : 4 - m]
        if j * 128 < inner:
            gv_ref[:, cols] = grad
        else:
            gs_ref[:, j * 128 - inner : (j + 1) * 128 - inner] = grad

    @pl.when(step_no == nblk - 1)
    def _():
        first = jnp.concatenate([jnp.zeros((8, both), F32), ext[0:8, :]], axis=0)
        tap = jnp.concatenate([tapv_ref[...], taps_ref[...]], axis=1)
        lent = jnp.zeros((8, both), F32)
        for m in range(1, 4):
            lent = lent + first[m : m + 8] * edge_masks[m] * tap[3 - m : 4 - m]
        lent_ref[...] = lent


def down_kernel(gv_ref, gs_ref, next_ref, gstep_ref, ggate_ref, normt_ref, wg_ref, wv_ref, wstep_ref,
                gn_ref, gso_ref, gvw_ref, gstepw_ref,
                gvl):
    blk = pl.program_id(0)
    nblk = pl.num_programs(0)
    inner = wg_ref.shape[1]
    last = (blk == nblk - 1).astype(F32)
    gvl[pl.ds(blk * TB, TB), :] = gv_ref[...].astype(BF16)

    tail = gv_ref[TB - 16 : TB, :] + jnp.concatenate(
        [jnp.zeros((8, inner), F32), next_ref[:, :inner] * last], axis=0)
    gvl[pl.ds(blk * TB + TB - 16, 16), :] = tail.astype(BF16)
    gso_ref[...] = gs_ref[...].astype(BF16)
    tail = gs_ref[TB - 16 : TB, :] + jnp.concatenate(
        [jnp.zeros((8, gs_ref.shape[1]), F32), next_ref[:, inner:] * last], axis=0)
    gso_ref[TB - 16 : TB, :] = tail.astype(BF16)
    gn = nt(ggate_ref[...], wg_ref[...]) + nt(gvl[pl.ds(blk * TB, TB), :], wv_ref[...])
    gn = gn + tn(gstep_ref[:, pl.ds(blk * TB, TB)], wstep_ref[...])
    gn_ref[...] = gn.astype(BF16)

    @pl.when(blk == nblk - 1)
    def _():
        gvw_ref[...] = nn(normt_ref[...], gvl[...]).astype(BF16)
        gstepw_ref[...] = nt(gstep_ref[...], normt_ref[...]).astype(BF16)


def end_kernel(mine_ref, other_ref, smine_ref, sother_ref, hid_ref, cot_ref, gain_ref, ws_ref, normt_ref,
               omine_ref, oother_ref, small_ref, hsum_ref, cmine_ref, cother_ref,
               gh_ref, tiny_ref, gsw_ref, out_ref,
               gsl):
    blk = pl.program_id(0)
    nblk = pl.num_programs(0)
    width = hid_ref.shape[1]
    inner_dev = small_ref.shape[1]

    @pl.when(blk == 0)
    def _():
        tiny_ref[...] = jnp.zeros_like(tiny_ref)
        tiny_ref[0:2, :inner_dev] = small_ref[0:2, :]
        tiny_ref[4:6, 0 : 2 * HP] = hsum_ref[...].T[0:2]
        tiny_ref[8:16, :inner_dev] = cmine_ref[:, :inner_dev]
        tiny_ref[8:16, inner_dev:] = cmine_ref[:, inner_dev:] + cother_ref[:, inner_dev:]

    grad_state = (smine_ref[...].astype(F32) + sother_ref[...].astype(F32)).astype(BF16)
    gsl[pl.ds(blk * TB, TB), :] = grad_state
    gn = mine_ref[...].astype(F32) + other_ref[...].astype(F32) + nt(grad_state, ws_ref[...])
    x = hid_ref[...].astype(F32)
    scale = lax.rsqrt(jnp.mean(x * x, axis=1, keepdims=True) + EPSILON)
    tiny_ref[2:3, :width] += jnp.sum(gn * x * scale, axis=0, keepdims=True)
    v = gn * gain_ref[...]
    inner = jnp.mean(x * v, axis=1, keepdims=True)
    gh_ref[...] = cot_ref[...].astype(F32) + scale * v - x * (scale * scale * scale * inner)
    out_ref[...] = (x + (omine_ref[...].astype(F32) + oother_ref[...].astype(F32))).astype(BF16)

    @pl.when(blk == nblk - 1)
    def _():
        gsw_ref[...] = nn(normt_ref[...], gsl[...]).astype(BF16)


def whole_spec(array):
    zeros = (0,) * array.ndim
    return pl.BlockSpec(array.shape, lambda i: zeros)


def rows_spec(array, rows=TB, flip=0):
    rest = (0,) * (array.ndim - 1)
    if flip:
        return pl.BlockSpec((rows,) + array.shape[1:], lambda i: (flip - 1 - i,) + rest)
    return pl.BlockSpec((rows,) + array.shape[1:], lambda i: (i,) + rest)


def cols_spec(array, flip=0):
    if flip:
        return pl.BlockSpec((array.shape[0], TB), lambda i: (0, flip - 1 - i))
    return pl.BlockSpec((array.shape[0], TB), lambda i: (0, i))


SMEM_SPEC = pl.BlockSpec(memory_space=pltpu.SMEM)


def call(kernel, grid, ins, outs, scratch, vmem, flops):
    arrays = [a for a, _ in ins]
    return pl.pallas_call(
        kernel,
        grid=(grid,),
        in_specs=[s for _, s in ins],
        out_specs=[s for _, s in outs],
        out_shape=[jax.ShapeDtypeStruct(a.shape, a.dtype) for a, _ in outs],
        scratch_shapes=scratch,
        compiler_params=pltpu.CompilerParams(
            dimension_semantics=("arbitrary",), vmem_limit_bytes=vmem * MIB),
        cost_estimate=pl.CostEstimate(
            flops=int(flops), transcendentals=0,
            bytes_accessed=sum(a.size * a.dtype.itemsize for a in arrays)
            + sum(a.size * a.dtype.itemsize for a, _ in outs)),
    )(*arrays)


def padded(x, axis):
    pads = [(0, 0)] * x.ndim
    pads[axis] = (0, HP - x.shape[axis])
    return jnp.pad(x, pads)


def shape(dims, dtype):
    return jax.ShapeDtypeStruct(dims, dtype)


def body(
    hidden_in, norm_gain, gate_proj, value_proj, state_proj, step_proj, conv_value, conv_state,
    step_bias, decay_log, skip_scale, gate_gain, out_proj, lengths, cotangent,
):
    length, width = hidden_in.shape
    inner = gate_proj.shape[1]
    heads = decay_log.shape[0]
    maps = state_proj.shape[1]
    both = inner + maps
    nblk = length // TB
    nchunk = length // Q
    count = lax.axis_size("seq")
    reach = min(1 + (LEN_MOST - 2) // length, count - 1)
    mib = MIB

    halo = lax.ppermute(hidden_in[length - 16 :], "seq", [(i, i + 1) for i in range(count - 1)])
    wstep = padded(step_proj.transpose(0, 2, 1), 1).reshape(2 * HP, width)
    bias = padded(step_bias, 1).reshape(2 * HP, 1)
    dlog = padded(decay_log, 0)
    dlog = jnp.concatenate([dlog, dlog]).reshape(2 * HP, 1)
    skip = padded(skip_scale, 0).reshape(HP, 1)
    gain_in = norm_gain.reshape(1, width)
    gain_gate = gate_gain.reshape(1, inner)

    normt = shape((width, length), BF16)
    gate = shape((length, inner), F32)
    joined = shape((length, both), BF16)
    jhalo = shape((16, both), BF16)
    act = shape((length, both), BF16)
    step = shape((2 * HP, length), F32)
    inc = shape((nchunk, 128, inner), F32)
    pexp = shape((nchunk, 2, inner), F32)
    msg = shape((80, inner), BF16)
    meta = shape((8,), jnp.int32)
    cq = TB // Q
    meta, normt, gate, joined, jhalo, act, step, inc, pexp, msgf, msgr = call(
        front_kernel, nblk,
        [(lengths, SMEM_SPEC), (hidden_in, rows_spec(hidden_in)), (halo, whole_spec(halo)),
         (gain_in, whole_spec(gain_in)), (gate_proj, whole_spec(gate_proj)), (value_proj, whole_spec(value_proj)),
         (state_proj, whole_spec(state_proj)), (wstep, whole_spec(wstep)), (conv_value, whole_spec(conv_value)),
         (conv_state, whole_spec(conv_state)), (bias, whole_spec(bias)), (dlog, whole_spec(dlog))],
        [(meta, SMEM_SPEC), (normt, cols_spec(normt)), (gate, rows_spec(gate)), (joined, rows_spec(joined)),
         (jhalo, whole_spec(jhalo)), (act, rows_spec(act)), (step, cols_spec(step)), (inc, rows_spec(inc, cq)),
         (pexp, rows_spec(pexp, cq)), (msg, whole_spec(msg)), (msg, whole_spec(msg))],
        [pltpu.VMEM((TB + 8, both), F32), pltpu.VMEM((64, inner), F32), pltpu.VMEM((64, inner), F32),
         pltpu.VMEM((8, inner), F32)],
        48, 2 * length * width * (2 * inner + maps))
    low, high = swap(msgf, msgr, reach, 1)

    mixed = shape((length, inner), F32)
    state = shape((nchunk, 128, inner), BF16)
    sums = shape((8, length), F32)
    mixed, state, sums = call(
        mix_kernel, nblk,
        [(meta, SMEM_SPEC), (act, rows_spec(act)), (step, cols_spec(step)), (bias, whole_spec(bias)),
         (dlog, whole_spec(dlog)), (gate, rows_spec(gate)), (cotangent, rows_spec(cotangent)),
         (out_proj, whole_spec(out_proj)), (gain_gate, whole_spec(gain_gate)), (skip, whole_spec(skip)),
         (inc, whole_spec(inc)), (pexp, whole_spec(pexp)), (low, whole_spec(low)), (high, whole_spec(high))],
        [(mixed, rows_spec(mixed)), (state, whole_spec(state)), (sums, cols_spec(sums))],
        [], 48, 2 * length * width * inner * 2)
    (sums_other,) = core_swap([sums], 2)

    out_part = shape((length, width), BF16)
    ggate = shape((length, inner), BF16)
    dy = shape((length, inner), F32)
    dhy = shape((nchunk, 128, inner), F32)
    small = shape((8, inner), F32)
    ggw = shape((width, inner), BF16)
    ng = shape((nblk, TB, inner), BF16)
    out_part, ggate, dy, dhy, msgf, msgr, small, ggw, ng = call(
        gate_kernel, nblk,
        [(meta, SMEM_SPEC), (sums, cols_spec(sums)), (sums_other, cols_spec(sums_other)), (mixed, rows_spec(mixed)),
         (gate, rows_spec(gate)), (cotangent, rows_spec(cotangent)), (out_proj, whole_spec(out_proj)),
         (gain_gate, whole_spec(gain_gate)), (act, rows_spec(act)), (step, cols_spec(step)),
         (bias, whole_spec(bias)), (dlog, whole_spec(dlog)), (pexp, whole_spec(pexp)), (normt, whole_spec(normt))],
        [(out_part, rows_spec(out_part)), (ggate, whole_spec(ggate)), (dy, rows_spec(dy)),
         (dhy, rows_spec(dhy, cq)), (msg, whole_spec(msg)), (msg, whole_spec(msg)), (small, whole_spec(small)),
         (ggw, whole_spec(ggw)), (ng, whole_spec(ng))],
        [pltpu.VMEM((64, inner), F32), pltpu.VMEM((64, inner), F32), pltpu.VMEM((8, inner), F32)],
        48, 2 * length * width * inner * 4)
    low, high = swap(msgr, msgf, reach, 3)

    ng = ng.reshape(length, inner)
    gow = shape((inner, width), BF16)
    (gow,) = call(
        outgrad_kernel, 1, [(ng, whole_spec(ng)), (cotangent, whole_spec(cotangent))], [(gow, whole_spec(gow))],
        [], 32, 2 * length * width * inner)

    gv = shape((length, inner), F32)
    gs = shape((length, maps), F32)
    gstep = shape((2 * HP, length), BF16)
    lent = shape((8, both), F32)
    convg = shape((8, both), F32)
    hsum = shape((2 * HP, 128), F32)
    prev_spec = pl.BlockSpec((16, both), lambda i: (jnp.maximum((nblk - 1 - i) * (TB // 16) - 1, 0), 0))
    gv, gs, gstep, lent, convg, hsum = call(
        back_kernel, nblk,
        [(meta, SMEM_SPEC), (act, rows_spec(act, TB, nblk)), (step, cols_spec(step, nblk)), (bias, whole_spec(bias)),
         (dlog, whole_spec(dlog)), (dy, rows_spec(dy, TB, nblk)), (skip, whole_spec(skip)),
         (state, whole_spec(state)), (dhy, whole_spec(dhy)), (pexp, whole_spec(pexp)), (low, whole_spec(low)),
         (high, whole_spec(high)), (joined, rows_spec(joined, TB, nblk)), (joined, prev_spec),
         (jhalo, whole_spec(jhalo)), (conv_value, whole_spec(conv_value)), (conv_state, whole_spec(conv_state))],
        [(gv, rows_spec(gv, TB, nblk)), (gs, rows_spec(gs, TB, nblk)), (gstep, cols_spec(gstep, nblk)),
         (lent, whole_spec(lent)), (convg, whole_spec(convg)), (hsum, whole_spec(hsum))],
        [pltpu.VMEM((nchunk, 128, inner), BF16), pltpu.VMEM((TB + 8, both), F32), pltpu.VMEM((TB + 16, both), F32),
         pltpu.VMEM((4 * HP, Q), F32), pltpu.VMEM((TB, both), F32)],
        56, 2 * length * width * inner * 4)
    from_next = lax.ppermute(lent, "seq", [(i + 1, i) for i in range(count - 1)])

    gn = shape((length, width), BF16)
    gso = shape((length, maps), BF16)
    gvw = shape((width, inner), BF16)
    gstepw = shape((2 * HP, width), BF16)
    gn, gso, gvw, gstepw = call(
        down_kernel, nblk,
        [(gv, rows_spec(gv)), (gs, rows_spec(gs)), (from_next, whole_spec(from_next)), (gstep, whole_spec(gstep)),
         (ggate, rows_spec(ggate)), (normt, whole_spec(normt)), (gate_proj, whole_spec(gate_proj)),
         (value_proj, whole_spec(value_proj)), (wstep, whole_spec(wstep))],
        [(gn, rows_spec(gn)), (gso, rows_spec(gso)), (gvw, whole_spec(gvw)), (gstepw, whole_spec(gstepw))],
        [pltpu.VMEM((length, inner), BF16)],
        48, 2 * length * width * inner * 3)
    gn_other, gso_other, out_other, convg_other = core_swap([gn, gso, out_part, convg], 4)

    gh = shape((length, width), F32)
    tiny = shape((16, both), F32)
    gsw = shape((width, maps), BF16)
    out = shape((length, width), BF16)
    gh, tiny, gsw, out = call(
        end_kernel, nblk,
        [(gn, rows_spec(gn)), (gn_other, rows_spec(gn_other)), (gso, rows_spec(gso)),
         (gso_other, rows_spec(gso_other)), (hidden_in, rows_spec(hidden_in)), (cotangent, rows_spec(cotangent)),
         (gain_in, whole_spec(gain_in)), (state_proj, whole_spec(state_proj)), (normt, whole_spec(normt)),
         (out_part, rows_spec(out_part)), (out_other, rows_spec(out_other)), (small, whole_spec(small)),
         (hsum, whole_spec(hsum)), (convg, whole_spec(convg)), (convg_other, whole_spec(convg_other))],
        [(gh, rows_spec(gh)), (tiny, whole_spec(tiny)), (gsw, whole_spec(gsw)), (out, rows_spec(out))],
        [pltpu.VMEM((length, maps), BF16)],
        48, 2 * length * width * maps * 2)

    (ggw, gow, gvw, gsw, gstepw), tiny = reduce_all([ggw, gow, gvw, gsw, gstepw], tiny, count, 5)
    gstepw = gstepw.astype(F32).reshape(2, HP, width)[:, :heads].transpose(0, 2, 1)
    hsum = tiny[4:6, : 2 * HP].reshape(2, 2, HP)[:, :, :heads]
    return (
        out,
        gh,
        tiny[2, :width],
        ggw.astype(F32),
        gvw.astype(F32),
        gsw.astype(F32),
        gstepw,
        tiny[8:12, :inner],
        tiny[8:12, inner:],
        hsum[0],
        hsum[1, 0] + hsum[1, 1],
        jnp.sum(tiny[1, :inner].reshape(heads, inner // heads), axis=1),
        tiny[0, :inner],
        gow.astype(F32),
    )


def solution(mesh):
    in_specs = (
        P("seq", None),
        P(),
        P(None, "head"),
        P(None, "head"),
        P(),
        P(None, None, "head"),
        P(None, "head"),
        P(),
        P(None, "head"),
        P("head"),
        P("head"),
        P("head"),
        P("head", None),
        P(),
        P("seq", None),
    )
    out_specs = (
        P("seq", None),
        P("seq", None),
        P(),
        P(None, "head"),
        P(None, "head"),
        P(),
        P(None, None, "head"),
        P(None, "head"),
        P(),
        P(None, "head"),
        P("head"),
        P("head"),
        P("head"),
        P("head", None),
    )
    return jax.shard_map(body, mesh=mesh, in_specs=in_specs, out_specs=out_specs, check_vma=False)
```

```python
from functools import partial

import jax
import jax.numpy as jnp
from jax import lax
from jax.experimental import pallas as pl
from jax.experimental.pallas import tpu as pltpu
from jax.sharding import PartitionSpec as P

EPSILON = 1e-05
LEN_MOST = 4096
Q = 128
TB = 256
HP = 16
MIB = 1024 * 1024
HIGHEST = lax.Precision.HIGHEST
F32 = jnp.float32
BF16 = jnp.bfloat16
MESH = pl.DeviceIdType.MESH


def nn(a, b, precision=None):
    return jnp.dot(a, b, preferred_element_type=F32, precision=precision)


def nt(a, b, precision=None):
    return lax.dot_general(a, b, (((1,), (1,)), ((), ())), preferred_element_type=F32, precision=precision)


def tn(a, b, precision=None):
    return lax.dot_general(a, b, (((0,), (0,)), ((), ())), preferred_element_type=F32, precision=precision)


def iota(shape, axis):
    return lax.broadcasted_iota(jnp.int32, shape, axis)


def spread_matrix(width, hdim):
    return (iota((HP, width), 1) // hdim == iota((HP, width), 0)).astype(F32)


def split(x):
    hi = x.astype(BF16)
    return hi, (x - hi.astype(F32)).astype(BF16)


def widen(rows, spread2):
    hi, lo = split(rows.T)
    return nn(jnp.concatenate([hi, lo], axis=1), spread2)


def widen_col(col, spread):
    return tn(jnp.broadcast_to(col, (HP, 8)), spread, HIGHEST)[0:1]


def silu(x):
    return x * jax.nn.sigmoid(x)


def softplus(x):
    return jnp.maximum(x, 0.0) + jnp.log1p(jnp.exp(-jnp.abs(x)))


def step_parts(step, bias, dlog):
    dt = softplus(step + bias)
    ld = -jnp.exp(dlog) * dt
    upto = (iota((Q, Q), 0) <= iota((Q, Q), 1)).astype(F32)
    run = nn(ld, upto, HIGHEST)
    return dt, ld, run, run - ld


def state_factors(dt, run, bef, t0, b):
    t1 = t0 + Q
    tok = iota((1, Q), 1) + t0
    ef = jnp.where((tok < b) | (t0 > b), jnp.exp(bef[:HP]), 0.0)
    er = jnp.where((tok >= b) | (t1 < b), jnp.exp(run[HP:, Q - 1 : Q] - run[HP:]), 0.0)
    tf = jnp.where((tok >= b) | (t1 <= b), jnp.exp(run[:HP, Q - 1 : Q] - run[:HP]), 0.0) * dt[:HP]
    tr = jnp.where((tok < b) | (t0 >= b), jnp.exp(bef[HP:]), 0.0) * dt[HP:]
    return ef, er, tf, tr


def conv_mask(tok, shift, b, off0):
    lost = ((tok < b) & (tok + off0 < shift)) | ((tok >= b) & (tok < b + shift))
    return jnp.where(lost, 0.0, 1.0)


def put_message(ref, state, passed):
    hi, lo = split(passed)
    ref[0:64, :] = state.astype(BF16)
    row = iota((16, state.shape[1]), 0)
    tail = jnp.where(row == 0, hi.astype(F32), jnp.where(row == 1, lo.astype(F32), 0.0))
    ref[64:80, :] = tail.astype(BF16)


def chain(ref):
    total = ref[0, 0:64, :].astype(F32)
    passed = None
    for k in range(1, ref.shape[0]):
        tail = ref[k - 1, 64:80, :].astype(F32)
        here = tail[0:1] + tail[1:2]
        passed = here if passed is None else passed * here
        total = total + passed * ref[k, 0:64, :].astype(F32)
    return total


def front_kernel(len_ref, hid_ref, halo_ref, gain_ref, wg_ref, wv_ref, ws_ref, wstep_ref, tapv_ref, taps_ref,
                 bias_ref, dlog_ref,
                 meta_ref, normt_ref, gate_ref, joined_ref, jhalo_ref, act_ref, step_ref, inc_ref, pexp_ref,
                 msgf_ref, msgr_ref,
                 ext, sumf, sumr, prod):
    blk = pl.program_id(0)
    nblk = pl.num_programs(0)
    inner = wv_ref.shape[1]
    both = inner + ws_ref.shape[1]
    base = lax.axis_index("seq") * (TB * nblk)
    length = TB * nblk

    @pl.when(blk == 0)
    def _():
        def one(j, carry):
            start, b, off0, after = carry
            end = start + len_ref[j]
            b = jnp.where((start > base) & (start < base + length), start - base, b)
            off0 = jnp.where((start <= base) & (base < end), base - start, off0)
            after = jnp.where(end == base + length, 0, after)
            return end, b, off0, after

        _, b, off0, after = lax.fori_loop(
            0, len_ref.shape[0], one, (jnp.int32(0), jnp.int32(length + 1), jnp.int32(0), jnp.int32(1)))
        meta_ref[0] = b
        meta_ref[1] = off0
        meta_ref[2] = jnp.where(off0 > 0, 1, 0).astype(jnp.int32)
        meta_ref[3] = after

    b = meta_ref[0]
    off0 = meta_ref[1]

    def norm(x):
        x = x.astype(F32)
        scale = lax.rsqrt(jnp.mean(x * x, axis=1, keepdims=True) + EPSILON)
        return (x * scale * gain_ref[...]).astype(BF16)

    @pl.when(blk == 0)
    def _():
        nh = norm(halo_ref[...])
        pre = jnp.concatenate([nn(nh, wv_ref[...]), nn(nh, ws_ref[...])], axis=1).astype(BF16)
        jhalo_ref[...] = pre
        ext[0:8, :] = pre.astype(F32)[8:16]
        sumf[...] = jnp.zeros_like(sumf)
        sumr[...] = jnp.zeros_like(sumr)
        prod[...] = jnp.ones_like(prod)

    @pl.when(blk > 0)
    def _():
        ext[0:8, :] = ext[TB : TB + 8, :]

    x = hid_ref[...].astype(F32)
    scale = lax.rsqrt(jnp.mean(x * x, axis=1, keepdims=True) + EPSILON)
    normed32 = x * scale * gain_ref[...]
    normed = normed32.astype(BF16)
    normt_ref[...] = normed.T
    gate_ref[...] = nn(normed, wg_ref[...])
    jv = nn(normed, wv_ref[...]).astype(BF16)
    js = nn(normed, ws_ref[...]).astype(BF16)
    joined_ref[:, :inner] = jv
    joined_ref[:, inner:] = js
    ext[8 : 8 + TB, :inner] = jv.astype(F32)
    ext[8 : 8 + TB, inner:] = js.astype(F32)
    step_all = nt(wstep_ref[...], normed)
    step_ref[...] = step_all
    tok = iota((TB, 1), 0) + blk * TB
    masks = [conv_mask(tok, m, b, off0) for m in range(4)]
    for j in range(both // 128):
        cols = slice(j * 128, (j + 1) * 128)
        tap = tapv_ref[:, cols] if j * 128 < inner else taps_ref[:, j * 128 - inner : (j + 1) * 128 - inner]
        total = ext[8 : 8 + TB, cols] * tap[3:4]
        for m in range(1, 4):
            total = total + ext[8 - m : 8 - m + TB, cols] * tap[3 - m : 4 - m] * masks[m]
        act_ref[:, cols] = silu(total).astype(BF16)
    spread = spread_matrix(inner, 64)
    spread2 = jnp.concatenate([spread, spread], axis=0).astype(BF16)
    for q in range(TB // Q):
        rows = slice(q * Q, (q + 1) * Q)
        t0 = blk * TB + q * Q
        dt, ld, run, bef = step_parts(step_all[:, rows], bias_ref[...], dlog_ref[...])
        _, _, tf, tr = state_factors(dt, run, bef, t0, b)
        values = act_ref[rows, :inner].astype(F32)
        maps_t = act_ref[rows, inner:].astype(F32).T.astype(BF16)
        incf = nn(maps_t[0:64], (values * widen(tf, spread2)).astype(BF16))
        incr = nn(maps_t[128:192], (values * widen(tr, spread2)).astype(BF16))
        inc_ref[q, 0:64, :] = incf
        inc_ref[q, 64:128, :] = incr
        gone = jnp.exp(run[:, Q - 1 : Q])
        passf = jnp.where((t0 <= b) & (b < t0 + Q), 0.0, 1.0)
        passr = jnp.where((t0 < b) & (b <= t0 + Q), 0.0, 1.0)
        pf = widen_col(gone[:HP], spread) * passf
        pr = widen_col(gone[HP:], spread) * passr
        pexp_ref[q, 0:1, :] = pf
        pexp_ref[q, 1:2, :] = pr
        sumf[...] = pf * sumf[...] + incf
        sumr[...] = sumr[...] + prod[1:2, :] * incr
        prod[0:1, :] = prod[0:1, :] * pf
        prod[1:2, :] = prod[1:2, :] * pr

    @pl.when(blk == nblk - 1)
    def _():
        put_message(msgf_ref, sumf[...], prod[0:1, :] * meta_ref[2].astype(F32))
        put_message(msgr_ref, sumr[...], prod[1:2, :] * meta_ref[3].astype(F32))


class Swap:
    def __init__(self, reach, up_ref, down_ref, from_low, from_high, up_send, up_recv, down_send, down_recv):
        self.me, self.core, self.count = lax.axis_index("seq"), lax.axis_index("head"), lax.axis_size("seq")
        self.reach, self.up_ref, self.down_ref, self.from_low, self.from_high = reach, up_ref, down_ref, from_low, from_high
        self.sems = up_send, up_recv, down_send, down_recv

    def up(self, k):
        return pltpu.make_async_remote_copy(
            src_ref=self.up_ref, dst_ref=self.from_low.at[k - 1], send_sem=self.sems[0].at[k - 1],
            recv_sem=self.sems[1].at[k - 1], device_id=(self.me + k, self.core), device_id_type=MESH)

    def down(self, k):
        return pltpu.make_async_remote_copy(
            src_ref=self.down_ref, dst_ref=self.from_high.at[k - 1], send_sem=self.sems[2].at[k - 1],
            recv_sem=self.sems[3].at[k - 1], device_id=(self.me - k, self.core), device_id_type=MESH)

    def greet(self, barrier):
        me, core, count = self.me, self.core, self.count
        for k in range(1, self.reach + 1):
            @pl.when(me + k < count)
            def _():
                pl.semaphore_signal(barrier, inc=1, device_id=(me + k, core), device_id_type=MESH)

            @pl.when(me >= k)
            def _():
                pl.semaphore_signal(barrier, inc=1, device_id=(me - k, core), device_id_type=MESH)
        return jnp.minimum(me, self.reach) + jnp.minimum(count - 1 - me, self.reach)

    def start(self):
        me, count = self.me, self.count
        for k in range(1, self.reach + 1):
            @pl.when(me + k < count)
            def _():
                self.up(k).start()

            @pl.when(me >= k)
            def _():
                self.down(k).start()

            @pl.when(me < k)
            def _():
                self.from_low[k - 1] = jnp.zeros_like(self.from_low[k - 1])

            @pl.when(me + k >= count)
            def _():
                self.from_high[k - 1] = jnp.zeros_like(self.from_high[k - 1])

    def finish(self):
        me, count = self.me, self.count
        for k in range(1, self.reach + 1):
            @pl.when(me + k < count)
            def _():
                self.up(k).wait_send()
                self.down(k).wait_recv()

            @pl.when(me >= k)
            def _():
                self.down(k).wait_send()
                self.up(k).wait_recv()


def swap_scratch(reach, inner):
    return [pltpu.VMEM((reach, 80, inner), BF16)] * 2 + [pltpu.SemaphoreType.DMA((reach,))] * 4


def core_swap_kernel(count, *refs):
    ins, outs, (send, recv) = refs[:count], refs[count : 2 * count], refs[2 * count :]
    me = lax.axis_index("seq")
    other = 1 - lax.axis_index("head")
    barrier = pltpu.get_barrier_semaphore()
    pl.semaphore_signal(barrier, inc=1, device_id=(me, other), device_id_type=MESH)
    pl.semaphore_wait(barrier, 1)
    copies = [
        pltpu.make_async_remote_copy(
            src_ref=ins[i], dst_ref=outs[i], send_sem=send.at[i], recv_sem=recv.at[i],
            device_id=(me, other), device_id_type=MESH)
        for i in range(count)
    ]
    for copy in copies:
        copy.start()
    for copy in copies:
        copy.wait()


def core_swap(arrays, ident):
    count = len(arrays)
    vm = pl.BlockSpec(memory_space=pltpu.VMEM)
    return pl.pallas_call(
        partial(core_swap_kernel, count),
        out_shape=tuple(jax.ShapeDtypeStruct(a.shape, a.dtype) for a in arrays),
        in_specs=[vm] * count,
        out_specs=(vm,) * count,
        scratch_shapes=[pltpu.SemaphoreType.DMA((count,))] * 2,
        compiler_params=pltpu.CompilerParams(
            collective_id=ident, has_side_effects=True, vmem_limit_bytes=32 * MIB),
    )(*arrays)


def pieces_of(arrays, bits):
    found = []
    for a, array in enumerate(arrays):
        rows, cols = array.shape
        halvings = 0
        while halvings < bits and (rows >> halvings) % 32 == 0:
            halvings += 1
        parts = 2 if rows * cols >= 512 * 512 else 1
        for p in range(parts):
            order = list(range(bits))
            if len(found) % 2 and bits > 1:
                order[0], order[1] = order[1], order[0]
            found.append((a, p * (cols // parts), cols // parts, order, halvings))
    return found


def reduce_kernel(count, bits, *refs):
    ins, tiny_ref = refs[:count], refs[count]
    outs, tiny_out = refs[count + 1 : 2 * count + 1], refs[2 * count + 1]
    works, recvs = refs[2 * count + 2 : 3 * count + 2], refs[3 * count + 2 : 4 * count + 2]
    tiny_work, tiny_recv, rs_send, rs_recv, ag_send, ag_recv, t_send, t_recv = refs[4 * count + 2 :]
    me = lax.axis_index("seq")
    core = lax.axis_index("head")
    bit = [lax.rem(me // (1 << k), 2) for k in range(bits)]
    partner = [me + (1 - 2 * bit[k]) * (1 << k) for k in range(bits)]
    pieces = pieces_of(ins, bits)

    barrier = pltpu.get_barrier_semaphore()
    for k in range(bits):
        pl.semaphore_signal(barrier, inc=1, device_id=(partner[k], core), device_id_type=MESH)
    pl.semaphore_wait(barrier, bits)

    def remote(src, dst, send, recv, k):
        return pltpu.make_async_remote_copy(
            src_ref=src, dst_ref=dst, send_sem=send, recv_sem=recv, device_id=(partner[k], core),
            device_id_type=MESH)

    state = []
    for p, (a, c0, cols, order, halvings) in enumerate(pieces):
        state.append({"off": jnp.int32(0), "size": ins[a].shape[0], "slot": 0, "copy": None})

    def rs_start(p, s):
        a, c0, cols, order, halvings = pieces[p]
        st = state[p]
        k = order[s]
        src = ins[a] if s == 0 else works[a]
        half = st["size"] // 2 if s < halvings else st["size"]
        if s < halvings:
            st["keep"] = pl.multiple_of(st["off"] + bit[k] * half, 16)
            st["give"] = pl.multiple_of(st["off"] + (1 - bit[k]) * half, 16)
        else:
            st["keep"] = st["give"] = st["off"]
        st["half"] = half
        st["copy"] = remote(
            src.at[pl.ds(st["give"], half), pl.ds(c0, cols)],
            recvs[a].at[pl.ds(st["slot"], half), pl.ds(c0, cols)],
            rs_send.at[p, s], rs_recv.at[p, s], k)
        st["copy"].start()

    def rs_finish(p, s):
        a, c0, cols, order, halvings = pieces[p]
        st = state[p]
        half, keep, slot = st["half"], st["keep"], st["slot"]
        if s < halvings:
            st["copy"].wait_recv()
            st.setdefault("sends", []).append(st["copy"])
        else:
            st["copy"].wait()
        src = ins[a] if s == 0 else works[a]
        dst = outs[a] if s == bits - 1 else works[a]
        step = 48 if half % 48 == 0 else 16

        def add(i, _):
            r = pl.multiple_of(keep + i * step, 16)
            q = pl.multiple_of(slot + i * step, 16)
            total = src[pl.ds(r, step), pl.ds(c0, cols)].astype(F32) + recvs[a][pl.ds(q, step), pl.ds(c0, cols)].astype(F32)
            dst[pl.ds(r, step), pl.ds(c0, cols)] = total.astype(BF16)
            return 0

        lax.fori_loop(0, half // step, add, 0)
        st["off"], st["size"], st["slot"] = keep, half, slot + half

    def ag_start(p, s):
        a, c0, cols, order, halvings = pieces[p]
        st = state[p]
        k = order[s]
        where = outs[a].at[pl.ds(st["off"], st["size"]), pl.ds(c0, cols)]
        st["copy"] = remote(where, where, ag_send.at[p, s], ag_recv.at[p, s], k)
        st["copy"].start()

    def ag_finish(p, s):
        a, c0, cols, order, halvings = pieces[p]
        st = state[p]
        st["copy"].wait_recv()
        st["sends"].append(st["copy"])
        st["off"] = pl.multiple_of(st["off"] - bit[order[s]] * st["size"], 16)
        st["size"] = 2 * st["size"]

    def tiny_copy(s):
        src = tiny_ref if s == 0 else tiny_work.at[s - 1]
        return remote(src, tiny_recv.at[s], t_send.at[s], t_recv.at[s], s)

    every = range(len(pieces))
    for p in every:
        rs_start(p, 0)
    tiny_copy(0).start()
    for s in range(bits):
        for p in every:
            rs_finish(p, s)
            if s + 1 < bits:
                rs_start(p, s + 1)
            elif pieces[p][4]:
                ag_start(p, pieces[p][4] - 1)
        tiny_copy(s).wait()
        total = (tiny_ref[...] if s == 0 else tiny_work[s - 1]) + tiny_recv[s]
        if s + 1 < bits:
            tiny_work[s] = total
            tiny_copy(s + 1).start()
        else:
            tiny_out[...] = total
    for back in range(bits):
        for p in every:
            s = pieces[p][4] - 1 - back
            if s >= 0:
                ag_finish(p, s)
                if s > 0:
                    ag_start(p, s - 1)
    for p in every:
        for copy in state[p].get("sends", []):
            copy.wait_send()


def reduce_all(arrays, tiny, devices, ident):
    count = len(arrays)
    bits = devices.bit_length() - 1
    assert devices == 1 << bits
    npieces = len(pieces_of(arrays, bits))
    vm = pl.BlockSpec(memory_space=pltpu.VMEM)
    received = []
    for array in arrays:
        rows, halvings = array.shape[0], pieces_of([array], bits)[0][4]
        total = 0
        for s in range(bits):
            rows = rows // 2 if s < halvings else rows
            total += rows
        received.append(total)
    outs = pl.pallas_call(
        partial(reduce_kernel, count, bits),
        out_shape=[jax.ShapeDtypeStruct(a.shape, a.dtype) for a in arrays + [tiny]],
        in_specs=[vm] * (count + 1),
        out_specs=[vm] * (count + 1),
        scratch_shapes=[pltpu.VMEM(a.shape, a.dtype) for a in arrays]
        + [pltpu.VMEM((r, a.shape[1]), a.dtype) for r, a in zip(received, arrays)]
        + [pltpu.VMEM((bits,) + tiny.shape, F32), pltpu.VMEM((bits,) + tiny.shape, F32)]
        + [pltpu.SemaphoreType.DMA((npieces, bits))] * 4
        + [pltpu.SemaphoreType.DMA((bits,))] * 2,
        compiler_params=pltpu.CompilerParams(
            collective_id=ident, has_side_effects=True, vmem_limit_bytes=48 * MIB),
    )(*arrays, tiny)
    return outs[:count], outs[count]


def chunk_scores(maps, t0, b):
    tr, tc = iota((Q, Q), 0), iota((Q, Q), 1)
    same = (tr + t0 < b) == (tc + t0 < b)
    fwd = nt(maps[:, 64:128], maps[:, 0:64])
    rev = nt(maps[:, 192:256], maps[:, 128:192])
    return jnp.where((tr > tc) & same, fwd, jnp.where((tr < tc) & same, rev, 0.0))


def halves(x):
    left = iota(x.shape, 1) < 64
    zero = jnp.zeros_like(x)
    return jnp.concatenate([jnp.where(left, x, zero), jnp.where(left, zero, x)], axis=0)


def mix_kernel(reach, meta_ref, act_ref, step_ref, bias_ref, dlog_ref, gate_ref, cot_ref, wo_ref, ggain_ref, skip_ref,
               inc_ref, pexp_ref, msgf_ref, msgr_ref, normt_ref,
               state_ref, out_ref, ggate_ref, dy_ref, dhy_ref, gmsgf_ref, gmsgr_ref, small_ref, ggw_ref, gow_ref,
               mixed_ref, ngt, mine, other, gsum_f, gsum_r, prod, s_send, s_recv,
               from_low, from_high, up_send, up_recv, down_send, down_recv):
    turn = pl.program_id(0)
    nblk = pl.num_programs(0) // 3
    blk = lax.rem(turn, nblk)
    inner = wo_ref.shape[0]
    whole = inner * 2
    nchunk = inc_ref.shape[0]
    b = meta_ref[0]
    swap = Swap(reach, msgf_ref, msgr_ref, from_low, from_high, up_send, up_recv, down_send, down_recv)
    me, partner = lax.axis_index("seq"), 1 - lax.axis_index("head")
    place = pl.ds(pl.multiple_of(blk * TB, TB), TB)

    def sums_copy(k):
        return pltpu.make_async_remote_copy(
            src_ref=mine.at[k], dst_ref=other.at[k], send_sem=s_send.at[k], recv_sem=s_recv.at[k],
            device_id=(me, partner), device_id_type=MESH)

    @pl.when(turn == 0)
    def _():
        barrier = pltpu.get_barrier_semaphore()
        near = swap.greet(barrier)
        pl.semaphore_signal(barrier, inc=1, device_id=(me, partner), device_id_type=MESH)
        pl.semaphore_wait(barrier, near + 1)
        swap.start()
        gsum_f[...] = jnp.zeros_like(gsum_f)
        gsum_r[...] = jnp.zeros_like(gsum_r)
        prod[...] = jnp.ones_like(prod)
        small_ref[...] = jnp.zeros_like(small_ref)

    spread = spread_matrix(inner, 64)
    spread2 = jnp.concatenate([spread, spread], axis=0).astype(BF16)

    @pl.when(turn < nblk)
    def _():
        skip = widen_col(skip_ref[...], spread)
        lower = iota((Q, Q), 0) > iota((Q, Q), 1)
        for q in range(TB // Q):
            rows = slice(q * Q, (q + 1) * Q)
            dest = pl.ds(pl.multiple_of(blk * TB + q * Q, Q), Q)
            t0 = blk * TB + q * Q
            dt, ld, run, bef = step_parts(step_ref[:, rows], bias_ref[...], dlog_ref[...])
            ldt = jnp.log(jnp.maximum(dt, 1e-37))
            rowf = ldt[:HP] - run[:HP]
            rowr = ldt[HP:] + bef[HP:]
            cols = jnp.concatenate([bef[:HP], -run[HP:]], axis=0).T
            scores = chunk_scores(act_ref[rows, inner:], t0, b)
            for j in range(inner // 128):
                lanes = slice(j * 128, (j + 1) * 128)
                weights = []
                for h in (2 * j, 2 * j + 1):
                    e = jnp.where(lower, cols[:, h : h + 1] + rowf[h : h + 1],
                                  cols[:, HP + h : HP + h + 1] + rowr[h : h + 1])
                    weights.append((jnp.exp(jnp.minimum(e, 60.0)) * scores).astype(BF16))
                vp = act_ref[rows, lanes]
                y = nn(jnp.concatenate(weights, axis=1), halves(vp))
                mixed_ref[dest, lanes] = y + skip[:, lanes] * vp.astype(F32)

    @pl.when(turn == nblk)
    def _():
        swap.finish()
        hf = chain(from_low) * meta_ref[2].astype(F32)
        hr = chain(from_high) * meta_ref[3].astype(F32)
        for c in range(nchunk):
            state_ref[c, 0:64, :] = hf.astype(BF16)
            hf = pexp_ref[c, 0:1, :] * hf + inc_ref[c, 0:64, :]
            d = nchunk - 1 - c
            state_ref[d, 64:128, :] = hr.astype(BF16)
            hr = pexp_ref[d, 1:2, :] * hr + inc_ref[d, 64:128, :]

    @pl.when((turn >= nblk) & (turn < 2 * nblk))
    def _():
        lane = iota((Q, 128), 1)
        u_all = nt(cot_ref[place, :], wo_ref[...])
        for q in range(TB // Q):
            rows = slice(q * Q, (q + 1) * Q)
            dest = pl.ds(pl.multiple_of(blk * TB + q * Q, Q), Q)
            t0 = blk * TB + q * Q
            dt, ld, run, bef = step_parts(step_ref[:, rows], bias_ref[...], dlog_ref[...])
            ef, er, _, _ = state_factors(dt, run, bef, t0, b)
            maps = act_ref[rows, inner:]
            state = state_ref[blk * (TB // Q) + q]
            ys = nn(maps[:, 64:128], state[0:64]) * widen(ef, spread2)
            ys = ys + nn(maps[:, 192:256], state[64:128]) * widen(er, spread2)
            square = jnp.zeros((Q, 1), F32)
            cross = jnp.zeros((Q, 1), F32)
            for j in range(inner // 128):
                lanes = slice(j * 128, (j + 1) * 128)
                y = mixed_ref[dest, lanes] + ys[:, lanes]
                mixed_ref[dest, lanes] = y
                gated = y * silu(gate_ref[rows, lanes])
                square = square + jnp.sum(gated * gated, axis=1, keepdims=True)
                cross = cross + jnp.sum(gated * (u_all[rows, lanes] * ggain_ref[:, lanes]), axis=1, keepdims=True)
            both = jnp.where(lane == 0, square, jnp.where(lane == 1, cross, 0.0))
            mine[blk, :, rows] = both.T[0:8]
        sums_copy(blk).start()

    @pl.when(turn >= 2 * nblk)
    def _():
        sums_copy(blk).wait()
        sums = mine[blk] + other[blk]
        sums = jnp.concatenate([sums, jnp.zeros((120, TB), F32)], axis=0).T
        scale = lax.rsqrt(sums[:, 0:1] / whole + EPSILON)
        back = scale * scale * scale * sums[:, 1:2] / whole
        gng = nt(cot_ref[place, :], wo_ref[...])
        for j in range(inner // 128):
            lanes = slice(j * 128, (j + 1) * 128)
            mixed = mixed_ref[place, lanes]
            pre = gate_ref[:, lanes]
            sig = jax.nn.sigmoid(pre)
            gated = mixed * (pre * sig)
            ng = gated * scale
            gain = ggain_ref[:, lanes]
            ngt[place, lanes] = (ng * gain).astype(BF16)
            g = gng[:, lanes]
            small_ref[0:1, lanes] += jnp.sum(g * ng, axis=0, keepdims=True)
            grad_gated = scale * (g * gain) - gated * back
            dy = grad_gated * (pre * sig)
            small_ref[1:2, lanes] += jnp.sum(dy * act_ref[:, lanes].astype(F32), axis=0, keepdims=True)
            dy_ref[:, lanes] = dy
            ggate_ref[place, lanes] = (grad_gated * mixed * (sig * (1.0 + pre * (1.0 - sig)))).astype(BF16)
        out_ref[...] = nn(ngt[place, :], wo_ref[...]).astype(BF16)
        for q in range(TB // Q):
            rows = slice(q * Q, (q + 1) * Q)
            t0 = blk * TB + q * Q
            chunk = blk * (TB // Q) + q
            dt, ld, run, bef = step_parts(step_ref[:, rows], bias_ref[...], dlog_ref[...])
            ef, er, _, _ = state_factors(dt, run, bef, t0, b)
            maps_t = act_ref[rows, inner:].astype(F32).T.astype(BF16)
            dy = dy_ref[rows, :]
            df = nn(maps_t[64:128], (dy * widen(ef, spread2)).astype(BF16))
            dr = nn(maps_t[192:256], (dy * widen(er, spread2)).astype(BF16))
            dhy_ref[q, 0:64, :] = df
            dhy_ref[q, 64:128, :] = dr
            pf, pr = pexp_ref[chunk, 0:1, :], pexp_ref[chunk, 1:2, :]
            gsum_f[...] = gsum_f[...] + prod[0:1, :] * df
            gsum_r[...] = pr * gsum_r[...] + dr
            prod[0:1, :] = prod[0:1, :] * pf
            prod[1:2, :] = prod[1:2, :] * pr

    @pl.when(turn == 3 * nblk - 1)
    def _():
        before = meta_ref[2].astype(F32)
        after = meta_ref[3].astype(F32)
        put_message(gmsgf_ref, gsum_f[...] * before, prod[0:1, :] * before)
        put_message(gmsgr_ref, gsum_r[...] * after, prod[1:2, :] * after)
        ggw_ref[...] = nn(normt_ref[...], ggate_ref[...]).astype(BF16)
        gow_ref[...] = tn(ngt[...], cot_ref[...]).astype(BF16)


def back_kernel(reach, meta_ref, act_ref, step_ref, bias_ref, dlog_ref, dy_ref, skip_ref, state_ref, dhy_ref, pexp_ref,
                msgf_ref, msgr_ref, joined_ref, jprev_ref, jhalo_ref, tapv_ref, taps_ref,
                gv_ref, gs_ref, gstep_ref, lent_ref, convg_ref, heads_ref,
                dstate, ext, jext, rowbuf, dact,
                from_low, from_high, up_send, up_recv, down_send, down_recv):
    turn = pl.program_id(0)
    nblk = pl.num_programs(0) // 2
    blk = nblk - 1 - lax.rem(turn, nblk)
    inner = tapv_ref.shape[1]
    both = act_ref.shape[1]
    nchunk = state_ref.shape[0]
    b = meta_ref[0]
    off0 = meta_ref[1]
    swap = Swap(reach, msgr_ref, msgf_ref, from_low, from_high, up_send, up_recv, down_send, down_recv)

    @pl.when(turn == 0)
    def _():
        barrier = pltpu.get_barrier_semaphore()
        pl.semaphore_wait(barrier, swap.greet(barrier))
        swap.start()
        ext[TB : TB + 8, :] = jnp.zeros((8, both), F32)
        convg_ref[...] = jnp.zeros_like(convg_ref)
        heads_ref[...] = jnp.zeros_like(heads_ref)
        rowbuf[...] = jnp.zeros_like(rowbuf)

    spread = spread_matrix(inner, 64)
    spread_low = spread.astype(BF16)
    spread2 = jnp.concatenate([spread_low, spread_low], axis=0)
    i0, i1 = iota((Q, Q), 0), iota((Q, Q), 1)
    after, before = (i0 > i1), (i0 < i1)

    @pl.when(turn < nblk)
    def _():
        skip = widen_col(skip_ref[...], spread)
        diag = i0 == i1
        sums_low = jnp.concatenate([after, before], axis=1).astype(BF16)
        for q in range(TB // Q):
            rows = slice(q * Q, (q + 1) * Q)
            t0 = blk * TB + q * Q
            chunk = blk * (TB // Q) + q
            dest = pl.ds(pl.multiple_of(blk * TB + q * Q, Q), Q)
            dt, ld, run, bef = step_parts(step_ref[:, rows], bias_ref[...], dlog_ref[...])
            ldt = jnp.log(jnp.maximum(dt, 1e-37))
            cols = jnp.concatenate([ldt[:HP] - run[:HP], ldt[HP:] + bef[HP:]], axis=0).T
            rowf, rowr = bef[:HP], -run[HP:]
            maps = act_ref[rows, inner:]
            entf, readf, entr, readr = maps[:, 0:64], maps[:, 64:128], maps[:, 128:192], maps[:, 192:256]
            same = (i0 + t0 < b) == (i1 + t0 < b)
            okf, okr = before & same, after & same
            scores = jnp.where(okf, nt(entf, readf), jnp.where(okr, nt(entr, readr), 0.0))
            dscore = jnp.zeros((Q, Q), F32)
            for j in range(inner // 128):
                lanes = slice(j * 128, (j + 1) * 128)
                vp = act_ref[rows, lanes]
                dyp32 = dy_ref[rows, lanes]
                dyp = dyp32.astype(BF16)
                dw = nt(halves(vp), dyp)
                weights = []
                for i, h in enumerate((2 * j, 2 * j + 1)):
                    e = jnp.where(before, cols[:, h : h + 1] + rowf[h : h + 1],
                                  cols[:, HP + h : HP + h + 1] + rowr[h : h + 1])
                    x = jnp.exp(jnp.minimum(e, 60.0))
                    weights.append((x * scores).astype(BF16))
                    dwx = dw[i * Q : (i + 1) * Q] * x
                    dscore = dscore + dwx
                    sums = nn((dwx * scores).astype(BF16), sums_low)
                    pf, pr = sums[:, :Q], sums[:, Q:]
                    for place, part in enumerate((jnp.where(before, pf, 0.0), jnp.where(after, pr, 0.0),
                                                  jnp.where(diag, pf, 0.0), jnp.where(diag, pr, 0.0))):
                        rowbuf[chunk, place * HP + h : place * HP + h + 1, :] = jnp.sum(part, axis=0, keepdims=True)
                dv = nn(jnp.concatenate(weights, axis=1), halves(dyp))
                dact[dest, lanes] = dv + dyp32 * skip[:, lanes]
            dsf = jnp.where(okf, dscore, 0.0)
            dsr = jnp.where(okr, dscore, 0.0)
            dsf_low, dsr_low = dsf.astype(BF16), dsr.astype(BF16)
            dact[dest, inner:] = jnp.concatenate(
                [nn(dsf_low, readf), nn(dsf.T.astype(BF16), entf), nn(dsr_low, readr), nn(dsr.T.astype(BF16), entr)],
                axis=1)

    @pl.when(turn == nblk)
    def _():
        swap.finish()
        df = chain(from_high)
        dr = chain(from_low)
        for c in range(nchunk):
            d = nchunk - 1 - c
            dstate[d, 0:64, :] = df.astype(BF16)
            df = pexp_ref[d, 0:1, :] * df + dhy_ref[d, 0:64, :]
            dstate[c, 64:128, :] = dr.astype(BF16)
            dr = pexp_ref[c, 1:2, :] * dr + dhy_ref[c, 64:128, :]

    @pl.when(turn > nblk)
    def _():
        ext[TB : TB + 8, :] = ext[0:8, :]

    @pl.when(turn >= nblk)
    def _():
        after32, before32 = after.astype(F32), before.astype(F32)
        for q in range(TB // Q):
            rows = slice(q * Q, (q + 1) * Q)
            t0 = blk * TB + q * Q
            chunk = blk * (TB // Q) + q
            dest = pl.ds(pl.multiple_of(blk * TB + q * Q, Q), Q)
            dt, ld, run, bef = step_parts(step_ref[:, rows], bias_ref[...], dlog_ref[...])
            ef, er, tf, tr = state_factors(dt, run, bef, t0, b)
            maps = act_ref[rows, inner:]
            entf, readf, entr, readr = maps[:, 0:64], maps[:, 64:128], maps[:, 128:192], maps[:, 192:256]
            state = state_ref[chunk]
            grad_state = dstate[chunk]
            efe, ere = widen(ef, spread2), widen(er, spread2)
            tfe, tre = widen(tf, spread2), widen(tr, spread2)
            dy = dy_ref[rows, :]
            values = act_ref[rows, :inner].astype(F32)
            dyf, dyr = dy * efe, dy * ere
            dreadf = nt(dyf.astype(BF16), state[0:64])
            dreadr = nt(dyr.astype(BF16), state[64:128])
            qf = nt(spread_low, (nn(readf, state[0:64]) * dyf).astype(BF16))
            qr = nt(spread_low, (nn(readr, state[64:128]) * dyr).astype(BF16))
            dvf = nn(entf, grad_state[0:64]) * tfe
            dvr = nn(entr, grad_state[64:128]) * tre
            wf = nt(spread_low, (values * dvf).astype(BF16))
            wr = nt(spread_low, (values * dvr).astype(BF16))
            dentf = nt((values * tfe).astype(BF16), grad_state[0:64])
            dentr = nt((values * tre).astype(BF16), grad_state[64:128])
            through = state.astype(F32) * grad_state.astype(F32)
            zf = jnp.sum(through[0:64], axis=0, keepdims=True) * pexp_ref[chunk, 0:1, :]
            zr = jnp.sum(through[64:128], axis=0, keepdims=True) * pexp_ref[chunk, 1:2, :]
            zf = nt(spread, jnp.broadcast_to(zf, (8, inner)), HIGHEST)[:, 0:1]
            zr = nt(spread, jnp.broadcast_to(zr, (8, inner)), HIGHEST)[:, 0:1]
            dact[dest, :inner] = dact[dest, :inner] + dvf + dvr
            dact[dest, inner:] = dact[dest, inner:] + jnp.concatenate([dentf, dreadf, dentr, dreadr], axis=1)
            late = nn(jnp.concatenate([qf, wr], axis=0), after32, HIGHEST)
            early = nn(jnp.concatenate([wf, qr], axis=0), before32, HIGHEST)
            rowsum = rowbuf[chunk]
            dld = jnp.concatenate(
                [rowsum[0:HP] + late[:HP] + early[:HP] + zf, rowsum[HP : 2 * HP] + late[HP:] + early[HP:] + zr], axis=0)
            dldt = rowsum[2 * HP : 4 * HP] + jnp.concatenate([wf, wr], axis=0)
            sig = jax.nn.sigmoid(step_ref[:, rows] + bias_ref[...])
            ratio = jnp.where(dt < 1e-30, 1.0, sig / jnp.maximum(dt, 1e-30))
            graw = dldt * ratio - jnp.exp(dlog_ref[...]) * sig * dld
            gstep_ref[:, rows] = graw.astype(BF16)
            heads_ref[:, 0:1] += jnp.sum(graw, axis=1, keepdims=True)
            heads_ref[:, 1:2] += jnp.sum(dld * ld, axis=1, keepdims=True)

        prev = jnp.where(blk == 0, jhalo_ref[...], jprev_ref[...])
        jext[0:16, :] = prev.astype(F32)
        jext[16 : 16 + TB, :] = joined_ref[...].astype(F32)
        tok = iota((TB, 1), 0) + blk * TB
        masks = [conv_mask(tok, m, b, off0) for m in range(4)]
        later_masks = [conv_mask(tok + m, m, b, off0) for m in range(4)]
        for j in range(both // 128):
            cols = slice(j * 128, (j + 1) * 128)
            tap = tapv_ref[:, cols] if j * 128 < inner else taps_ref[:, j * 128 - inner : (j + 1) * 128 - inner]
            shifted = [jext[16 : 16 + TB, cols]]
            total = shifted[0] * tap[3:4]
            for m in range(1, 4):
                shifted.append(jext[16 - m : 16 - m + TB, cols] * masks[m])
                total = total + shifted[m] * tap[3 - m : 4 - m]
            sig = jax.nn.sigmoid(total)
            dconv = dact[pl.ds(pl.multiple_of(blk * TB, TB), TB), cols] * (sig * (1.0 + total * (1.0 - sig)))
            ext[0:TB, cols] = dconv
            for m in range(4):
                convg_ref[3 - m : 4 - m, cols] += jnp.sum(dconv * shifted[m], axis=0, keepdims=True)
            grad = dconv * tap[3:4]
            for m in range(1, 4):
                grad = grad + ext[m : m + TB, cols] * later_masks[m] * tap[3 - m : 4 - m]
            if j * 128 < inner:
                gv_ref[:, cols] = grad
            else:
                gs_ref[:, j * 128 - inner : (j + 1) * 128 - inner] = grad

    @pl.when(turn == 2 * nblk - 1)
    def _():
        first = jnp.concatenate([jnp.zeros((8, both), F32), ext[0:8, :]], axis=0)
        tap = jnp.concatenate([tapv_ref[...], taps_ref[...]], axis=1)
        edge_masks = [conv_mask(iota((8, 1), 0) - 8 + m, m, b, off0) for m in range(4)]
        lent = jnp.zeros((8, both), F32)
        for m in range(1, 4):
            lent = lent + first[m : m + 8] * edge_masks[m] * tap[3 - m : 4 - m]
        lent_ref[...] = lent


def down_kernel(gv_ref, gs_ref, next_ref, gstep_ref, ggate_ref, normt_ref, wg_ref, wv_ref, wstep_ref,
                gn_ref, gso_ref, gvw_ref, gstepw_ref,
                gvl):
    blk = pl.program_id(0)
    nblk = pl.num_programs(0)
    inner = wg_ref.shape[1]
    last = (blk == nblk - 1).astype(F32)
    gvl[pl.ds(blk * TB, TB), :] = gv_ref[...].astype(BF16)

    tail = gv_ref[TB - 16 : TB, :] + jnp.concatenate(
        [jnp.zeros((8, inner), F32), next_ref[:, :inner] * last], axis=0)
    gvl[pl.ds(blk * TB + TB - 16, 16), :] = tail.astype(BF16)
    gso_ref[...] = gs_ref[...].astype(BF16)
    tail = gs_ref[TB - 16 : TB, :] + jnp.concatenate(
        [jnp.zeros((8, gs_ref.shape[1]), F32), next_ref[:, inner:] * last], axis=0)
    gso_ref[TB - 16 : TB, :] = tail.astype(BF16)
    gn = nt(ggate_ref[...], wg_ref[...]) + nt(gvl[pl.ds(blk * TB, TB), :], wv_ref[...])
    gn = gn + tn(gstep_ref[:, pl.ds(blk * TB, TB)], wstep_ref[...])
    gn_ref[...] = gn.astype(BF16)

    @pl.when(blk == nblk - 1)
    def _():
        gvw_ref[...] = nn(normt_ref[...], gvl[...]).astype(BF16)
        gstepw_ref[...] = nt(gstep_ref[...], normt_ref[...]).astype(BF16)


def end_kernel(mine_ref, other_ref, smine_ref, sother_ref, hid_ref, cot_ref, gain_ref, ws_ref, normt_ref,
               omine_ref, oother_ref, small_ref, hsum_ref, cmine_ref, cother_ref,
               gh_ref, tiny_ref, gsw_ref, out_ref,
               gsl):
    blk = pl.program_id(0)
    nblk = pl.num_programs(0)
    width = hid_ref.shape[1]
    inner_dev = small_ref.shape[1]

    @pl.when(blk == 0)
    def _():
        tiny_ref[...] = jnp.zeros_like(tiny_ref)
        tiny_ref[0:2, :inner_dev] = small_ref[0:2, :]
        tiny_ref[4:6, 0 : 2 * HP] = hsum_ref[...].T[0:2]
        tiny_ref[8:16, :inner_dev] = cmine_ref[:, :inner_dev]
        tiny_ref[8:16, inner_dev:] = cmine_ref[:, inner_dev:] + cother_ref[:, inner_dev:]

    grad_state = (smine_ref[...].astype(F32) + sother_ref[...].astype(F32)).astype(BF16)
    gsl[pl.ds(blk * TB, TB), :] = grad_state
    gn = mine_ref[...].astype(F32) + other_ref[...].astype(F32) + nt(grad_state, ws_ref[...])
    x = hid_ref[...].astype(F32)
    scale = lax.rsqrt(jnp.mean(x * x, axis=1, keepdims=True) + EPSILON)
    tiny_ref[2:3, :width] += jnp.sum(gn * x * scale, axis=0, keepdims=True)
    v = gn * gain_ref[...]
    inner = jnp.mean(x * v, axis=1, keepdims=True)
    gh_ref[...] = cot_ref[...].astype(F32) + scale * v - x * (scale * scale * scale * inner)
    out_ref[...] = (x + (omine_ref[...].astype(F32) + oother_ref[...].astype(F32))).astype(BF16)

    @pl.when(blk == nblk - 1)
    def _():
        gsw_ref[...] = nn(normt_ref[...], gsl[...]).astype(BF16)


def whole_spec(array):
    zeros = (0,) * array.ndim
    return pl.BlockSpec(array.shape, lambda i: zeros)


def rows_spec(array, rows=TB, flip=0):
    rest = (0,) * (array.ndim - 1)
    if flip:
        return pl.BlockSpec((rows,) + array.shape[1:], lambda i: (flip - 1 - i,) + rest)
    return pl.BlockSpec((rows,) + array.shape[1:], lambda i: (i,) + rest)


def cols_spec(array, flip=0):
    if flip:
        return pl.BlockSpec((array.shape[0], TB), lambda i: (0, flip - 1 - i))
    return pl.BlockSpec((array.shape[0], TB), lambda i: (0, i))


SMEM_SPEC = pl.BlockSpec(memory_space=pltpu.SMEM)


def call(kernel, grid, ins, outs, scratch, vmem, flops, ident=None):
    arrays = [a for a, _ in ins]
    return pl.pallas_call(
        kernel,
        grid=(grid,),
        in_specs=[s for _, s in ins],
        out_specs=[s for _, s in outs],
        out_shape=[jax.ShapeDtypeStruct(a.shape, a.dtype) for a, _ in outs],
        scratch_shapes=scratch,
        compiler_params=pltpu.CompilerParams(
            dimension_semantics=("arbitrary",), vmem_limit_bytes=vmem * MIB, collective_id=ident,
            has_side_effects=ident is not None),
        cost_estimate=pl.CostEstimate(
            flops=int(flops), transcendentals=0,
            bytes_accessed=sum(a.size * a.dtype.itemsize for a in arrays)
            + sum(a.size * a.dtype.itemsize for a, _ in outs)),
    )(*arrays)


def padded(x, axis):
    pads = [(0, 0)] * x.ndim
    pads[axis] = (0, HP - x.shape[axis])
    return jnp.pad(x, pads)


def shape(dims, dtype):
    return jax.ShapeDtypeStruct(dims, dtype)


def body(
    hidden_in, norm_gain, gate_proj, value_proj, state_proj, step_proj, conv_value, conv_state,
    step_bias, decay_log, skip_scale, gate_gain, out_proj, lengths, cotangent,
):
    length, width = hidden_in.shape
    inner = gate_proj.shape[1]
    heads = decay_log.shape[0]
    maps = state_proj.shape[1]
    both = inner + maps
    nblk = length // TB
    nchunk = length // Q
    count = lax.axis_size("seq")
    reach = min(1 + (LEN_MOST - 2) // length, count - 1)
    mib = MIB

    halo = lax.ppermute(hidden_in[length - 16 :], "seq", [(i, i + 1) for i in range(count - 1)])
    wstep = padded(step_proj.transpose(0, 2, 1), 1).reshape(2 * HP, width)
    bias = padded(step_bias, 1).reshape(2 * HP, 1)
    dlog = padded(decay_log, 0)
    dlog = jnp.concatenate([dlog, dlog]).reshape(2 * HP, 1)
    skip = padded(skip_scale, 0).reshape(HP, 1)
    gain_in = norm_gain.reshape(1, width)
    gain_gate = gate_gain.reshape(1, inner)

    normt = shape((width, length), BF16)
    gate = shape((length, inner), F32)
    joined = shape((length, both), BF16)
    jhalo = shape((16, both), BF16)
    act = shape((length, both), BF16)
    step = shape((2 * HP, length), F32)
    inc = shape((nchunk, 128, inner), F32)
    pexp = shape((nchunk, 2, inner), F32)
    msg = shape((80, inner), BF16)
    meta = shape((8,), jnp.int32)
    cq = TB // Q
    meta, normt, gate, joined, jhalo, act, step, inc, pexp, msgf, msgr = call(
        front_kernel, nblk,
        [(lengths, SMEM_SPEC), (hidden_in, rows_spec(hidden_in)), (halo, whole_spec(halo)),
         (gain_in, whole_spec(gain_in)), (gate_proj, whole_spec(gate_proj)), (value_proj, whole_spec(value_proj)),
         (state_proj, whole_spec(state_proj)), (wstep, whole_spec(wstep)), (conv_value, whole_spec(conv_value)),
         (conv_state, whole_spec(conv_state)), (bias, whole_spec(bias)), (dlog, whole_spec(dlog))],
        [(meta, SMEM_SPEC), (normt, cols_spec(normt)), (gate, rows_spec(gate)), (joined, rows_spec(joined)),
         (jhalo, whole_spec(jhalo)), (act, rows_spec(act)), (step, cols_spec(step)), (inc, rows_spec(inc, cq)),
         (pexp, rows_spec(pexp, cq)), (msg, whole_spec(msg)), (msg, whole_spec(msg))],
        [pltpu.VMEM((TB + 8, both), F32), pltpu.VMEM((64, inner), F32), pltpu.VMEM((64, inner), F32),
         pltpu.VMEM((8, inner), F32)],
        48, 2 * length * width * (2 * inner + maps))

    def turned(array):
        rest = (0,) * (array.ndim - 1)
        return pl.BlockSpec((TB,) + array.shape[1:], lambda i: (lax.rem(i, nblk),) + rest)

    def turned_cols(array):
        return pl.BlockSpec((array.shape[0], TB), lambda i: (0, lax.rem(i, nblk)))

    def final(array, rows=TB):
        rest = (0,) * (array.ndim - 1)
        return pl.BlockSpec((rows,) + array.shape[1:], lambda i: (jnp.maximum(i - 2 * nblk, 0),) + rest)

    state = shape((nchunk, 128, inner), BF16)
    out_part = shape((length, width), BF16)
    ggate = shape((length, inner), BF16)
    dy = shape((length, inner), F32)
    dhy = shape((nchunk, 128, inner), F32)
    small = shape((8, inner), F32)
    ggw = shape((width, inner), BF16)
    gow = shape((inner, width), BF16)
    state, out_part, ggate, dy, dhy, gmsgf, gmsgr, small, ggw, gow = call(
        partial(mix_kernel, reach), 3 * nblk,
        [(meta, SMEM_SPEC), (act, turned(act)), (step, turned_cols(step)), (bias, whole_spec(bias)),
         (dlog, whole_spec(dlog)), (gate, turned(gate)), (cotangent, whole_spec(cotangent)),
         (out_proj, whole_spec(out_proj)), (gain_gate, whole_spec(gain_gate)), (skip, whole_spec(skip)),
         (inc, whole_spec(inc)), (pexp, whole_spec(pexp)), (msgf, whole_spec(msgf)), (msgr, whole_spec(msgr)),
         (normt, whole_spec(normt))],
        [(state, whole_spec(state)), (out_part, final(out_part)), (ggate, whole_spec(ggate)), (dy, final(dy)),
         (dhy, final(dhy, cq)), (msg, whole_spec(msg)), (msg, whole_spec(msg)), (small, whole_spec(small)),
         (ggw, whole_spec(ggw)), (gow, whole_spec(gow))],
        [pltpu.VMEM((length, inner), F32), pltpu.VMEM((length, inner), BF16), pltpu.VMEM((nblk, 8, TB), F32),
         pltpu.VMEM((nblk, 8, TB), F32), pltpu.VMEM((64, inner), F32), pltpu.VMEM((64, inner), F32),
         pltpu.VMEM((8, inner), F32), pltpu.SemaphoreType.DMA((nblk,)), pltpu.SemaphoreType.DMA((nblk,))]
        + swap_scratch(reach, inner),
        56, 2 * length * width * inner * 6, 1)

    gv = shape((length, inner), F32)
    gs = shape((length, maps), F32)
    gstep = shape((2 * HP, length), BF16)
    lent = shape((8, both), F32)
    convg = shape((8, both), F32)
    hsum = shape((2 * HP, 128), F32)

    def flipped(array):
        rest = (0,) * (array.ndim - 1)
        return pl.BlockSpec((TB,) + array.shape[1:], lambda i: (nblk - 1 - lax.rem(i, nblk),) + rest)

    def flipped_late(array):
        rest = (0,) * (array.ndim - 1)
        return pl.BlockSpec((TB,) + array.shape[1:], lambda i: (jnp.minimum(2 * nblk - 1 - i, nblk - 1),) + rest)

    step_spec = pl.BlockSpec((2 * HP, TB), lambda i: (0, nblk - 1 - lax.rem(i, nblk)))
    gstep_spec = pl.BlockSpec((2 * HP, TB), lambda i: (0, jnp.minimum(2 * nblk - 1 - i, nblk - 1)))
    prev_spec = pl.BlockSpec(
        (16, both), lambda i: (jnp.maximum(jnp.minimum(2 * nblk - 1 - i, nblk - 1) * (TB // 16) - 1, 0), 0))
    gv, gs, gstep, lent, convg, hsum = call(
        partial(back_kernel, reach), 2 * nblk,
        [(meta, SMEM_SPEC), (act, flipped(act)), (step, step_spec), (bias, whole_spec(bias)),
         (dlog, whole_spec(dlog)), (dy, flipped(dy)), (skip, whole_spec(skip)),
         (state, whole_spec(state)), (dhy, whole_spec(dhy)), (pexp, whole_spec(pexp)), (gmsgf, whole_spec(gmsgf)),
         (gmsgr, whole_spec(gmsgr)), (joined, flipped_late(joined)), (joined, prev_spec),
         (jhalo, whole_spec(jhalo)), (conv_value, whole_spec(conv_value)), (conv_state, whole_spec(conv_state))],
        [(gv, flipped_late(gv)), (gs, flipped_late(gs)), (gstep, gstep_spec),
         (lent, whole_spec(lent)), (convg, whole_spec(convg)), (hsum, whole_spec(hsum))],
        [pltpu.VMEM((nchunk, 128, inner), BF16), pltpu.VMEM((TB + 8, both), F32), pltpu.VMEM((TB + 16, both), F32),
         pltpu.VMEM((nchunk, 4 * HP, Q), F32), pltpu.VMEM((length, both), F32)] + swap_scratch(reach, inner),
        56, 2 * length * width * inner * 4, 3)
    from_next = lax.ppermute(lent, "seq", [(i + 1, i) for i in range(count - 1)])

    gn = shape((length, width), BF16)
    gso = shape((length, maps), BF16)
    gvw = shape((width, inner), BF16)
    gstepw = shape((2 * HP, width), BF16)
    gn, gso, gvw, gstepw = call(
        down_kernel, nblk,
        [(gv, rows_spec(gv)), (gs, rows_spec(gs)), (from_next, whole_spec(from_next)), (gstep, whole_spec(gstep)),
         (ggate, rows_spec(ggate)), (normt, whole_spec(normt)), (gate_proj, whole_spec(gate_proj)),
         (value_proj, whole_spec(value_proj)), (wstep, whole_spec(wstep))],
        [(gn, rows_spec(gn)), (gso, rows_spec(gso)), (gvw, whole_spec(gvw)), (gstepw, whole_spec(gstepw))],
        [pltpu.VMEM((length, inner), BF16)],
        48, 2 * length * width * inner * 3)
    gn_other, gso_other, out_other, convg_other = core_swap([gn, gso, out_part, convg], 4)

    gh = shape((length, width), F32)
    tiny = shape((16, both), F32)
    gsw = shape((width, maps), BF16)
    out = shape((length, width), BF16)
    gh, tiny, gsw, out = call(
        end_kernel, nblk,
        [(gn, rows_spec(gn)), (gn_other, rows_spec(gn_other)), (gso, rows_spec(gso)),
         (gso_other, rows_spec(gso_other)), (hidden_in, rows_spec(hidden_in)), (cotangent, rows_spec(cotangent)),
         (gain_in, whole_spec(gain_in)), (state_proj, whole_spec(state_proj)), (normt, whole_spec(normt)),
         (out_part, rows_spec(out_part)), (out_other, rows_spec(out_other)), (small, whole_spec(small)),
         (hsum, whole_spec(hsum)), (convg, whole_spec(convg)), (convg_other, whole_spec(convg_other))],
        [(gh, rows_spec(gh)), (tiny, whole_spec(tiny)), (gsw, whole_spec(gsw)), (out, rows_spec(out))],
        [pltpu.VMEM((length, maps), BF16)],
        48, 2 * length * width * maps * 2)

    (ggw, gow, gvw, gsw, gstepw), tiny = reduce_all([ggw, gow, gvw, gsw, gstepw], tiny, count, 5)
    gstepw = gstepw.astype(F32).reshape(2, HP, width)[:, :heads].transpose(0, 2, 1)
    hsum = tiny[4:6, : 2 * HP].reshape(2, 2, HP)[:, :, :heads]
    return (
        out,
        gh,
        tiny[2, :width],
        ggw.astype(F32),
        gvw.astype(F32),
        gsw.astype(F32),
        gstepw,
        tiny[8:12, :inner],
        tiny[8:12, inner:],
        hsum[0],
        hsum[1, 0] + hsum[1, 1],
        jnp.sum(tiny[1, :inner].reshape(heads, inner // heads), axis=1),
        tiny[0, :inner],
        gow.astype(F32),
    )


def solution(mesh):
    in_specs = (
        P("seq", None),
        P(),
        P(None, "head"),
        P(None, "head"),
        P(),
        P(None, None, "head"),
        P(None, "head"),
        P(),
        P(None, "head"),
        P("head"),
        P("head"),
        P("head"),
        P("head", None),
        P(),
        P("seq", None),
    )
    out_specs = (
        P("seq", None),
        P("seq", None),
        P(),
        P(None, "head"),
        P(None, "head"),
        P(),
        P(None, None, "head"),
        P(None, "head"),
        P(),
        P(None, "head"),
        P("head"),
        P("head"),
        P("head"),
        P("head", None),
    )
    return jax.shard_map(body, mesh=mesh, in_specs=in_specs, out_specs=out_specs, check_vma=False)
```

```python
from functools import partial

import jax
import jax.numpy as jnp
from jax import lax
from jax.experimental import pallas as pl
from jax.experimental.pallas import tpu as pltpu
from jax.sharding import PartitionSpec as P

EPSILON = 1e-05
LEN_MOST = 4096
Q = 128
TB = 256
HP = 16
MIB = 1024 * 1024
VMEM_LIMIT = 63 * MIB
HIGHEST = lax.Precision.HIGHEST
F32 = jnp.float32
BF16 = jnp.bfloat16
MESH = pl.DeviceIdType.MESH


def nn(a, b, precision=None):
    return jnp.dot(a, b, preferred_element_type=F32, precision=precision)


def nt(a, b, precision=None):
    return lax.dot_general(a, b, (((1,), (1,)), ((), ())), preferred_element_type=F32, precision=precision)


def tn(a, b, precision=None):
    return lax.dot_general(a, b, (((0,), (0,)), ((), ())), preferred_element_type=F32, precision=precision)


def iota(shape, axis):
    return lax.broadcasted_iota(jnp.int32, shape, axis)


def spread_matrix(width, hdim):
    return (iota((HP, width), 1) // hdim == iota((HP, width), 0)).astype(F32)


def split(x):
    hi = x.astype(BF16)
    return hi, (x - hi.astype(F32)).astype(BF16)


def widen(rows, spread2):
    hi, lo = split(rows.T)
    return nn(jnp.concatenate([hi, lo], axis=1), spread2)


def widen_col(col, spread):
    return tn(jnp.broadcast_to(col, (HP, 8)), spread, HIGHEST)[0:1]


def silu(x):
    return x * jax.nn.sigmoid(x)


def softplus(x):
    return jnp.maximum(x, 0.0) + jnp.log1p(jnp.exp(-jnp.abs(x)))


def step_parts(step, bias, dlog):
    dt = softplus(step + bias)
    ld = -jnp.exp(dlog) * dt
    upto = (iota((Q, Q), 0) <= iota((Q, Q), 1)).astype(F32)
    run = nn(ld, upto, HIGHEST)
    return dt, ld, run, run - ld


def state_factors(dt, run, bef, t0, b):
    t1 = t0 + Q
    tok = iota((1, Q), 1) + t0
    ef = jnp.where((tok < b) | (t0 > b), jnp.exp(bef[:HP]), 0.0)
    er = jnp.where((tok >= b) | (t1 < b), jnp.exp(run[HP:, Q - 1 : Q] - run[HP:]), 0.0)
    tf = jnp.where((tok >= b) | (t1 <= b), jnp.exp(run[:HP, Q - 1 : Q] - run[:HP]), 0.0) * dt[:HP]
    tr = jnp.where((tok < b) | (t0 >= b), jnp.exp(bef[HP:]), 0.0) * dt[HP:]
    return ef, er, tf, tr


def conv_mask(tok, shift, b, off0):
    lost = ((tok < b) & (tok + off0 < shift)) | ((tok >= b) & (tok < b + shift))
    return jnp.where(lost, 0.0, 1.0)


def put_message(ref, state, passed):
    hi, lo = split(passed)
    ref[0:64, :] = state.astype(BF16)
    row = iota((16, state.shape[1]), 0)
    tail = jnp.where(row == 0, hi.astype(F32), jnp.where(row == 1, lo.astype(F32), 0.0))
    ref[64:80, :] = tail.astype(BF16)


def chain(ref):
    total = ref[0, 0:64, :].astype(F32)
    passed = None
    for k in range(1, ref.shape[0]):
        tail = ref[k - 1, 64:80, :].astype(F32)
        here = tail[0:1] + tail[1:2]
        passed = here if passed is None else passed * here
        total = total + passed * ref[k, 0:64, :].astype(F32)
    return total


class Swap:
    def __init__(self, reach, up_ref, down_ref, from_low, from_high, up_send, up_recv, down_send, down_recv):
        self.me, self.core, self.count = lax.axis_index("seq"), lax.axis_index("head"), lax.axis_size("seq")
        self.reach, self.up_ref, self.down_ref, self.from_low, self.from_high = reach, up_ref, down_ref, from_low, from_high
        self.sems = up_send, up_recv, down_send, down_recv

    def up(self, k):
        return pltpu.make_async_remote_copy(
            src_ref=self.up_ref, dst_ref=self.from_low.at[k - 1], send_sem=self.sems[0].at[k - 1],
            recv_sem=self.sems[1].at[k - 1], device_id=(self.me + k, self.core), device_id_type=MESH)

    def down(self, k):
        return pltpu.make_async_remote_copy(
            src_ref=self.down_ref, dst_ref=self.from_high.at[k - 1], send_sem=self.sems[2].at[k - 1],
            recv_sem=self.sems[3].at[k - 1], device_id=(self.me - k, self.core), device_id_type=MESH)

    def greet(self, barrier):
        me, core, count = self.me, self.core, self.count
        for k in range(1, self.reach + 1):
            @pl.when(me + k < count)
            def _():
                pl.semaphore_signal(barrier, inc=1, device_id=(me + k, core), device_id_type=MESH)

            @pl.when(me >= k)
            def _():
                pl.semaphore_signal(barrier, inc=1, device_id=(me - k, core), device_id_type=MESH)
        return jnp.minimum(me, self.reach) + jnp.minimum(count - 1 - me, self.reach)

    def start(self):
        me, count = self.me, self.count
        for k in range(1, self.reach + 1):
            @pl.when(me + k < count)
            def _():
                self.up(k).start()

            @pl.when(me >= k)
            def _():
                self.down(k).start()

            @pl.when(me < k)
            def _():
                self.from_low[k - 1] = jnp.zeros_like(self.from_low[k - 1])

            @pl.when(me + k >= count)
            def _():
                self.from_high[k - 1] = jnp.zeros_like(self.from_high[k - 1])

    def finish(self):
        me, count = self.me, self.count
        for k in range(1, self.reach + 1):
            @pl.when(me + k < count)
            def _():
                self.up(k).wait_send()
                self.down(k).wait_recv()

            @pl.when(me >= k)
            def _():
                self.down(k).wait_send()
                self.up(k).wait_recv()


def chunk_scores(maps, t0, b):
    tr, tc = iota((Q, Q), 0), iota((Q, Q), 1)
    same = (tr + t0 < b) == (tc + t0 < b)
    fwd = nt(maps[:, 64:128], maps[:, 0:64])
    rev = nt(maps[:, 192:256], maps[:, 128:192])
    return jnp.where((tr > tc) & same, fwd, jnp.where((tr < tc) & same, rev, 0.0))


def halves(x):
    left = iota(x.shape, 1) < 64
    zero = jnp.zeros_like(x)
    return jnp.concatenate([jnp.where(left, x, zero), jnp.where(left, zero, x)], axis=0)


class Reduce:
    def __init__(self, bits, pieces, rs_send, rs_recv, ag_send, ag_recv):
        me, core = lax.axis_index("seq"), lax.axis_index("head")
        bit = [lax.rem(me // (1 << k), 2) for k in range(bits)]
        mate = [me + (1 - 2 * bit[k]) * (1 << k) for k in range(bits)]
        self.mates = list(mate)
        self.bits, self.bit, self.mate, self.core, self.pieces = bits, bit, mate, core, pieces
        self.sems = rs_send, rs_recv, ag_send, ag_recv
        self.pos = [0] * len(pieces)
        self.steps = []
        for piece in pieces:
            halvings = halvings_of(piece["work"].shape[0], bits)
            self.steps.append([("rs", s) for s in range(bits)] + [("ag", s) for s in reversed(range(halvings))])

    def geometry(self, p, s):
        rows = self.pieces[p]["work"].shape[0]
        halvings = halvings_of(rows, self.bits)
        off, slot = jnp.int32(0), 0
        for t in range(s):
            if t < halvings:
                rows = rows // 2
                off = off + self.bit[self.pieces[p]["order"][t]] * rows
            slot += rows
        return off, rows, slot, s < halvings

    def remote(self, src, dst, send, recv, k):
        return pltpu.make_async_remote_copy(
            src_ref=src, dst_ref=dst, send_sem=send, recv_sem=recv, device_id=(self.mate[k], self.core),
            device_id_type=MESH)

    def first(self, p):
        return self.bit[self.pieces[p]["order"][0]] * (self.pieces[p]["work"].shape[0] // 2)

    def copy(self, p, step):
        kind, s = step
        piece = self.pieces[p]
        k = piece["order"][s]
        if kind == "rs":
            off, rows, slot, halved = self.geometry(p, s)
            source, off = (piece["work"], off) if s == 0 else (piece["kept"], off - self.first(p))
            if halved:
                rows = rows // 2
                off = off + (1 - self.bit[k]) * rows
            return self.remote(
                source.at[pl.ds(pl.multiple_of(off, 16), rows)], piece["recv"].at[pl.ds(slot, rows)],
                self.sems[0].at[p, s], self.sems[1].at[p, s], k)
        off, rows, _, _ = self.geometry(p, s + 1)
        where = piece["out"].at[pl.ds(pl.multiple_of(off, 16), rows)]
        return self.remote(where, where, self.sems[2].at[p, s], self.sems[3].at[p, s], k)

    def arriving(self, p, s):
        off, rows, _, _ = self.geometry(p, s + 1)
        k = self.pieces[p]["order"][s]
        off = off + (1 - 2 * self.bit[k]) * rows
        where = self.pieces[p]["out"].at[pl.ds(pl.multiple_of(off, 16), rows)]
        return self.remote(where, where, self.sems[2].at[p, s], self.sems[3].at[p, s], k)

    def start(self, p):
        self.copy(p, self.steps[p][0]).start()

    def step(self, p, at):
        kind, s = self.steps[p][at]
        if kind == "rs":
            self.add(p, s, self.copy(p, (kind, s)))
        else:
            self.arriving(p, s).wait_recv()
        if at + 1 < len(self.steps[p]):
            self.copy(p, self.steps[p][at + 1]).start()

    def plan(self, p):
        at = self.pos[p]
        if at >= len(self.steps[p]):
            return []
        self.pos[p] = at + 1
        return [(p, at)]

    def advance(self, p):
        for q, at in self.plan(p):
            self.step(q, at)

    def plans(self, wanted):
        return {turn: [step for p in wanted[turn] for step in self.plan(p)] for turn in sorted(wanted)}

    def hook(self, turn, plans):
        for k, steps in plans.items():
            @pl.when(turn == k)
            def _():
                for p, at in steps:
                    self.step(p, at)

    def add(self, p, s, copy):
        piece = self.pieces[p]
        off, rows, slot, halved = self.geometry(p, s)
        if halved:
            copy.wait_recv()
            rows = rows // 2
            off = off + self.bit[piece["order"][s]] * rows
        else:
            copy.wait()
        recv, rel = piece["recv"], off - self.first(p)
        source, at = (piece["work"], off) if s == 0 else (piece["kept"], rel)
        dest, to = (piece["out"], off) if s == self.bits - 1 else (piece["kept"], rel)
        size = 48 if rows % 48 == 0 else 16

        def one(i, _):
            total = source[pl.ds(pl.multiple_of(at + i * size, 16), size), :].astype(F32)
            total = total + recv[pl.ds(pl.multiple_of(slot + i * size, 16), size), :].astype(F32)
            dest[pl.ds(pl.multiple_of(to + i * size, 16), size), :] = total.astype(BF16)
            return 0

        lax.fori_loop(0, rows // size, one, 0)

    def finish(self, p):
        for kind, s in self.steps[p]:
            if kind == "ag" or self.geometry(p, s)[3]:
                self.copy(p, (kind, s)).wait_send()


def halvings_of(rows, bits):
    made = 0
    while made < bits and (rows >> made) % 32 == 0:
        made += 1
    return made


def received_rows(rows, bits):
    halvings, total = halvings_of(rows, bits), 0
    for s in range(bits):
        rows = rows // 2 if s < halvings else rows
        total += rows
    return total


def part(i, size):
    return pl.ds(pl.multiple_of(i * size, size), size)


def at_turns(*groups):
    found = {}
    for turns, pieces in groups:
        for turn in turns:
            found.setdefault(turn, []).extend(pieces)
    return found


class Refs:
    pass


NAMES_IN = ("lengths", "hid_any", "wg_any", "wv_any", "ws_any", "wo_any", "cot_any",
            "gain", "wstep", "tapv", "taps", "bias", "dlog", "skip", "ggain")
NAMES_OUT = ("block_out", "grad_hidden", "ggw_any", "gow_any", "gvw_any", "gsw_any", "tiny_any")


def layer_kernel(reach, bits, names, *refs):
    r = Refs()
    for name, ref in zip(names, refs):
        setattr(r, name, ref)
    length, width = r.hid.shape
    inner = r.wo.shape[0]
    maps = r.ws.shape[1]
    both = inner + maps
    heads = r.dlog.shape[0]
    nblk, nchunk, per = length // TB, length // Q, TB // Q
    me, core, count = lax.axis_index("seq"), lax.axis_index("head"), lax.axis_size("seq")
    base = me * length

    loads = [pltpu.make_async_copy(src, dst, r.load.at[i]) for i, (src, dst) in enumerate(
        ((r.hid_any, r.hid), (r.wv_any, r.wv), (r.ws_any, r.ws), (r.wg_any, r.wg), (r.wo_any, r.wo),
         (r.cot_any, r.cot)))]
    for load in loads:
        load.start()

    swap1 = Swap(reach, r.msgs.at[0], r.msgs.at[1], r.low1, r.high1, r.up_s.at[0], r.up_r.at[0], r.dn_s.at[0], r.dn_r.at[0])
    swap2 = Swap(reach, r.msgs.at[2], r.msgs.at[3], r.low2, r.high2, r.up_s.at[1], r.up_r.at[1], r.dn_s.at[1], r.dn_r.at[1])
    plain = list(range(bits))
    turned = plain[1:2] + plain[:1] + plain[2:]
    groups = inner // 256
    first_state = 2 + groups
    sums = ["ggw", "gow"] + [f"gv{g}" for g in range(groups)] + ["gsw"]
    pieces = [
        dict(work=getattr(r, name + "_w"), kept=getattr(r, name + "_k"), recv=getattr(r, name + "_r"),
             out=getattr(r, name + "_o"), order=turned if i % 2 else plain)
        for i, name in enumerate(sums)
    ]
    red = Reduce(bits, pieces, r.rs_s, r.rs_r, r.ag_s, r.ag_r)
    first = [0, 1]
    barrier = pltpu.get_barrier_semaphore()
    near = swap1.greet(barrier)
    for mate in red.mates:
        pl.semaphore_signal(barrier, inc=1, device_id=(mate, core), device_id_type=MESH)
    pl.semaphore_signal(barrier, inc=1, device_id=(me, 1 - core), device_id_type=MESH)

    def over(src, dst, sems, k):
        return pltpu.make_async_remote_copy(
            src_ref=src, dst_ref=dst, send_sem=sems.at[0, k], recv_sem=sems.at[1, k], device_id=(me, 1 - core),
            device_id_type=MESH)

    def one_sequence(j, carry):
        start, b, off0, after = carry
        end = start + r.lengths[j]
        b = jnp.where((start > base) & (start < base + length), start - base, b)
        off0 = jnp.where((start <= base) & (base < end), base - start, off0)
        after = jnp.where(end == base + length, 0, after)
        return end, b, off0, after

    _, b, off0, after = lax.fori_loop(
        0, r.lengths.shape[0], one_sequence, (jnp.int32(0), jnp.int32(length + 1), jnp.int32(0), jnp.int32(1)))
    before_f = jnp.where(off0 > 0, 1.0, 0.0)
    after_f = after.astype(F32)

    def lanes128(x):
        return jnp.concatenate([x, jnp.zeros((x.shape[0], 128 - x.shape[1]), F32)], axis=1)

    small_cols = jnp.concatenate(
        [lanes128(r.bias[...]), lanes128(r.dlog[...].reshape(1, heads)), lanes128(r.skip[...].reshape(1, heads)),
         jnp.zeros((4, 128), F32)], axis=0).T
    bias = jnp.concatenate([small_cols[:HP, 0:1], small_cols[:HP, 1:2]], axis=0)
    dlog = jnp.concatenate([small_cols[:HP, 2:3], small_cols[:HP, 2:3]], axis=0)
    spread = spread_matrix(inner, inner // heads)
    spread_low = spread.astype(BF16)
    spread2 = jnp.concatenate([spread_low, spread_low], axis=0)
    skip = widen_col(small_cols[:HP, 3:4], spread)
    gain = r.gain[...].reshape(1, width)
    ggain = r.ggain[...].reshape(1, inner)
    r.wst[...] = jnp.zeros_like(r.wst)
    wstep = r.wstep[...].astype(F32)
    for k in range(2):
        r.wst[k * HP : (k + 1) * HP, :] = jnp.concatenate(
            [wstep[:, k, :], jnp.zeros((HP - heads, width), F32)], axis=0).astype(BF16)

    loads[0].wait()
    loads[1].wait()
    loads[2].wait()

    def normalize(x):
        x = x.astype(F32)
        scale = lax.rsqrt(jnp.mean(x * x, axis=1, keepdims=True) + EPSILON)
        return (x * scale * gain).astype(BF16)

    def project(blk, _):
        rows = part(blk, TB)
        normed = normalize(r.hid[rows, :])
        r.buf[rows, :] = normed
        r.normt[:, rows] = normed.T
        dest = pl.ds(pl.multiple_of(16 + blk * TB, 16), TB)
        r.joined[dest, :inner] = nn(normed, r.wv[...]).astype(BF16)
        r.joined[dest, inner:] = nn(normed, r.ws[...]).astype(BF16)
        r.step[:, rows] = nt(r.wst[...], normed)
        return 0

    lax.fori_loop(0, nblk, project, 0)

    pl.semaphore_wait(barrier, near + bits + 1)

    def halo_copy(to):
        return pltpu.make_async_remote_copy(
            src_ref=r.hid.at[pl.ds(length - 16, 16)], dst_ref=r.halo, send_sem=r.edge.at[0], recv_sem=r.edge.at[1],
            device_id=(to, core), device_id_type=MESH)

    @pl.when(me + 1 < count)
    def _():
        halo_copy(me + 1).start()

    @pl.when(me == 0)
    def _():
        r.halo[...] = jnp.zeros_like(r.halo)

    def conv_rows(blk, cols, c0, masks, width_now):
        r.jx[...] = r.joined[pl.ds(pl.multiple_of(blk * TB, 16), TB + 16), cols].astype(F32)
        shifted = [r.jx[16 : 16 + TB, :]]
        tap = r.tap[:, cols]
        total = shifted[0] * tap[3:4]
        for m in range(1, 4):
            shifted.append(r.jx[16 - m : 16 - m + TB, :] * masks[m])
            total = total + shifted[m] * tap[3 - m : 4 - m]
        return shifted, tap, total

    r.tap[:, :inner] = r.tapv[...]
    r.tap[:, inner:] = r.taps[...]

    def chunk_parts(chunk):
        cols = part(chunk, Q)
        return step_parts(r.step[:, cols], bias, dlog)

    def summarize(blk, _):
        rows = part(blk, TB)
        tok = iota((TB, 1), 0) + blk * TB
        masks = [conv_mask(tok, m, b, off0) for m in range(4)]
        for g in range(both // 256):
            cols = slice(g * 256, (g + 1) * 256)
            _, _, total = conv_rows(blk, cols, g * 256, masks, 256)
            r.act[rows, cols] = silu(total).astype(BF16)
        for q in range(per):
            chunk = blk * per + q
            t0 = chunk * Q
            at = part(chunk, Q)
            dt, ld, run, bef = chunk_parts(chunk)
            _, _, tf, tr = state_factors(dt, run, bef, t0, b)
            values = r.act[at, :inner].astype(F32)
            maps_t = r.act[at, inner:].astype(F32).T.astype(BF16)
            r.inc[chunk, 0:64, :] = nn(maps_t[0:64], (values * widen(tf, spread2)).astype(BF16))
            r.inc[chunk, 64:128, :] = nn(maps_t[128:192], (values * widen(tr, spread2)).astype(BF16))
            gone = jnp.exp(run[:, Q - 1 : Q])
            r.pexp[chunk, 0:1, :] = widen_col(gone[:HP], spread) * jnp.where((t0 <= b) & (b < t0 + Q), 0.0, 1.0)
            r.pexp[chunk, 1:2, :] = widen_col(gone[HP:], spread) * jnp.where((t0 < b) & (b <= t0 + Q), 0.0, 1.0)
        return 0

    lax.fori_loop(1, nblk, summarize, 0)

    @pl.when(me > 0)
    def _():
        halo_copy(me + 1).wait_recv()

    nh = normalize(r.halo[...])
    r.joined[0:16, :inner] = nn(nh, r.wv[...]).astype(BF16)
    r.joined[0:16, inner:] = nn(nh, r.ws[...]).astype(BF16)
    summarize(jnp.int32(0), 0)
    sumf, prodf = r.inc[0, 0:64, :], r.pexp[0, 0:1, :]
    sumr, prodr = r.inc[nchunk - 1, 64:128, :], r.pexp[nchunk - 1, 1:2, :]
    for c in range(1, nchunk):
        d = nchunk - 1 - c
        pf, pr = r.pexp[c, 0:1, :], r.pexp[d, 1:2, :]
        sumf, prodf = pf * sumf + r.inc[c, 0:64, :], prodf * pf
        sumr, prodr = pr * sumr + r.inc[d, 64:128, :], prodr * pr
    put_message(r.msgs.at[0], sumf, prodf * before_f)
    put_message(r.msgs.at[1], sumr, prodr * after_f)
    swap1.start()

    loads[3].wait()
    tri0, tri1 = iota((Q, Q), 0), iota((Q, Q), 1)
    lower, upper = tri0 > tri1, tri0 < tri1

    def within(blk, _):
        rows = part(blk, TB)
        r.gate[rows, :] = nn(r.buf[rows, :], r.wg[...])
        for q in range(per):
            chunk = blk * per + q
            at = part(chunk, Q)
            t0 = chunk * Q
            dt, ld, run, bef = chunk_parts(chunk)
            ldt = jnp.log(jnp.maximum(dt, 1e-37))
            rowf = ldt[:HP] - run[:HP]
            rowr = ldt[HP:] + bef[HP:]
            cols = jnp.concatenate([bef[:HP], -run[HP:]], axis=0).T
            scores = chunk_scores(r.act[at, inner:], t0, b)
            for j in range(inner // 128):
                lanes = slice(j * 128, (j + 1) * 128)
                weights = []
                for h in (2 * j, 2 * j + 1):
                    e = jnp.where(lower, cols[:, h : h + 1] + rowf[h : h + 1],
                                  cols[:, HP + h : HP + h + 1] + rowr[h : h + 1])
                    weights.append((jnp.exp(jnp.minimum(e, 60.0)) * scores).astype(BF16))
                vp = r.act[at, lanes]
                y = nn(jnp.concatenate(weights, axis=1), halves(vp))
                r.mixed[at, lanes] = y + skip[:, lanes] * vp.astype(F32)
        return 0

    lax.fori_loop(0, nblk, within, 0)
    loads[4].wait()
    loads[5].wait()
    swap1.finish()
    hf = chain(r.low1) * before_f
    hr = chain(r.high1) * after_f
    for c in range(nchunk):
        r.state[c, 0:64, :] = hf.astype(BF16)
        hf = r.pexp[c, 0:1, :] * hf + r.inc[c, 0:64, :]
        d = nchunk - 1 - c
        r.state[d, 64:128, :] = hr.astype(BF16)
        hr = r.pexp[d, 1:2, :] * hr + r.inc[d, 64:128, :]

    def enter(blk, _):
        lane = iota((Q, 128), 1)
        u_all = nt(r.cot[part(blk, TB), :], r.wo[...])
        for q in range(per):
            chunk = blk * per + q
            at = part(chunk, Q)
            dt, ld, run, bef = chunk_parts(chunk)
            ef, er, _, _ = state_factors(dt, run, bef, chunk * Q, b)
            maps_here = r.act[at, inner:]
            state = r.state[chunk]
            ys = nn(maps_here[:, 64:128], state[0:64]) * widen(ef, spread2)
            ys = ys + nn(maps_here[:, 192:256], state[64:128]) * widen(er, spread2)
            square = jnp.zeros((Q, 1), F32)
            cross = jnp.zeros((Q, 1), F32)
            for j in range(inner // 128):
                lanes = slice(j * 128, (j + 1) * 128)
                y = r.mixed[at, lanes] + ys[:, lanes]
                r.mixed[at, lanes] = y
                gated = y * silu(r.gate[at, lanes])
                square = square + jnp.sum(gated * gated, axis=1, keepdims=True)
                cross = cross + jnp.sum(
                    gated * (u_all[q * Q : (q + 1) * Q, lanes] * ggain[:, lanes]), axis=1, keepdims=True)
            two = jnp.where(lane == 0, square, jnp.where(lane == 1, cross, 0.0))
            r.mine[blk, :, q * Q : (q + 1) * Q] = two.T[0:8]
        over(r.mine.at[blk], r.other.at[blk], r.sum_sem, blk).start()
        return 0

    lax.fori_loop(0, nblk, enter, 0)
    r.small[...] = jnp.zeros_like(r.small)

    def gating(blk, _):
        rows = part(blk, TB)
        over(r.mine.at[blk], r.other.at[blk], r.sum_sem, blk).wait()
        sums = r.mine[blk] + r.other[blk]
        sums = jnp.concatenate([sums, jnp.zeros((120, TB), F32)], axis=0).T
        scale = lax.rsqrt(sums[:, 0:1] / (2 * inner) + EPSILON)
        back = scale * scale * scale * sums[:, 1:2] / (2 * inner)
        gng = nt(r.cot[rows, :], r.wo[...])
        for j in range(inner // 128):
            lanes = slice(j * 128, (j + 1) * 128)
            mixed = r.mixed[rows, lanes]
            pre = r.gate[rows, lanes]
            sig = jax.nn.sigmoid(pre)
            gated = mixed * (pre * sig)
            ng = gated * scale
            r.buf[rows, lanes] = (ng * ggain[:, lanes]).astype(BF16)
            g = gng[:, lanes]
            r.small[0:1, lanes] += jnp.sum(g * ng, axis=0, keepdims=True)
            grad_gated = scale * (g * ggain[:, lanes]) - gated * back
            dy = grad_gated * (pre * sig)
            r.small[1:2, lanes] += jnp.sum(dy * r.act[rows, lanes].astype(F32), axis=0, keepdims=True)
            r.dy[rows, lanes] = dy
            r.ggate[rows, lanes] = (grad_gated * mixed * (sig * (1.0 + pre * (1.0 - sig)))).astype(BF16)
        r.out_mine[rows, :] = nn(r.buf[rows, :], r.wo[...]).astype(BF16)
        over(r.out_mine.at[rows], r.out_other.at[rows], r.out_sem, blk).start()
        for q in range(per):
            chunk = blk * per + q
            at = part(chunk, Q)
            dt, ld, run, bef = chunk_parts(chunk)
            ef, er, _, _ = state_factors(dt, run, bef, chunk * Q, b)
            maps_t = r.act[at, inner:].astype(F32).T.astype(BF16)
            dy = r.dy[at, :]
            r.inc[chunk, 0:64, :] = nn(maps_t[64:128], (dy * widen(ef, spread2)).astype(BF16))
            r.inc[chunk, 64:128, :] = nn(maps_t[192:256], (dy * widen(er, spread2)).astype(BF16))
        return 0

    lax.fori_loop(0, nblk, gating, 0)
    sumf, sumr = r.inc[nchunk - 1, 0:64, :], r.inc[0, 64:128, :]
    for c in range(1, nchunk):
        d = nchunk - 1 - c
        sumf = r.pexp[d, 0:1, :] * sumf + r.inc[d, 0:64, :]
        sumr = r.pexp[c, 1:2, :] * sumr + r.inc[c, 64:128, :]
    put_message(r.msgs.at[2], sumr * after_f, prodr * after_f)
    put_message(r.msgs.at[3], sumf * before_f, prodf * before_f)
    swap2.start()
    r.ggw_w[...] = nn(r.normt[...], r.ggate[...]).astype(BF16)
    red.start(0)
    r.gow_w[...] = tn(r.buf[...], r.cot[...]).astype(BF16)
    red.start(1)

    sums_low = jnp.concatenate([lower, upper], axis=1).astype(BF16)
    diag = tri0 == tri1
    r.rowbuf[...] = jnp.zeros_like(r.rowbuf)

    plans_within = red.plans(at_turns((G1_WITHIN, first)))

    def back_within(blk, _):
        for q in range(per):
            chunk = blk * per + q
            at = part(chunk, Q)
            t0 = chunk * Q
            dt, ld, run, bef = chunk_parts(chunk)
            ldt = jnp.log(jnp.maximum(dt, 1e-37))
            cols = jnp.concatenate([ldt[:HP] - run[:HP], ldt[HP:] + bef[HP:]], axis=0).T
            rowf, rowr = bef[:HP], -run[HP:]
            m = r.act[at, inner:]
            entf, readf, entr, readr = m[:, 0:64], m[:, 64:128], m[:, 128:192], m[:, 192:256]
            same = (tri0 + t0 < b) == (tri1 + t0 < b)
            okf, okr = upper & same, lower & same
            scores = jnp.where(okf, nt(entf, readf), jnp.where(okr, nt(entr, readr), 0.0))
            dscore = jnp.zeros((Q, Q), F32)
            for j in range(inner // 128):
                lanes = slice(j * 128, (j + 1) * 128)
                vp = r.act[at, lanes]
                dyp32 = r.dy[at, lanes]
                dyp = dyp32.astype(BF16)
                dw = nt(halves(vp), dyp)
                weights = []
                for i, h in enumerate((2 * j, 2 * j + 1)):
                    e = jnp.where(upper, cols[:, h : h + 1] + rowf[h : h + 1],
                                  cols[:, HP + h : HP + h + 1] + rowr[h : h + 1])
                    x = jnp.exp(jnp.minimum(e, 60.0))
                    weights.append((x * scores).astype(BF16))
                    dwx = dw[i * Q : (i + 1) * Q] * x
                    dscore = dscore + dwx
                    sums = nn((dwx * scores).astype(BF16), sums_low)
                    pf, pr = sums[:, :Q], sums[:, Q:]
                    for place, kept in enumerate((jnp.where(upper, pf, 0.0), jnp.where(lower, pr, 0.0),
                                                  jnp.where(diag, pf, 0.0), jnp.where(diag, pr, 0.0))):
                        r.rowbuf[chunk, place * HP + h : place * HP + h + 1, :] = jnp.sum(kept, axis=0, keepdims=True)
                dv = nn(jnp.concatenate(weights, axis=1), halves(dyp))
                r.mixed[at, lanes] = dv + dyp32 * skip[:, lanes]
            dsf = jnp.where(okf, dscore, 0.0)
            dsr = jnp.where(okr, dscore, 0.0)
            r.mixed[at, inner:] = jnp.concatenate(
                [nn(dsf.astype(BF16), readf), nn(dsf.T.astype(BF16), entf),
                 nn(dsr.astype(BF16), readr), nn(dsr.T.astype(BF16), entr)], axis=1)

        red.hook(blk, plans_within)
        return 0

    lax.fori_loop(0, nblk, back_within, 0)
    swap2.finish()
    df = chain(r.high2)
    dr = chain(r.low2)
    for c in range(nchunk):
        d = nchunk - 1 - c
        r.dstate[d, 0:64, :] = df.astype(BF16)
        df = r.pexp[d, 0:1, :] * df + r.inc[d, 0:64, :]
        r.dstate[c, 64:128, :] = dr.astype(BF16)
        dr = r.pexp[c, 1:2, :] * dr + r.inc[c, 64:128, :]
    r.cg_mine[...] = jnp.zeros_like(r.cg_mine)
    r.hsum[...] = jnp.zeros_like(r.hsum)

    def lent_copy(to):
        return pltpu.make_async_remote_copy(
            src_ref=r.lent_mine, dst_ref=r.lent_other, send_sem=r.edge.at[2], recv_sem=r.edge.at[3],
            device_id=(to, core), device_id_type=MESH)

    lower32, upper32 = lower.astype(F32), upper.astype(F32)

    plans_states = red.plans(at_turns((G1_STATES, first)))

    def back_states(blk, _):
        for q in range(per):
            chunk = blk * per + q
            at = part(chunk, Q)
            dt, ld, run, bef = chunk_parts(chunk)
            ef, er, tf, tr = state_factors(dt, run, bef, chunk * Q, b)
            m = r.act[at, inner:]
            entf, readf, entr, readr = m[:, 0:64], m[:, 64:128], m[:, 128:192], m[:, 192:256]
            state = r.state[chunk]
            grad_state = r.dstate[chunk]
            dy = r.dy[at, :]
            values = r.act[at, :inner].astype(F32)
            dyf, dyr = dy * widen(ef, spread2), dy * widen(er, spread2)
            dreadf = nt(dyf.astype(BF16), state[0:64])
            dreadr = nt(dyr.astype(BF16), state[64:128])
            qf = nt(spread_low, (nn(readf, state[0:64]) * dyf).astype(BF16))
            qr = nt(spread_low, (nn(readr, state[64:128]) * dyr).astype(BF16))
            tfe, tre = widen(tf, spread2), widen(tr, spread2)
            dvf = nn(entf, grad_state[0:64]) * tfe
            dvr = nn(entr, grad_state[64:128]) * tre
            wf = nt(spread_low, (values * dvf).astype(BF16))
            wr = nt(spread_low, (values * dvr).astype(BF16))
            dentf = nt((values * tfe).astype(BF16), grad_state[0:64])
            dentr = nt((values * tre).astype(BF16), grad_state[64:128])
            through = state.astype(F32) * grad_state.astype(F32)
            zf = jnp.sum(through[0:64], axis=0, keepdims=True) * r.pexp[chunk, 0:1, :]
            zr = jnp.sum(through[64:128], axis=0, keepdims=True) * r.pexp[chunk, 1:2, :]
            zf = nt(spread, jnp.broadcast_to(zf, (8, inner)), HIGHEST)[:, 0:1]
            zr = nt(spread, jnp.broadcast_to(zr, (8, inner)), HIGHEST)[:, 0:1]
            r.mixed[at, :inner] = r.mixed[at, :inner] + dvf + dvr
            r.mixed[at, inner:] = r.mixed[at, inner:] + jnp.concatenate([dentf, dreadf, dentr, dreadr], axis=1)
            late = nn(jnp.concatenate([qf, wr], axis=0), lower32, HIGHEST)
            early = nn(jnp.concatenate([wf, qr], axis=0), upper32, HIGHEST)
            rowsum = r.rowbuf[chunk]
            dld = jnp.concatenate(
                [rowsum[0:HP] + late[:HP] + early[:HP] + zf, rowsum[HP : 2 * HP] + late[HP:] + early[HP:] + zr], axis=0)
            dldt = rowsum[2 * HP : 4 * HP] + jnp.concatenate([wf, wr], axis=0)
            sig = jax.nn.sigmoid(r.step[:, at] + bias)
            ratio = jnp.where(dt < 1e-30, 1.0, sig / jnp.maximum(dt, 1e-30))
            graw = dldt * ratio - jnp.exp(dlog) * sig * dld
            r.gstep[:, at] = graw.astype(BF16)
            r.hsum[:, 0:1] += jnp.sum(graw, axis=1, keepdims=True)
            r.hsum[:, 1:2] += jnp.sum(dld * ld, axis=1, keepdims=True)

        @pl.when(blk == 0)
        def _():
            tok8 = iota((8, 1), 0)
            masks = [conv_mask(tok8, m, b, off0) for m in range(4)]
            rows = r.joined[0:32, :].astype(F32)
            tap = r.tap[...]
            total = rows[16:24] * tap[3:4]
            for m in range(1, 4):
                total = total + rows[16 - m : 24 - m] * masks[m] * tap[3 - m : 4 - m]
            sig = jax.nn.sigmoid(total)
            dconv = r.mixed[0:8, :] * (sig * (1.0 + total * (1.0 - sig)))
            first = jnp.concatenate([jnp.zeros((8, both), F32), dconv], axis=0)
            lent = jnp.zeros((8, both), F32)
            for m in range(1, 4):
                lent = lent + first[m : m + 8] * conv_mask(tok8 - 8 + m, m, b, off0) * tap[3 - m : 4 - m]
            r.lent_mine[...] = lent

            @pl.when(me > 0)
            def _():
                lent_copy(me - 1).start()

        red.hook(blk, plans_states)
        return 0

    lax.fori_loop(0, nblk, back_states, 0)

    @pl.when(me + 1 < count)
    def _():
        lent_copy(me - 1).wait_recv()

    @pl.when(me + 1 == count)
    def _():
        r.lent_other[...] = jnp.zeros_like(r.lent_other)

    r.dbuf[length : length + 8, :] = jnp.zeros((8, 256), F32)

    def back_conv(g):
        cols = slice(g * 256, (g + 1) * 256)

        def one(i, _):
            blk = nblk - 1 - i
            rows = part(blk, TB)
            tok = iota((TB, 1), 0) + blk * TB
            masks = [conv_mask(tok, m, b, off0) for m in range(4)]
            later = [conv_mask(tok + m, m, b, off0) for m in range(4)]
            shifted, tap, total = conv_rows(blk, cols, g * 256, masks, 256)
            sig = jax.nn.sigmoid(total)
            dconv = r.mixed[rows, cols] * (sig * (1.0 + total * (1.0 - sig)))
            r.dbuf[rows, :] = dconv
            for m in range(4):
                r.cg_mine[3 - m : 4 - m, cols] += jnp.sum(dconv * shifted[m], axis=0, keepdims=True)
            grad = dconv * tap[3:4]
            ahead = r.dbuf[pl.ds(pl.multiple_of(blk * TB, TB), TB + 8), :]
            for m in range(1, 4):
                grad = grad + ahead[m : m + TB] * later[m] * tap[3 - m : 4 - m]
            last = jnp.where(blk == nblk - 1, 1.0, 0.0)
            grad = jnp.concatenate([grad[: TB - 8], grad[TB - 8 :] + r.lent_other[:, cols] * last], axis=0)
            if g * 256 < inner:
                r.buf[rows, cols] = grad.astype(BF16)
            else:
                r.gs_mine[rows, :] = grad.astype(BF16)
            return 0

        lax.fori_loop(0, nblk, one, 0)

    back_conv(inner // 256)
    gs_copy = over(r.gs_mine, r.gs_other, r.misc_sem, 0)
    gs_copy.start()
    cg_copy = over(r.cg_mine.at[:, pl.ds(inner, maps)], r.cg_other, r.misc_sem, 1)
    cg_copy.start()
    for g in range(inner // 256):
        cols = slice(g * 256, (g + 1) * 256)
        back_conv(g)
        pieces[2 + g]["work"][...] = nn(r.normt[...], r.buf[:, cols]).astype(BF16)
        red.start(2 + g)
        if g in G1_CONV:
            red.advance(0)
            red.advance(1)
    gs_copy.wait()
    cg_copy.wait()
    r.gs[...] = (r.gs_mine[...].astype(F32) + r.gs_other[...].astype(F32)).astype(BF16)
    r.gsw_w[:, :maps] = nn(r.normt[...], r.gs[...]).astype(BF16)
    gstep = jnp.concatenate([r.gstep[...].astype(F32), jnp.zeros((128 - 2 * HP, length), F32)], axis=0)
    r.gsw_w[:, maps:] = nt(r.normt[...], gstep.astype(BF16)).astype(BF16)
    red.start(first_state)

    later_pieces = list(range(2, len(pieces)))

    plans_down = red.plans(at_turns((G1_DOWN, first), (G2_DOWN, later_pieces)))

    def down(blk, _):
        rows = part(blk, TB)
        gn = nt(r.ggate[rows, :], r.wg[...]) + nt(r.buf[rows, :], r.wv[...]) + tn(r.gstep[:, rows], r.wst[...])
        r.gn_mine[rows, :] = gn.astype(BF16)
        over(r.gn_mine.at[rows], r.gn_other.at[rows], r.gn_sem, blk).start()
        red.hook(blk, plans_down)
        return 0

    lax.fori_loop(0, nblk, down, 0)
    tiny = r.tiny_w.at[0]
    tiny[...] = jnp.zeros((16, both), F32)
    tiny[0:2, :inner] = r.small[0:2, :]
    tiny[4:6, 0 : 2 * HP] = r.hsum[...].T[0:2]
    tiny[8:16, :inner] = r.cg_mine[:, :inner]
    tiny[8:16, inner:] = r.cg_mine[:, inner:] + r.cg_other[...]

    def out_copy(blk):
        rows = part(blk, TB)
        return (pltpu.make_async_copy(r.out_other.at[rows], r.block_out.at[rows], r.store.at[0, blk]),
                pltpu.make_async_copy(r.gate.at[rows], r.grad_hidden.at[rows], r.store.at[1, blk]))

    plans_end = red.plans(at_turns((G1_END, first), (G2_END, later_pieces)))

    def ending(blk, _):
        rows = part(blk, TB)
        over(r.out_mine.at[rows], r.out_other.at[rows], r.out_sem, blk).wait()
        over(r.gn_mine.at[rows], r.gn_other.at[rows], r.gn_sem, blk).wait()
        x = r.hid[rows, :].astype(F32)
        r.out_other[rows, :] = (
            x + (r.out_mine[rows, :].astype(F32) + r.out_other[rows, :].astype(F32))).astype(BF16)
        gn = r.gn_mine[rows, :].astype(F32) + r.gn_other[rows, :].astype(F32) + nt(r.gs[rows, :], r.ws[...])
        scale = lax.rsqrt(jnp.mean(x * x, axis=1, keepdims=True) + EPSILON)
        tiny[2:3, :width] += jnp.sum(gn * x * scale, axis=0, keepdims=True)
        v = gn * gain
        mean = jnp.mean(x * v, axis=1, keepdims=True)
        r.gate[rows, :] = r.cot[rows, :].astype(F32) + scale * v - x * (scale * scale * scale * mean)
        for copy in out_copy(blk):
            copy.start()
        red.hook(blk, plans_end)
        return 0

    lax.fori_loop(0, nblk, ending, 0)

    def tiny_copy(s):
        return pltpu.make_async_remote_copy(
            src_ref=r.tiny_w.at[s], dst_ref=r.tiny_r.at[s], send_sem=r.tiny_sem.at[0, s],
            recv_sem=r.tiny_sem.at[1, s], device_id=(red.mates[s], core), device_id_type=MESH)

    tiny_copy(0).start()
    for s in range(bits):
        tiny_copy(s).wait()
        r.tiny_w[s + 1] = r.tiny_w[s] + r.tiny_r[s]
        if s + 1 < bits:
            tiny_copy(s + 1).start()
        for p in range(len(pieces)):
            red.advance(p)
    stores = [
        pltpu.make_async_copy(src, dst, r.store.at[2, i]) for i, (src, dst) in enumerate(
            ((r.ggw_o, r.ggw_any), (r.gow_o, r.gow_any), (r.gsw_o, r.gsw_any),
             *((pieces[2 + g]["out"], r.gvw_any.at[:, pl.ds(g * 256, 256)]) for g in range(groups)),
             (r.tiny_w.at[bits], r.tiny_any)))]
    stores[-1].start()
    while any(red.pos[p] < len(red.steps[p]) for p in range(len(pieces))):
        for p in range(len(pieces)):
            red.advance(p)
    for p in range(len(pieces)):
        red.finish(p)
    for store in stores[:-1]:
        store.start()
    for store in stores:
        store.wait()
    for blk in range(nblk):
        for copy in out_copy(blk):
            copy.wait()

    @pl.when(me + 1 < count)
    def _():
        halo_copy(me + 1).wait_send()

    @pl.when(me > 0)
    def _():
        lent_copy(me - 1).wait_send()


G1_WITHIN = (2, 3)
G1_STATES = (1, 2, 3)
G1_CONV = (1, 2)
G1_DOWN = (1, 3)
G2_DOWN = (2,)
G1_END = ()
G2_END = (0, 2)


def last_kernel(heads, ggw_ref, gow_ref, gvw_ref, gsw_ref, tiny_ref,
                ngain_ref, ggwo_ref, gvwo_ref, gswo_ref, gsteo_ref, convv_ref, convs_ref, bias_ref, decay_ref,
                skip_ref, ggain_ref, gowo_ref):
    ggwo_ref[...] = ggw_ref[...].astype(F32)
    gvwo_ref[...] = gvw_ref[...].astype(F32)
    maps = gswo_ref.shape[1]
    gswo_ref[...] = gsw_ref[:, :maps].astype(F32)
    step = gsw_ref[:, maps:].astype(F32).T
    gsteo_ref[...] = jnp.stack([step[:heads], step[HP : HP + heads]], axis=1)
    gowo_ref[...] = gow_ref[...].astype(F32)

    @pl.when(pl.program_id(0) == 0)
    def _():
        width, inner = ngain_ref.shape[0], convv_ref.shape[1]
        ngain_ref[...] = tiny_ref[2, :width]
        ggain_ref[...] = tiny_ref[0, :inner]
        convv_ref[...] = tiny_ref[8:12, :inner]
        convs_ref[...] = tiny_ref[8:12, inner:]
        bias_ref[...] = jnp.concatenate([tiny_ref[4:5, 0:heads], tiny_ref[4:5, HP : HP + heads]], axis=0)
        decay_ref[...] = (tiny_ref[5:6, 0:heads] + tiny_ref[5:6, HP : HP + heads]).reshape(heads)
        spread = spread_matrix(inner, inner // heads)
        total = nt(jnp.broadcast_to(tiny_ref[1:2, :inner], (8, inner)), spread, HIGHEST)
        skip_ref[...] = total[0:1, :heads].reshape(heads)


SMEM_SPEC = pl.BlockSpec(memory_space=pltpu.SMEM)
VMEM_SPEC = pl.BlockSpec(memory_space=pltpu.VMEM)
ANY_SPEC = pl.BlockSpec(memory_space=pl.ANY)


def body(
    hidden_in, norm_gain, gate_proj, value_proj, state_proj, step_proj, conv_value, conv_state,
    step_bias, decay_log, skip_scale, gate_gain, out_proj, lengths, cotangent,
):
    length, width = hidden_in.shape
    inner = gate_proj.shape[1]
    heads = decay_log.shape[0]
    maps = state_proj.shape[1]
    both = inner + maps
    nblk, nchunk = length // TB, length // Q
    count = lax.axis_size("seq")
    bits = count.bit_length() - 1
    assert count == 1 << bits
    reach = min(1 + (LEN_MOST - 2) // length, count - 1)
    npieces = 3 + inner // 256

    def vmem(*dims, dtype=F32):
        return pltpu.VMEM(dims, dtype)

    dma = pltpu.SemaphoreType.DMA
    low = dict(dtype=BF16)
    scratch = dict(
        hid=vmem(length, width, **low), wg=vmem(width, inner, **low), wv=vmem(width, inner, **low),
        ws=vmem(width, maps, **low), wo=vmem(inner, width, **low), cot=vmem(length, width, **low),
        wst=vmem(2 * HP, width, **low), tap=vmem(4, both),
        normt=vmem(width, length, **low), buf=vmem(length, inner, **low), gate=vmem(length, inner),
        joined=vmem(16 + length, both, **low), act=vmem(length, both, **low), step=vmem(2 * HP, length),
        inc=vmem(nchunk, 128, inner), pexp=vmem(nchunk, 2, inner), mixed=vmem(length, both),
        state=vmem(nchunk, 128, inner, **low), dstate=vmem(nchunk, 128, inner, **low),
        dy=vmem(length, inner), ggate=vmem(length, inner, **low), gstep=vmem(2 * HP, length, **low),
        msgs=vmem(4, 80, inner, **low),
        low1=vmem(reach, 80, inner, **low), high1=vmem(reach, 80, inner, **low),
        low2=vmem(reach, 80, inner, **low), high2=vmem(reach, 80, inner, **low),
        rowbuf=vmem(nchunk, 4 * HP, Q), jx=vmem(TB + 16, 256), dbuf=vmem(length + 8, 256),
        halo=vmem(16, width, **low), mine=vmem(nblk, 8, TB), other=vmem(nblk, 8, TB),
        out_mine=vmem(length, width, **low), out_other=vmem(length, width, **low),
        gn_mine=vmem(length, width, **low), gn_other=vmem(length, width, **low),
        gs_mine=vmem(length, maps, **low), gs_other=vmem(length, maps, **low), gs=vmem(length, maps, **low),
        lent_mine=vmem(8, both), lent_other=vmem(8, both), cg_mine=vmem(8, both), cg_other=vmem(8, maps),
        hsum=vmem(2 * HP, 128), small=vmem(8, inner),
        tiny_w=vmem(bits + 1, 16, both), tiny_r=vmem(bits, 16, both),
    )
    for name, rows, cols in (("ggw", width, inner), ("gow", inner, width), ("gsw", width, maps + 128), *((f"gv{g}", width, 256) for g in range(inner // 256))):
        scratch[name + "_w"] = vmem(rows, cols, **low)
        scratch[name + "_k"] = vmem(rows // 2, cols, **low)
        scratch[name + "_r"] = vmem(received_rows(rows, bits), cols, **low)
        scratch[name + "_o"] = vmem(rows, cols, **low)
    scratch.update(
        load=dma((6,)), store=dma((3, max(nblk, 4 + inner // 256))), edge=dma((4,)), sum_sem=dma((2, nblk)), out_sem=dma((2, nblk)),
        gn_sem=dma((2, nblk)), misc_sem=dma((2, 2)), tiny_sem=dma((2, bits)),
        up_s=dma((2, reach)), up_r=dma((2, reach)), dn_s=dma((2, reach)), dn_r=dma((2, reach)),
        rs_s=dma((npieces, bits)), rs_r=dma((npieces, bits)), ag_s=dma((npieces, bits)), ag_r=dma((npieces, bits)),
    )

    def shape(*dims, dtype=F32):
        return jax.ShapeDtypeStruct(dims, dtype)

    outs = pl.pallas_call(
        partial(layer_kernel, reach, bits, NAMES_IN + NAMES_OUT + tuple(scratch)),
        in_specs=[SMEM_SPEC] + [ANY_SPEC] * 6 + [VMEM_SPEC] * 8,
        out_specs=[ANY_SPEC] * 7,
        out_shape=[shape(length, width, **low), shape(length, width), shape(width, inner, **low),
                   shape(inner, width, **low), shape(width, inner, **low), shape(width, maps + 128, **low),
                   shape(16, both)],
        scratch_shapes=list(scratch.values()),
        compiler_params=pltpu.CompilerParams(
            collective_id=1, has_side_effects=True, vmem_limit_bytes=VMEM_LIMIT),
    )(lengths, hidden_in, gate_proj, value_proj, state_proj, out_proj, cotangent,
      norm_gain, step_proj.transpose(2, 0, 1), conv_value, conv_state, step_bias, decay_log, skip_scale, gate_gain)
    block_out, grad_hidden, ggw, gow, gvw, gsw, tiny = outs

    rows = 128
    def tall(cols):
        return pl.BlockSpec((rows, cols), lambda i: (i, 0))

    def whole(*dims):
        return pl.BlockSpec(dims, lambda i: (0,) * len(dims))

    assert width % rows == 0 and inner % rows == 0 and inner == width
    final = pl.pallas_call(
        partial(last_kernel, heads),
        grid=(width // rows,),
        in_specs=[tall(inner), tall(width), tall(inner), tall(maps + 128), whole(16, both)],
        out_specs=[whole(width), tall(inner), tall(inner), tall(maps), pl.BlockSpec((heads, 2, rows), lambda i: (0, 0, i)), whole(4, inner),
                   whole(4, maps), whole(2, heads), whole(heads), whole(heads), whole(inner), tall(width)],
        out_shape=[shape(width), shape(width, inner), shape(width, inner), shape(width, maps),
                   shape(heads, 2, width), shape(4, inner), shape(4, maps), shape(2, heads), shape(heads),
                   shape(heads), shape(inner), shape(inner, width)],
        compiler_params=pltpu.CompilerParams(dimension_semantics=("arbitrary",), vmem_limit_bytes=60 * MIB),
    )(ggw, gow, gvw, gsw, tiny)
    ngain, ggw, gvw, gsw, gstepw, convv, convs, bias, decay, skip, ggain, gow = final
    return (block_out, grad_hidden, ngain, ggw, gvw, gsw, gstepw.transpose(1, 2, 0), convv, convs, bias, decay, skip,
            ggain, gow)


def solution(mesh):
    in_specs = (
        P("seq", None),
        P(),
        P(None, "head"),
        P(None, "head"),
        P(),
        P(None, None, "head"),
        P(None, "head"),
        P(),
        P(None, "head"),
        P("head"),
        P("head"),
        P("head"),
        P("head", None),
        P(),
        P("seq", None),
    )
    out_specs = (
        P("seq", None),
        P("seq", None),
        P(),
        P(None, "head"),
        P(None, "head"),
        P(),
        P(None, None, "head"),
        P(None, "head"),
        P(),
        P(None, "head"),
        P("head"),
        P("head"),
        P("head"),
        P("head", None),
    )
    return jax.shard_map(body, mesh=mesh, in_specs=in_specs, out_specs=out_specs, check_vma=False)
```

```python
from functools import partial

import jax
import jax.numpy as jnp
from jax import lax
from jax.experimental import pallas as pl
from jax.experimental.pallas import tpu as pltpu
from jax.sharding import PartitionSpec as P

EPSILON = 1e-05
LEN_MOST = 4096
Q = 128
TB = 256
HP = 16
MIB = 1024 * 1024
VMEM_LIMIT = 63 * MIB
HIGHEST = lax.Precision.HIGHEST
F32 = jnp.float32
BF16 = jnp.bfloat16
MESH = pl.DeviceIdType.MESH


def nn(a, b, precision=None):
    return jnp.dot(a, b, preferred_element_type=F32, precision=precision)


def nt(a, b, precision=None):
    return lax.dot_general(a, b, (((1,), (1,)), ((), ())), preferred_element_type=F32, precision=precision)


def tn(a, b, precision=None):
    return lax.dot_general(a, b, (((0,), (0,)), ((), ())), preferred_element_type=F32, precision=precision)


def iota(shape, axis):
    return lax.broadcasted_iota(jnp.int32, shape, axis)


def spread_matrix(width, hdim):
    return (iota((HP, width), 1) // hdim == iota((HP, width), 0)).astype(F32)


def split(x):
    hi = x.astype(BF16)
    return hi, (x - hi.astype(F32)).astype(BF16)


def widen(rows, spread2):
    hi, lo = split(rows.T)
    return nn(jnp.concatenate([hi, lo], axis=1), spread2)


def widen_col(col, spread):
    return tn(jnp.broadcast_to(col, (HP, 8)), spread, HIGHEST)[0:1]


def silu(x):
    return x * jax.nn.sigmoid(x)


def softplus(x):
    return jnp.maximum(x, 0.0) + jnp.log1p(jnp.exp(-jnp.abs(x)))


def step_parts(step, bias, dlog):
    dt = softplus(step + bias)
    ld = -jnp.exp(dlog) * dt
    upto = (iota((Q, Q), 0) <= iota((Q, Q), 1)).astype(F32)
    run = nn(ld, upto, HIGHEST)
    return dt, ld, run, run - ld


def state_factors(dt, run, bef, t0, b):
    t1 = t0 + Q
    tok = iota((1, Q), 1) + t0
    ef = jnp.where((tok < b) | (t0 > b), jnp.exp(bef[:HP]), 0.0)
    er = jnp.where((tok >= b) | (t1 < b), jnp.exp(run[HP:, Q - 1 : Q] - run[HP:]), 0.0)
    tf = jnp.where((tok >= b) | (t1 <= b), jnp.exp(run[:HP, Q - 1 : Q] - run[:HP]), 0.0) * dt[:HP]
    tr = jnp.where((tok < b) | (t0 >= b), jnp.exp(bef[HP:]), 0.0) * dt[HP:]
    return ef, er, tf, tr


def conv_mask(tok, shift, b, off0):
    lost = ((tok < b) & (tok + off0 < shift)) | ((tok >= b) & (tok < b + shift))
    return jnp.where(lost, 0.0, 1.0)


def put_message(ref, state, passed):
    hi, lo = split(passed)
    ref[0:64, :] = state.astype(BF16)
    row = iota((16, state.shape[1]), 0)
    tail = jnp.where(row == 0, hi.astype(F32), jnp.where(row == 1, lo.astype(F32), 0.0))
    ref[64:80, :] = tail.astype(BF16)


def chain(ref):
    total = ref[0, 0:64, :].astype(F32)
    passed = None
    for k in range(1, ref.shape[0]):
        tail = ref[k - 1, 64:80, :].astype(F32)
        here = tail[0:1] + tail[1:2]
        passed = here if passed is None else passed * here
        total = total + passed * ref[k, 0:64, :].astype(F32)
    return total


class Swap:
    def __init__(self, reach, up_ref, down_ref, from_low, from_high, up_send, up_recv, down_send, down_recv):
        self.me, self.core, self.count = lax.axis_index("seq"), lax.axis_index("head"), lax.axis_size("seq")
        self.reach, self.up_ref, self.down_ref, self.from_low, self.from_high = reach, up_ref, down_ref, from_low, from_high
        self.sems = up_send, up_recv, down_send, down_recv

    def up(self, k):
        return pltpu.make_async_remote_copy(
            src_ref=self.up_ref, dst_ref=self.from_low.at[k - 1], send_sem=self.sems[0].at[k - 1],
            recv_sem=self.sems[1].at[k - 1], device_id=(self.me + k, self.core), device_id_type=MESH)

    def down(self, k):
        return pltpu.make_async_remote_copy(
            src_ref=self.down_ref, dst_ref=self.from_high.at[k - 1], send_sem=self.sems[2].at[k - 1],
            recv_sem=self.sems[3].at[k - 1], device_id=(self.me - k, self.core), device_id_type=MESH)

    def greet(self, barrier):
        me, core, count = self.me, self.core, self.count
        for k in range(1, self.reach + 1):
            @pl.when(me + k < count)
            def _():
                pl.semaphore_signal(barrier, inc=1, device_id=(me + k, core), device_id_type=MESH)

            @pl.when(me >= k)
            def _():
                pl.semaphore_signal(barrier, inc=1, device_id=(me - k, core), device_id_type=MESH)
        return jnp.minimum(me, self.reach) + jnp.minimum(count - 1 - me, self.reach)

    def start(self):
        me, count = self.me, self.count
        for k in range(1, self.reach + 1):
            @pl.when(me + k < count)
            def _():
                self.up(k).start()

            @pl.when(me >= k)
            def _():
                self.down(k).start()

            @pl.when(me < k)
            def _():
                self.from_low[k - 1] = jnp.zeros_like(self.from_low[k - 1])

            @pl.when(me + k >= count)
            def _():
                self.from_high[k - 1] = jnp.zeros_like(self.from_high[k - 1])

    def finish(self):
        me, count = self.me, self.count
        for k in range(1, self.reach + 1):
            @pl.when(me + k < count)
            def _():
                self.up(k).wait_send()
                self.down(k).wait_recv()

            @pl.when(me >= k)
            def _():
                self.down(k).wait_send()
                self.up(k).wait_recv()


def chunk_scores(maps, t0, b):
    tr, tc = iota((Q, Q), 0), iota((Q, Q), 1)
    same = (tr + t0 < b) == (tc + t0 < b)
    fwd = nt(maps[:, 64:128], maps[:, 0:64])
    rev = nt(maps[:, 192:256], maps[:, 128:192])
    return jnp.where((tr > tc) & same, fwd, jnp.where((tr < tc) & same, rev, 0.0))


def halves(x):
    left = iota(x.shape, 1) < 64
    zero = jnp.zeros_like(x)
    return jnp.concatenate([jnp.where(left, x, zero), jnp.where(left, zero, x)], axis=0)


class Reduce:
    def __init__(self, bits, pieces, rs_send, rs_recv, ag_send, ag_recv):
        me, core = lax.axis_index("seq"), lax.axis_index("head")
        bit = [lax.rem(me // (1 << k), 2) for k in range(bits)]
        mate = [me + (1 - 2 * bit[k]) * (1 << k) for k in range(bits)]
        self.mates = list(mate)
        self.bits, self.bit, self.mate, self.core, self.pieces = bits, bit, mate, core, pieces
        self.sems = rs_send, rs_recv, ag_send, ag_recv
        self.pos = [0] * len(pieces)
        self.steps = []
        for piece in pieces:
            halvings = halvings_of(piece["work"].shape[0], bits)
            self.steps.append([("rs", s) for s in range(bits)] + [("ag", s) for s in reversed(range(halvings))])

    def geometry(self, p, s):
        rows = self.pieces[p]["work"].shape[0]
        halvings = halvings_of(rows, self.bits)
        off, slot = jnp.int32(0), 0
        for t in range(s):
            if t < halvings:
                rows = rows // 2
                off = off + self.bit[self.pieces[p]["order"][t]] * rows
            slot += rows
        return off, rows, slot, s < halvings

    def remote(self, src, dst, send, recv, k):
        return pltpu.make_async_remote_copy(
            src_ref=src, dst_ref=dst, send_sem=send, recv_sem=recv, device_id=(self.mate[k], self.core),
            device_id_type=MESH)

    def first(self, p):
        return self.bit[self.pieces[p]["order"][0]] * (self.pieces[p]["work"].shape[0] // 2)

    def copy(self, p, step):
        kind, s = step
        piece = self.pieces[p]
        k = piece["order"][s]
        if kind == "rs":
            off, rows, slot, halved = self.geometry(p, s)
            source, off = (piece["work"], off) if s == 0 else (piece["kept"], off - self.first(p))
            if halved:
                rows = rows // 2
                off = off + (1 - self.bit[k]) * rows
            return self.remote(
                source.at[pl.ds(pl.multiple_of(off, 16), rows)], piece["recv"].at[pl.ds(slot, rows)],
                self.sems[0].at[p, s], self.sems[1].at[p, s], k)
        off, rows, _, _ = self.geometry(p, s + 1)
        where = piece["out"].at[pl.ds(pl.multiple_of(off, 16), rows)]
        return self.remote(where, where, self.sems[2].at[p, s], self.sems[3].at[p, s], k)

    def arriving(self, p, s):
        off, rows, _, _ = self.geometry(p, s + 1)
        k = self.pieces[p]["order"][s]
        off = off + (1 - 2 * self.bit[k]) * rows
        where = self.pieces[p]["out"].at[pl.ds(pl.multiple_of(off, 16), rows)]
        return self.remote(where, where, self.sems[2].at[p, s], self.sems[3].at[p, s], k)

    def start(self, p):
        self.copy(p, self.steps[p][0]).start()

    def step(self, p, at):
        kind, s = self.steps[p][at]
        if kind == "rs":
            self.add(p, s, self.copy(p, (kind, s)))
        else:
            self.arriving(p, s).wait_recv()
        if at + 1 < len(self.steps[p]):
            self.copy(p, self.steps[p][at + 1]).start()

    def take(self, name):
        if self.bits != TABLE_BITS:
            return []
        taken = TABLE.get(name, ())
        for p, at in taken:
            assert self.pos[p] == at
            self.pos[p] = at + 1
        return taken

    def at(self, name):
        for p, at in self.take(name):
            self.step(p, at)

    def takes(self, name, count):
        return {k: self.take(name + str(k)) for k in range(count)}

    def hook(self, turn, taken):
        for k, steps in taken.items():
            if steps:
                @pl.when(turn == k)
                def _():
                    for p, at in steps:
                        self.step(p, at)

    def left(self):
        order = list(TABLE["tail"]) if self.bits == TABLE_BITS else []
        rest = [(p, at) for p in range(len(self.pieces)) for at in range(self.pos[p], len(self.steps[p]))]
        return order + sorted((x for x in rest if x not in order), key=lambda x: x[::-1])

    def add(self, p, s, copy):
        piece = self.pieces[p]
        off, rows, slot, halved = self.geometry(p, s)
        if halved:
            copy.wait_recv()
            rows = rows // 2
            off = off + self.bit[piece["order"][s]] * rows
        else:
            copy.wait()
        recv, rel = piece["recv"], off - self.first(p)
        source, at = (piece["work"], off) if s == 0 else (piece["kept"], rel)
        dest, to = (piece["out"], off) if s == self.bits - 1 else (piece["kept"], rel)
        size = next(n for n in (64, 48, 32, 16) if rows % n == 0)

        def one(i, _):
            total = source[pl.ds(pl.multiple_of(at + i * size, 16), size), :].astype(F32)
            total = total + recv[pl.ds(pl.multiple_of(slot + i * size, 16), size), :].astype(F32)
            dest[pl.ds(pl.multiple_of(to + i * size, 16), size), :] = total.astype(BF16)
            return 0

        lax.fori_loop(0, rows // size, one, 0)

    def finish(self, p):
        for kind, s in self.steps[p]:
            if kind == "ag" or self.geometry(p, s)[3]:
                self.copy(p, (kind, s)).wait_send()


def halvings_of(rows, bits):
    made = 0
    while made < bits and (rows >> made) % 32 == 0:
        made += 1
    return made


def piece_names(width, inner):
    return ([f"ggw{g}" for g in range(width // 256)] + [f"gow{g}" for g in range(inner // 256)]
            + [f"gv{g}" for g in range(inner // 256)] + ["gsw"])


def received_rows(rows, bits):
    halvings, total = halvings_of(rows, bits), 0
    for s in range(bits):
        rows = rows // 2 if s < halvings else rows
        total += rows
    return total


def part(i, size):
    return pl.ds(pl.multiple_of(i * size, size), size)


class Refs:
    pass


NAMES_IN = ("lengths", "hid_any", "wg_any", "wv_any", "ws_any", "wo_any", "cot_any",
            "gain", "wstep", "tapv", "taps", "bias", "dlog", "skip", "ggain")
NAMES_OUT = ("block_out", "grad_hidden", "ggw_any", "gow_any", "gvw_any", "gsw_any", "tiny_any")


def layer_kernel(reach, bits, names, *refs):
    r = Refs()
    for name, ref in zip(names, refs):
        setattr(r, name, ref)
    length, width = r.hid.shape
    inner = r.wo.shape[0]
    maps = r.ws.shape[1]
    both = inner + maps
    heads = r.dlog.shape[0]
    nblk, nchunk, per = length // TB, length // Q, TB // Q
    me, core, count = lax.axis_index("seq"), lax.axis_index("head"), lax.axis_size("seq")
    base = me * length

    loads = [pltpu.make_async_copy(src, dst, r.load.at[i]) for i, (src, dst) in enumerate(
        ((r.hid_any, r.hid), (r.wv_any, r.wv), (r.ws_any, r.ws), (r.wg_any, r.wg), (r.wo_any, r.wo),
         (r.cot_any, r.cot)))]
    for load in loads:
        load.start()

    swap1 = Swap(reach, r.msgs.at[0], r.msgs.at[1], r.low1, r.high1, r.up_s.at[0], r.up_r.at[0], r.dn_s.at[0], r.dn_r.at[0])
    swap2 = Swap(reach, r.msgs.at[2], r.msgs.at[3], r.low2, r.high2, r.up_s.at[1], r.up_r.at[1], r.dn_s.at[1], r.dn_r.at[1])
    groups = inner // 256
    names = piece_names(width, inner)
    orders = [ORDERS[i % len(ORDERS)] if bits == TABLE_BITS else tuple(range(bits)) for i in range(len(names))]
    pieces = [
        dict(work=getattr(r, name + "_w"), kept=getattr(r, name + "_k"), recv=getattr(r, name + "_r"),
             out=getattr(r, name + "_o"), order=order)
        for name, order in zip(names, orders)
    ]
    of = {name: i for i, name in enumerate(names)}
    red = Reduce(bits, pieces, r.rs_s, r.rs_r, r.ag_s, r.ag_r)
    barrier = pltpu.get_barrier_semaphore()
    near = swap1.greet(barrier)
    for mate in red.mates:
        pl.semaphore_signal(barrier, inc=1, device_id=(mate, core), device_id_type=MESH)
    pl.semaphore_signal(barrier, inc=1, device_id=(me, 1 - core), device_id_type=MESH)

    def over(src, dst, sems, k):
        return pltpu.make_async_remote_copy(
            src_ref=src, dst_ref=dst, send_sem=sems.at[0, k], recv_sem=sems.at[1, k], device_id=(me, 1 - core),
            device_id_type=MESH)

    def one_sequence(j, carry):
        start, b, off0, after = carry
        end = start + r.lengths[j]
        b = jnp.where((start > base) & (start < base + length), start - base, b)
        off0 = jnp.where((start <= base) & (base < end), base - start, off0)
        after = jnp.where(end == base + length, 0, after)
        return end, b, off0, after

    _, b, off0, after = lax.fori_loop(
        0, r.lengths.shape[0], one_sequence, (jnp.int32(0), jnp.int32(length + 1), jnp.int32(0), jnp.int32(1)))
    before_f = jnp.where(off0 > 0, 1.0, 0.0)
    after_f = after.astype(F32)

    def lanes128(x):
        return jnp.concatenate([x, jnp.zeros((x.shape[0], 128 - x.shape[1]), F32)], axis=1)

    small_cols = jnp.concatenate(
        [lanes128(r.bias[...]), lanes128(r.dlog[...].reshape(1, heads)), lanes128(r.skip[...].reshape(1, heads)),
         jnp.zeros((4, 128), F32)], axis=0).T
    bias = jnp.concatenate([small_cols[:HP, 0:1], small_cols[:HP, 1:2]], axis=0)
    dlog = jnp.concatenate([small_cols[:HP, 2:3], small_cols[:HP, 2:3]], axis=0)
    spread = spread_matrix(inner, inner // heads)
    spread_low = spread.astype(BF16)
    spread2 = jnp.concatenate([spread_low, spread_low], axis=0)
    skip = widen_col(small_cols[:HP, 3:4], spread)
    gain = r.gain[...].reshape(1, width)
    ggain = r.ggain[...].reshape(1, inner)
    r.wst[...] = jnp.zeros_like(r.wst)
    wstep = r.wstep[...].astype(F32)
    for k in range(2):
        r.wst[k * HP : (k + 1) * HP, :] = jnp.concatenate(
            [wstep[:, k, :], jnp.zeros((HP - heads, width), F32)], axis=0).astype(BF16)

    r.tap[:, :inner] = r.tapv[...]
    r.tap[:, inner:] = r.taps[...]
    for blk in range(nblk):
        tok = iota((TB, 128), 0) + blk * TB
        for m in range(1, 4):
            r.valid[m - 1, blk * TB : (blk + 1) * TB, :] = conv_mask(tok, m, b, off0).astype(BF16)

    loads[0].wait()
    loads[1].wait()
    loads[2].wait()

    def normalize(x):
        x = x.astype(F32)
        scale = lax.rsqrt(jnp.mean(x * x, axis=1, keepdims=True) + EPSILON)
        return (x * scale * gain).astype(BF16)

    def project(blk, _):
        rows = part(blk, TB)
        normed = normalize(r.hid[rows, :])
        r.buf[rows, :] = normed
        r.normt[:, rows] = normed.T
        dest = pl.ds(pl.multiple_of(16 + blk * TB, 16), TB)
        r.joined[dest, :inner] = nn(normed, r.wv[...]).astype(BF16)
        r.joined[dest, inner:] = nn(normed, r.ws[...]).astype(BF16)
        r.step[:, rows] = nt(r.wst[...], normed)
        return 0

    lax.fori_loop(0, nblk, project, 0)

    pl.semaphore_wait(barrier, near + bits + 1)

    def halo_copy(to):
        return pltpu.make_async_remote_copy(
            src_ref=r.hid.at[pl.ds(length - 16, 16)], dst_ref=r.halo, send_sem=r.edge.at[0], recv_sem=r.edge.at[1],
            device_id=(to, core), device_id_type=MESH)

    @pl.when(me + 1 < count)
    def _():
        halo_copy(me + 1).start()

    @pl.when(me == 0)
    def _():
        r.halo[...] = jnp.zeros_like(r.halo)

    def valid_of(rows, m):
        one = r.valid[m - 1, rows, :].astype(F32)
        return jnp.concatenate([one, one], axis=1)

    def chunk_parts(chunk):
        cols = part(chunk, Q)
        return step_parts(r.step[:, cols], bias, dlog)

    def summarize(blk, _):
        rows = part(blk, TB)
        for g in range(both // 256):
            cols = slice(g * 256, (g + 1) * 256)
            r.jx[...] = r.joined[pl.ds(pl.multiple_of(blk * TB, 16), TB + 16), cols].astype(F32)
            tap = r.tap[:, cols]
            total = r.jx[16 : 16 + TB, :] * tap[3:4]
            for m in range(1, 4):
                total = total + r.jx[16 - m : 16 - m + TB, :] * valid_of(rows, m) * tap[3 - m : 4 - m]
            sig = jax.nn.sigmoid(total)
            r.act[rows, cols] = (total * sig).astype(BF16)
            r.slope[rows, cols] = (sig * (1.0 + total * (1.0 - sig))).astype(BF16)
        for q in range(per):
            chunk = blk * per + q
            t0 = chunk * Q
            at = part(chunk, Q)
            dt, ld, run, bef = chunk_parts(chunk)
            _, _, tf, tr = state_factors(dt, run, bef, t0, b)
            values = r.act[at, :inner].astype(F32)
            maps_t = r.act[at, inner:].astype(F32).T.astype(BF16)
            r.inc[chunk, 0:64, :] = nn(maps_t[0:64], (values * widen(tf, spread2)).astype(BF16))
            r.inc[chunk, 64:128, :] = nn(maps_t[128:192], (values * widen(tr, spread2)).astype(BF16))
            gone = jnp.exp(run[:, Q - 1 : Q])
            r.pexp[chunk, 0:1, :] = widen_col(gone[:HP], spread) * jnp.where((t0 <= b) & (b < t0 + Q), 0.0, 1.0)
            r.pexp[chunk, 1:2, :] = widen_col(gone[HP:], spread) * jnp.where((t0 < b) & (b <= t0 + Q), 0.0, 1.0)
        return 0

    lax.fori_loop(1, nblk, summarize, 0)

    @pl.when(me > 0)
    def _():
        halo_copy(me + 1).wait_recv()

    nh = normalize(r.halo[...])
    r.joined[0:16, :inner] = nn(nh, r.wv[...]).astype(BF16)
    r.joined[0:16, inner:] = nn(nh, r.ws[...]).astype(BF16)
    summarize(jnp.int32(0), 0)
    sumf, prodf = r.inc[0, 0:64, :], r.pexp[0, 0:1, :]
    sumr, prodr = r.inc[nchunk - 1, 64:128, :], r.pexp[nchunk - 1, 1:2, :]
    for c in range(1, nchunk):
        d = nchunk - 1 - c
        pf, pr = r.pexp[c, 0:1, :], r.pexp[d, 1:2, :]
        sumf, prodf = pf * sumf + r.inc[c, 0:64, :], prodf * pf
        sumr, prodr = pr * sumr + r.inc[d, 64:128, :], prodr * pr
    put_message(r.msgs.at[0], sumf, prodf * before_f)
    put_message(r.msgs.at[1], sumr, prodr * after_f)
    swap1.start()

    loads[3].wait()
    tri0, tri1 = iota((Q, Q), 0), iota((Q, Q), 1)
    lower, upper = tri0 > tri1, tri0 < tri1

    def within(blk, _):
        rows = part(blk, TB)
        r.gate[rows, :] = nn(r.buf[rows, :], r.wg[...])
        for q in range(per):
            chunk = blk * per + q
            at = part(chunk, Q)
            t0 = chunk * Q
            dt, ld, run, bef = chunk_parts(chunk)
            ldt = jnp.log(jnp.maximum(dt, 1e-37))
            rowf = ldt[:HP] - run[:HP]
            rowr = ldt[HP:] + bef[HP:]
            cols = jnp.concatenate([bef[:HP], -run[HP:]], axis=0).T
            scores = chunk_scores(r.act[at, inner:], t0, b)
            for j in range(inner // 128):
                lanes = slice(j * 128, (j + 1) * 128)
                weights = []
                for h in (2 * j, 2 * j + 1):
                    e = jnp.where(lower, cols[:, h : h + 1] + rowf[h : h + 1],
                                  cols[:, HP + h : HP + h + 1] + rowr[h : h + 1])
                    weights.append((jnp.exp(jnp.minimum(e, 60.0)) * scores).astype(BF16))
                vp = r.act[at, lanes]
                y = nn(jnp.concatenate(weights, axis=1), halves(vp))
                r.mixed[at, lanes] = y + skip[:, lanes] * vp.astype(F32)
        return 0

    lax.fori_loop(0, nblk, within, 0)
    loads[4].wait()
    loads[5].wait()
    swap1.finish()
    hf = chain(r.low1) * before_f
    hr = chain(r.high1) * after_f
    for c in range(nchunk):
        r.state[c, 0:64, :] = hf.astype(BF16)
        hf = r.pexp[c, 0:1, :] * hf + r.inc[c, 0:64, :]
        d = nchunk - 1 - c
        r.state[d, 64:128, :] = hr.astype(BF16)
        hr = r.pexp[d, 1:2, :] * hr + r.inc[d, 64:128, :]

    def enter(blk, _):
        lane = iota((Q, 128), 1)
        u_all = nt(r.cot[part(blk, TB), :], r.wo[...])
        r.dy[part(blk, TB), :] = u_all
        for q in range(per):
            chunk = blk * per + q
            at = part(chunk, Q)
            dt, ld, run, bef = chunk_parts(chunk)
            ef, er, _, _ = state_factors(dt, run, bef, chunk * Q, b)
            maps_here = r.act[at, inner:]
            state = r.state[chunk]
            ys = nn(maps_here[:, 64:128], state[0:64]) * widen(ef, spread2)
            ys = ys + nn(maps_here[:, 192:256], state[64:128]) * widen(er, spread2)
            square = jnp.zeros((Q, 1), F32)
            cross = jnp.zeros((Q, 1), F32)
            for j in range(inner // 128):
                lanes = slice(j * 128, (j + 1) * 128)
                y = r.mixed[at, lanes] + ys[:, lanes]
                r.mixed[at, lanes] = y
                gated = y * silu(r.gate[at, lanes])
                square = square + jnp.sum(gated * gated, axis=1, keepdims=True)
                cross = cross + jnp.sum(
                    gated * (u_all[q * Q : (q + 1) * Q, lanes] * ggain[:, lanes]), axis=1, keepdims=True)
            two = jnp.where(lane == 0, square, jnp.where(lane == 1, cross, 0.0))
            r.mine[blk, :, q * Q : (q + 1) * Q] = two.T[0:8]
        over(r.mine.at[blk], r.other.at[blk], r.sum_sem, blk).start()
        return 0

    lax.fori_loop(0, nblk, enter, 0)
    r.small[...] = jnp.zeros_like(r.small)

    def gating(blk, _):
        rows = part(blk, TB)
        over(r.mine.at[blk], r.other.at[blk], r.sum_sem, blk).wait()
        sums = r.mine[blk] + r.other[blk]
        sums = jnp.concatenate([sums, jnp.zeros((120, TB), F32)], axis=0).T
        scale = lax.rsqrt(sums[:, 0:1] / (2 * inner) + EPSILON)
        back = scale * scale * scale * sums[:, 1:2] / (2 * inner)
        for j in range(inner // 128):
            lanes = slice(j * 128, (j + 1) * 128)
            mixed = r.mixed[rows, lanes]
            pre = r.gate[rows, lanes]
            sig = jax.nn.sigmoid(pre)
            gated = mixed * (pre * sig)
            ng = gated * scale
            r.buf[rows, lanes] = (ng * ggain[:, lanes]).astype(BF16)
            g = r.dy[rows, lanes]
            r.small[0:1, lanes] += jnp.sum(g * ng, axis=0, keepdims=True)
            grad_gated = scale * (g * ggain[:, lanes]) - gated * back
            dy = grad_gated * (pre * sig)
            r.small[1:2, lanes] += jnp.sum(dy * r.act[rows, lanes].astype(F32), axis=0, keepdims=True)
            r.dy[rows, lanes] = dy
            r.ggate[rows, lanes] = (grad_gated * mixed * (sig * (1.0 + pre * (1.0 - sig)))).astype(BF16)
        for q in range(per):
            chunk = blk * per + q
            at = part(chunk, Q)
            dt, ld, run, bef = chunk_parts(chunk)
            ef, er, _, _ = state_factors(dt, run, bef, chunk * Q, b)
            maps_t = r.act[at, inner:].astype(F32).T.astype(BF16)
            dy = r.dy[at, :]
            r.inc[chunk, 0:64, :] = nn(maps_t[64:128], (dy * widen(ef, spread2)).astype(BF16))
            r.inc[chunk, 64:128, :] = nn(maps_t[192:256], (dy * widen(er, spread2)).astype(BF16))
        return 0

    lax.fori_loop(0, nblk, gating, 0)
    sumf, sumr = r.inc[nchunk - 1, 0:64, :], r.inc[0, 64:128, :]
    for c in range(1, nchunk):
        d = nchunk - 1 - c
        sumf = r.pexp[d, 0:1, :] * sumf + r.inc[d, 0:64, :]
        sumr = r.pexp[c, 1:2, :] * sumr + r.inc[c, 64:128, :]
    put_message(r.msgs.at[2], sumr * after_f, prodr * after_f)
    put_message(r.msgs.at[3], sumf * before_f, prodf * before_f)
    swap2.start()
    for g in range(width // 256):
        pieces[of[f"ggw{g}"]]["work"][...] = nn(r.normt[g * 256 : (g + 1) * 256, :], r.ggate[...]).astype(BF16)
        red.start(of[f"ggw{g}"])
    for g in range(groups):
        pieces[of[f"gow{g}"]]["work"][...] = tn(r.buf[:, g * 256 : (g + 1) * 256], r.cot[...]).astype(BF16)
        red.start(of[f"gow{g}"])

    def project_out(blk, _):
        rows = part(blk, TB)
        r.out_mine[rows, :] = nn(r.buf[rows, :], r.wo[...]).astype(BF16)
        over(r.out_mine.at[rows], r.out_other.at[rows], r.out_sem, blk).start()
        return 0

    lax.fori_loop(0, nblk, project_out, 0)

    sums_low = jnp.concatenate([lower, upper], axis=1).astype(BF16)
    diag = tri0 == tri1
    r.rowbuf[...] = jnp.zeros_like(r.rowbuf)

    taken_within = red.takes("within", nblk)

    def back_within(blk, _):
        for q in range(per):
            chunk = blk * per + q
            at = part(chunk, Q)
            t0 = chunk * Q
            dt, ld, run, bef = chunk_parts(chunk)
            ldt = jnp.log(jnp.maximum(dt, 1e-37))
            cols = jnp.concatenate([ldt[:HP] - run[:HP], ldt[HP:] + bef[HP:]], axis=0).T
            rowf, rowr = bef[:HP], -run[HP:]
            m = r.act[at, inner:]
            entf, readf, entr, readr = m[:, 0:64], m[:, 64:128], m[:, 128:192], m[:, 192:256]
            same = (tri0 + t0 < b) == (tri1 + t0 < b)
            okf, okr = upper & same, lower & same
            scores = jnp.where(okf, nt(entf, readf), jnp.where(okr, nt(entr, readr), 0.0))
            dscore = jnp.zeros((Q, Q), F32)
            for j in range(inner // 128):
                lanes = slice(j * 128, (j + 1) * 128)
                vp = r.act[at, lanes]
                dyp32 = r.dy[at, lanes]
                dyp = dyp32.astype(BF16)
                dw = nt(halves(vp), dyp)
                weights = []
                for i, h in enumerate((2 * j, 2 * j + 1)):
                    e = jnp.where(upper, cols[:, h : h + 1] + rowf[h : h + 1],
                                  cols[:, HP + h : HP + h + 1] + rowr[h : h + 1])
                    x = jnp.exp(jnp.minimum(e, 60.0))
                    weights.append((x * scores).astype(BF16))
                    dwx = dw[i * Q : (i + 1) * Q] * x
                    dscore = dscore + dwx
                    sums = nn((dwx * scores).astype(BF16), sums_low)
                    pf, pr = sums[:, :Q], sums[:, Q:]
                    for place, kept in enumerate((jnp.where(upper, pf, 0.0), jnp.where(lower, pr, 0.0),
                                                  jnp.where(diag, pf, 0.0), jnp.where(diag, pr, 0.0))):
                        r.rowbuf[chunk, place * HP + h : place * HP + h + 1, :] = jnp.sum(kept, axis=0, keepdims=True)
                dv = nn(jnp.concatenate(weights, axis=1), halves(dyp))
                r.mixed[at, lanes] = dv + dyp32 * skip[:, lanes]
            dsf = jnp.where(okf, dscore, 0.0)
            dsr = jnp.where(okr, dscore, 0.0)
            r.mixed[at, inner:] = jnp.concatenate(
                [nn(dsf.astype(BF16), readf), nn(dsf.T.astype(BF16), entf),
                 nn(dsr.astype(BF16), readr), nn(dsr.T.astype(BF16), entr)], axis=1)

        red.hook(blk, taken_within)
        return 0

    lax.fori_loop(0, nblk, back_within, 0)
    swap2.finish()
    df = chain(r.high2)
    dr = chain(r.low2)
    for c in range(nchunk):
        d = nchunk - 1 - c
        r.dstate[d, 0:64, :] = df.astype(BF16)
        df = r.pexp[d, 0:1, :] * df + r.inc[d, 0:64, :]
        r.dstate[c, 64:128, :] = dr.astype(BF16)
        dr = r.pexp[c, 1:2, :] * dr + r.inc[c, 64:128, :]
    r.cg_mine[...] = jnp.zeros_like(r.cg_mine)
    r.hsum[...] = jnp.zeros_like(r.hsum)

    def lent_copy(to):
        return pltpu.make_async_remote_copy(
            src_ref=r.lent_mine, dst_ref=r.lent_other, send_sem=r.edge.at[2], recv_sem=r.edge.at[3],
            device_id=(to, core), device_id_type=MESH)

    lower32, upper32 = lower.astype(F32), upper.astype(F32)

    taken_states = red.takes("states", nblk)

    def back_states(blk, _):
        for q in range(per):
            chunk = blk * per + q
            at = part(chunk, Q)
            dt, ld, run, bef = chunk_parts(chunk)
            ef, er, tf, tr = state_factors(dt, run, bef, chunk * Q, b)
            m = r.act[at, inner:]
            entf, readf, entr, readr = m[:, 0:64], m[:, 64:128], m[:, 128:192], m[:, 192:256]
            state = r.state[chunk]
            grad_state = r.dstate[chunk]
            dy = r.dy[at, :]
            values = r.act[at, :inner].astype(F32)
            dyf, dyr = dy * widen(ef, spread2), dy * widen(er, spread2)
            dreadf = nt(dyf.astype(BF16), state[0:64])
            dreadr = nt(dyr.astype(BF16), state[64:128])
            qf = nt(spread_low, (nn(readf, state[0:64]) * dyf).astype(BF16))
            qr = nt(spread_low, (nn(readr, state[64:128]) * dyr).astype(BF16))
            tfe, tre = widen(tf, spread2), widen(tr, spread2)
            dvf = nn(entf, grad_state[0:64]) * tfe
            dvr = nn(entr, grad_state[64:128]) * tre
            wf = nt(spread_low, (values * dvf).astype(BF16))
            wr = nt(spread_low, (values * dvr).astype(BF16))
            dentf = nt((values * tfe).astype(BF16), grad_state[0:64])
            dentr = nt((values * tre).astype(BF16), grad_state[64:128])
            through = state.astype(F32) * grad_state.astype(F32)
            zf = jnp.sum(through[0:64], axis=0, keepdims=True) * r.pexp[chunk, 0:1, :]
            zr = jnp.sum(through[64:128], axis=0, keepdims=True) * r.pexp[chunk, 1:2, :]
            zf = nt(spread, jnp.broadcast_to(zf, (8, inner)), HIGHEST)[:, 0:1]
            zr = nt(spread, jnp.broadcast_to(zr, (8, inner)), HIGHEST)[:, 0:1]
            r.mixed[at, :inner] = r.mixed[at, :inner] + dvf + dvr
            r.mixed[at, inner:] = r.mixed[at, inner:] + jnp.concatenate([dentf, dreadf, dentr, dreadr], axis=1)
            late = nn(jnp.concatenate([qf, wr], axis=0), lower32, HIGHEST)
            early = nn(jnp.concatenate([wf, qr], axis=0), upper32, HIGHEST)
            rowsum = r.rowbuf[chunk]
            dld = jnp.concatenate(
                [rowsum[0:HP] + late[:HP] + early[:HP] + zf, rowsum[HP : 2 * HP] + late[HP:] + early[HP:] + zr], axis=0)
            dldt = rowsum[2 * HP : 4 * HP] + jnp.concatenate([wf, wr], axis=0)
            sig = jax.nn.sigmoid(r.step[:, at] + bias)
            ratio = jnp.where(dt < 1e-30, 1.0, sig / jnp.maximum(dt, 1e-30))
            graw = dldt * ratio - jnp.exp(dlog) * sig * dld
            r.gstep[:, at] = graw.astype(BF16)
            r.hsum[:, 0:1] += jnp.sum(graw, axis=1, keepdims=True)
            r.hsum[:, 1:2] += jnp.sum(dld * ld, axis=1, keepdims=True)

        @pl.when(blk == 0)
        def _():
            tok8 = iota((8, 1), 0)
            tap = r.tap[...]
            dconv = r.mixed[0:8, :] * r.slope[0:16, :].astype(F32)[0:8]
            rows = r.joined[0:16, :].astype(F32)[8:16]
            lent = jnp.zeros((8, both), F32)
            for m in range(1, 4):
                first = jnp.concatenate([jnp.zeros((8, both), F32), dconv * conv_mask(tok8, m, b, off0)], axis=0)
                first = first[m : m + 8]
                lent = lent + first * tap[3 - m : 4 - m]
                r.cg_mine[3 - m : 4 - m, :] = jnp.sum(first * rows, axis=0, keepdims=True)
            r.lent_mine[...] = lent

            @pl.when(me > 0)
            def _():
                lent_copy(me - 1).start()

        red.hook(blk, taken_states)
        return 0

    lax.fori_loop(0, nblk, back_states, 0)

    @pl.when(me + 1 < count)
    def _():
        lent_copy(me - 1).wait_recv()

    @pl.when(me + 1 == count)
    def _():
        r.lent_other[...] = jnp.zeros_like(r.lent_other)

    def back_conv(g):
        cols = slice(g * 256, (g + 1) * 256)
        r.ext[...] = jnp.zeros_like(r.ext)

        def one(i, _):
            blk = nblk - 1 - i
            rows = part(blk, TB)
            tap = r.tap[:, cols]
            x = r.joined[pl.ds(pl.multiple_of(16 + blk * TB, 16), TB), cols].astype(F32)
            dconv = r.mixed[rows, cols] * r.slope[rows, cols].astype(F32)
            grad = dconv * tap[3:4]
            r.cg_mine[3:4, cols] += jnp.sum(dconv * x, axis=0, keepdims=True)
            for m in range(1, 4):
                r.ext[m - 1, TB : TB + 8, :] = r.ext[m - 1, 0:8, :]
                r.ext[m - 1, 0:TB, :] = dconv * valid_of(rows, m)
                moved = r.ext[m - 1, m : m + TB, :]
                r.cg_mine[3 - m : 4 - m, cols] += jnp.sum(moved * x, axis=0, keepdims=True)
                grad = grad + moved * tap[3 - m : 4 - m]
            last = jnp.where(blk == nblk - 1, 1.0, 0.0)
            grad = jnp.concatenate([grad[: TB - 8], grad[TB - 8 :] + r.lent_other[:, cols] * last], axis=0)
            if g * 256 < inner:
                r.buf[rows, cols] = grad.astype(BF16)
            else:
                r.gs_mine[rows, :] = grad.astype(BF16)
            return 0

        lax.fori_loop(0, nblk, one, 0)

    back_conv(inner // 256)
    gs_copy = over(r.gs_mine, r.gs_other, r.misc_sem, 0)
    gs_copy.start()
    cg_copy = over(r.cg_mine.at[:, pl.ds(inner, maps)], r.cg_other, r.misc_sem, 1)
    cg_copy.start()
    red.at("maps")

    def finish_maps():
        gs_copy.wait()
        cg_copy.wait()
        r.gs_mine[...] = (r.gs_mine[...].astype(F32) + r.gs_other[...].astype(F32)).astype(BF16)
        half = r.gs_mine[:, pl.ds(pl.multiple_of(core * 128, 128), 128)]
        r.gsw_w[:, 0:128] = nn(r.normt[...], half).astype(BF16)
        gstep = jnp.concatenate([r.gstep[...].astype(F32), jnp.zeros((128 - 2 * HP, length), F32)], axis=0)
        r.gsw_w[:, 128:256] = nt(r.normt[...], gstep.astype(BF16)).astype(BF16)
        red.start(of["gsw"])

    for g in range(groups):
        cols = slice(g * 256, (g + 1) * 256)
        back_conv(g)
        pieces[of[f"gv{g}"]]["work"][...] = nn(r.normt[...], r.buf[:, cols]).astype(BF16)
        red.start(of[f"gv{g}"])
        if g == 0:
            finish_maps()
        red.at("conv" + str(g))

    taken_down = red.takes("down", nblk)

    def down(blk, _):
        rows = part(blk, TB)
        gn = nt(r.ggate[rows, :], r.wg[...]) + nt(r.buf[rows, :], r.wv[...]) + tn(r.gstep[:, rows], r.wst[...])
        r.gn_mine[rows, :] = gn.astype(BF16)
        over(r.gn_mine.at[rows], r.gn_other.at[rows], r.gn_sem, blk).start()
        red.hook(blk, taken_down)
        return 0

    lax.fori_loop(0, nblk, down, 0)
    tiny = r.tiny_w.at[0]
    tiny[...] = jnp.zeros((8, both), F32)
    tiny[0:2, :inner] = r.small[0:2, :]
    head_sums = r.hsum[...].T
    tiny[3:4, 0 : 2 * HP] = head_sums[0:1]
    tiny[3:4, 128 : 128 + 2 * HP] = head_sums[1:2]
    tiny[4:8, :inner] = r.cg_mine[0:4, :inner]
    tiny[4:8, inner:] = r.cg_mine[0:4, inner:] + r.cg_other[0:4, :]

    def out_copy(blk):
        rows = part(blk, TB)
        return (pltpu.make_async_copy(r.out_other.at[rows], r.block_out.at[rows], r.store.at[0, blk]),
                pltpu.make_async_copy(r.gate.at[rows], r.grad_hidden.at[rows], r.store.at[1, blk]))

    taken_end = red.takes("end", nblk)

    def ending(blk, _):
        rows = part(blk, TB)
        over(r.out_mine.at[rows], r.out_other.at[rows], r.out_sem, blk).wait()
        over(r.gn_mine.at[rows], r.gn_other.at[rows], r.gn_sem, blk).wait()
        x = r.hid[rows, :].astype(F32)
        r.out_other[rows, :] = (
            x + (r.out_mine[rows, :].astype(F32) + r.out_other[rows, :].astype(F32))).astype(BF16)
        gn = r.gn_mine[rows, :].astype(F32) + r.gn_other[rows, :].astype(F32) + nt(r.gs_mine[rows, :], r.ws[...])
        scale = lax.rsqrt(jnp.mean(x * x, axis=1, keepdims=True) + EPSILON)
        tiny[2:3, :width] += jnp.sum(gn * x * scale, axis=0, keepdims=True)
        v = gn * gain
        mean = jnp.mean(x * v, axis=1, keepdims=True)
        r.gate[rows, :] = r.cot[rows, :].astype(F32) + scale * v - x * (scale * scale * scale * mean)
        for copy in out_copy(blk):
            copy.start()
        red.hook(blk, taken_end)
        return 0

    lax.fori_loop(0, nblk, ending, 0)

    def tiny_copy(s):
        return pltpu.make_async_remote_copy(
            src_ref=r.tiny_w.at[s], dst_ref=r.tiny_r.at[s], send_sem=r.tiny_sem.at[0, s],
            recv_sem=r.tiny_sem.at[1, s], device_id=(red.mates[s], core), device_id_type=MESH)

    halves_copy = over(r.gsw_o.at[:, pl.ds(0, 128)], r.gsx, r.misc_sem, 2)
    stores = []

    def store(src, dst):
        copy = pltpu.make_async_copy(src, dst, r.store.at[2, len(stores)])
        copy.start()
        stores.append(copy)

    def settle(p):
        red.finish(p)
        name, out = names[p], pieces[p]["out"]
        if name == "gsw":
            halves_copy.start()
            return
        kind, at = name[:-1], pl.ds(int(name[-1]) * 256, 256)
        store(out, r.ggw_any.at[at] if kind == "ggw" else r.gow_any.at[at] if kind == "gow" else r.gvw_any.at[:, at])

    for p in range(len(pieces)):
        if red.pos[p] == len(red.steps[p]):
            settle(p)
    tiny_copy(0).start()
    rest, turns = red.left(), 0
    for i, (p, at) in enumerate(rest):
        red.step(p, at)
        if at == len(red.steps[p]) - 1:
            settle(p)
        while turns < bits and (turns + 1) * len(rest) <= (i + 1) * (bits + 1) or i + 1 == len(rest) and turns < bits:
            tiny_copy(turns).wait()
            r.tiny_w[turns + 1] = r.tiny_w[turns] + r.tiny_r[turns]
            turns += 1
            if turns < bits:
                tiny_copy(turns).start()
    store(r.tiny_w.at[bits], r.tiny_any)
    halves_copy.wait()
    mine_at, other_at = pl.multiple_of(core * 128, 128), pl.multiple_of((1 - core) * 128, 128)
    store(r.gsw_o.at[:, pl.ds(0, 128)], r.gsw_any.at[:, pl.ds(mine_at, 128)])
    store(r.gsx, r.gsw_any.at[:, pl.ds(other_at, 128)])
    store(r.gsw_o.at[:, pl.ds(128, 128)], r.gsw_any.at[:, pl.ds(256, 128)])
    for copy in stores:
        copy.wait()
    for blk in range(nblk):
        for copy in out_copy(blk):
            copy.wait()

    @pl.when(me + 1 < count)
    def _():
        halo_copy(me + 1).wait_send()

    @pl.when(me > 0)
    def _():
        lent_copy(me - 1).wait_send()


TABLE_BITS = 4
ORDERS = (
    (1, 0, 3, 2),
    (0, 1, 3, 2),
    (0, 2, 1, 3),
    (2, 3, 1, 0),
    (1, 0, 2, 3),
    (1, 2, 0, 3),
    (0, 1, 2, 3),
    (2, 1, 0, 3),
    (1, 2, 0, 3),
    (0, 1, 3, 2),
)
TABLE = {
    "within1": (
        (3, 0),
    ),
    "within2": (
        (0, 0), (1, 0), (2, 0),
    ),
    "within3": (
        (4, 0), (5, 0),
    ),
    "states0": (
        (0, 1), (1, 1), (2, 1), (3, 1),
    ),
    "states1": (
        (4, 1), (5, 1),
    ),
    "states2": (
        (2, 2), (3, 2),
    ),
    "states3": (
        (0, 2), (1, 2), (4, 2), (5, 2),
    ),
    "maps": (
        (2, 3), (3, 3),
    ),
    "conv0": (
        (0, 3), (1, 3), (4, 3), (5, 3),
    ),
    "conv1": (
        (2, 4), (3, 4),
    ),
    "conv2": (
        (0, 4), (1, 4), (4, 4), (5, 4),
    ),
    "down0": (
        (2, 5), (3, 5), (6, 0),
    ),
    "down1": (
        (5, 5),
    ),
    "down2": (
        (4, 5), (7, 0), (8, 0),
    ),
    "down3": (
        (0, 5), (1, 5), (6, 1), (9, 0),
    ),
    "end2": (
        (2, 6), (3, 6), (4, 6), (7, 1),
    ),
    "end3": (
        (0, 6),
    ),
    "tail": (
        (5, 6), (6, 2), (8, 1), (1, 6), (9, 1), (6, 3), (7, 2), (9, 2), (8, 2), (6, 4), (7, 3), (3, 7),
        (9, 3), (8, 3), (2, 7), (7, 4), (1, 7), (6, 5), (4, 7), (9, 4), (8, 4), (7, 5), (0, 7), (5, 7),
        (8, 5), (9, 5), (6, 6), (7, 6), (8, 6), (9, 6), (6, 7), (7, 7), (8, 7), (9, 7),
    ),
}


def last_kernel(heads, ggw_ref, gow_ref, gvw_ref, gsw_ref, tiny_ref,
                ngain_ref, ggwo_ref, gvwo_ref, gswo_ref, gsteo_ref, convv_ref, convs_ref, bias_ref, decay_ref,
                skip_ref, ggain_ref, gowo_ref):
    ggwo_ref[...] = ggw_ref[...].astype(F32)
    gvwo_ref[...] = gvw_ref[...].astype(F32)
    maps = gswo_ref.shape[1]
    gswo_ref[...] = gsw_ref[:, :maps].astype(F32)
    step = gsw_ref[:, maps:].astype(F32).T
    gsteo_ref[...] = jnp.stack([step[:heads], step[HP : HP + heads]], axis=1)
    gowo_ref[...] = gow_ref[...].astype(F32)

    @pl.when(pl.program_id(0) == 0)
    def _():
        width, inner = ngain_ref.shape[0], convv_ref.shape[1]
        ngain_ref[...] = tiny_ref[2, :width]
        ggain_ref[...] = tiny_ref[0, :inner]
        convv_ref[...] = tiny_ref[4:8, :inner]
        convs_ref[...] = tiny_ref[4:8, inner:]
        bias_ref[...] = jnp.concatenate([tiny_ref[3:4, 0:heads], tiny_ref[3:4, HP : HP + heads]], axis=0)
        decay_ref[...] = (tiny_ref[3:4, 128 : 128 + heads] + tiny_ref[3:4, 128 + HP : 128 + HP + heads]).reshape(heads)
        spread = spread_matrix(inner, inner // heads)
        total = nt(jnp.broadcast_to(tiny_ref[1:2, :inner], (8, inner)), spread, HIGHEST)
        skip_ref[...] = total[0:1, :heads].reshape(heads)


SMEM_SPEC = pl.BlockSpec(memory_space=pltpu.SMEM)
VMEM_SPEC = pl.BlockSpec(memory_space=pltpu.VMEM)
ANY_SPEC = pl.BlockSpec(memory_space=pl.ANY)


def body(
    hidden_in, norm_gain, gate_proj, value_proj, state_proj, step_proj, conv_value, conv_state,
    step_bias, decay_log, skip_scale, gate_gain, out_proj, lengths, cotangent,
):
    length, width = hidden_in.shape
    inner = gate_proj.shape[1]
    heads = decay_log.shape[0]
    maps = state_proj.shape[1]
    both = inner + maps
    nblk, nchunk = length // TB, length // Q
    count = lax.axis_size("seq")
    bits = count.bit_length() - 1
    assert count == 1 << bits
    reach = min(1 + (LEN_MOST - 2) // length, count - 1)
    npieces = len(piece_names(width, inner))

    def vmem(*dims, dtype=F32):
        return pltpu.VMEM(dims, dtype)

    dma = pltpu.SemaphoreType.DMA
    low = dict(dtype=BF16)
    scratch = dict(
        hid=vmem(length, width, **low), wg=vmem(width, inner, **low), wv=vmem(width, inner, **low),
        ws=vmem(width, maps, **low), wo=vmem(inner, width, **low), cot=vmem(length, width, **low),
        wst=vmem(2 * HP, width, **low), tap=vmem(4, both),
        normt=vmem(width, length, **low), buf=vmem(length, inner, **low), gate=vmem(length, inner),
        joined=vmem(16 + length, both, **low), act=vmem(length, both, **low), step=vmem(2 * HP, length),
        inc=vmem(nchunk, 128, inner), pexp=vmem(nchunk, 2, inner), mixed=vmem(length, both),
        state=vmem(nchunk, 128, inner, **low), dstate=vmem(nchunk, 128, inner, **low),
        dy=vmem(length, inner), ggate=vmem(length, inner, **low), gstep=vmem(2 * HP, length, **low),
        msgs=vmem(4, 80, inner, **low),
        low1=vmem(reach, 80, inner, **low), high1=vmem(reach, 80, inner, **low),
        low2=vmem(reach, 80, inner, **low), high2=vmem(reach, 80, inner, **low),
        rowbuf=vmem(nchunk, 4 * HP, Q), jx=vmem(TB + 16, 256), ext=vmem(3, TB + 8, 256),
        valid=vmem(3, length, 128, **low), slope=vmem(length, both, **low), gsx=vmem(width, 128, **low),
        halo=vmem(16, width, **low), mine=vmem(nblk, 8, TB), other=vmem(nblk, 8, TB),
        out_mine=vmem(length, width, **low), out_other=vmem(length, width, **low),
        gn_mine=vmem(length, width, **low), gn_other=vmem(length, width, **low),
        gs_mine=vmem(length, maps, **low), gs_other=vmem(length, maps, **low),
        lent_mine=vmem(8, both), lent_other=vmem(8, both), cg_mine=vmem(8, both), cg_other=vmem(8, maps),
        hsum=vmem(2 * HP, 128), small=vmem(8, inner),
        tiny_w=vmem(bits + 1, 8, both), tiny_r=vmem(bits, 8, both),
    )
    for name in piece_names(width, inner):
        rows, cols = (256, width) if name[:3] in ("ggw", "gow") else (width, 256)
        scratch[name + "_w"] = vmem(rows, cols, **low)
        scratch[name + "_k"] = vmem(rows // 2, cols, **low)
        scratch[name + "_r"] = vmem(received_rows(rows, bits), cols, **low)
        scratch[name + "_o"] = vmem(rows, cols, **low)
    scratch.update(
        load=dma((6,)), store=dma((3, npieces + nblk)), edge=dma((4,)), sum_sem=dma((2, nblk)), out_sem=dma((2, nblk)),
        gn_sem=dma((2, nblk)), misc_sem=dma((2, 3)), tiny_sem=dma((2, bits)),
        up_s=dma((2, reach)), up_r=dma((2, reach)), dn_s=dma((2, reach)), dn_r=dma((2, reach)),
        rs_s=dma((npieces, bits)), rs_r=dma((npieces, bits)), ag_s=dma((npieces, bits)), ag_r=dma((npieces, bits)),
    )

    def shape(*dims, dtype=F32):
        return jax.ShapeDtypeStruct(dims, dtype)

    outs = pl.pallas_call(
        partial(layer_kernel, reach, bits, NAMES_IN + NAMES_OUT + tuple(scratch)),
        in_specs=[SMEM_SPEC] + [ANY_SPEC] * 6 + [VMEM_SPEC] * 8,
        out_specs=[ANY_SPEC] * 7,
        out_shape=[shape(length, width, **low), shape(length, width), shape(width, inner, **low),
                   shape(inner, width, **low), shape(width, inner, **low), shape(width, maps + 128, **low),
                   shape(8, both)],
        scratch_shapes=list(scratch.values()),
        compiler_params=pltpu.CompilerParams(
            collective_id=1, has_side_effects=True, vmem_limit_bytes=VMEM_LIMIT),
    )(lengths, hidden_in, gate_proj, value_proj, state_proj, out_proj, cotangent,
      norm_gain, step_proj.transpose(2, 0, 1), conv_value, conv_state, step_bias, decay_log, skip_scale, gate_gain)
    block_out, grad_hidden, ggw, gow, gvw, gsw, tiny = outs

    rows = 128
    def tall(cols):
        return pl.BlockSpec((rows, cols), lambda i: (i, 0))

    def whole(*dims):
        return pl.BlockSpec(dims, lambda i: (0,) * len(dims))

    assert width % rows == 0 and inner % rows == 0 and inner == width
    final = pl.pallas_call(
        partial(last_kernel, heads),
        grid=(width // rows,),
        in_specs=[tall(inner), tall(width), tall(inner), tall(maps + 128), whole(8, both)],
        out_specs=[whole(width), tall(inner), tall(inner), tall(maps), pl.BlockSpec((heads, 2, rows), lambda i: (0, 0, i)), whole(4, inner),
                   whole(4, maps), whole(2, heads), whole(heads), whole(heads), whole(inner), tall(width)],
        out_shape=[shape(width), shape(width, inner), shape(width, inner), shape(width, maps),
                   shape(heads, 2, width), shape(4, inner), shape(4, maps), shape(2, heads), shape(heads),
                   shape(heads), shape(inner), shape(inner, width)],
        compiler_params=pltpu.CompilerParams(dimension_semantics=("arbitrary",), vmem_limit_bytes=60 * MIB),
    )(ggw, gow, gvw, gsw, tiny)
    ngain, ggw, gvw, gsw, gstepw, convv, convs, bias, decay, skip, ggain, gow = final
    return (block_out, grad_hidden, ngain, ggw, gvw, gsw, gstepw.transpose(1, 2, 0), convv, convs, bias, decay, skip,
            ggain, gow)


def solution(mesh):
    in_specs = (
        P("seq", None),
        P(),
        P(None, "head"),
        P(None, "head"),
        P(),
        P(None, None, "head"),
        P(None, "head"),
        P(),
        P(None, "head"),
        P("head"),
        P("head"),
        P("head"),
        P("head", None),
        P(),
        P("seq", None),
    )
    out_specs = (
        P("seq", None),
        P("seq", None),
        P(),
        P(None, "head"),
        P(None, "head"),
        P(),
        P(None, None, "head"),
        P(None, "head"),
        P(),
        P(None, "head"),
        P("head"),
        P("head"),
        P("head"),
        P("head", None),
    )
    return jax.shard_map(body, mesh=mesh, in_specs=in_specs, out_specs=out_specs, check_vma=False)
```

```python
from functools import partial

import jax
import jax.numpy as jnp
from jax import lax
from jax.experimental import pallas as pl
from jax.experimental.pallas import tpu as pltpu
from jax.sharding import PartitionSpec as P

EPSILON = 1e-05
LEN_MOST = 4096
Q = 128
TB = 256
HP = 16
MIB = 1024 * 1024
VMEM_LIMIT = 63 * MIB + MIB // 2
HIGHEST = lax.Precision.HIGHEST
F32 = jnp.float32
BF16 = jnp.bfloat16
MESH = pl.DeviceIdType.MESH


def nn(a, b, precision=None):
    return jnp.dot(a, b, preferred_element_type=F32, precision=precision)


def nt(a, b, precision=None):
    return lax.dot_general(a, b, (((1,), (1,)), ((), ())), preferred_element_type=F32, precision=precision)


def tn(a, b, precision=None):
    return lax.dot_general(a, b, (((0,), (0,)), ((), ())), preferred_element_type=F32, precision=precision)


def iota(shape, axis):
    return lax.broadcasted_iota(jnp.int32, shape, axis)


def spread_matrix(width, hdim):
    return (iota((HP, width), 1) // hdim == iota((HP, width), 0)).astype(F32)


def split(x):
    hi = x.astype(BF16)
    return hi, (x - hi.astype(F32)).astype(BF16)


def thirds(x):
    hi = x.astype(BF16)
    rest = x - hi.astype(F32)
    mid = rest.astype(BF16)
    return jnp.concatenate([hi, mid, (rest - mid.astype(F32)).astype(BF16)], axis=0)


def exact(product, rows):
    return product[:rows] + product[rows : 2 * rows] + product[2 * rows :]


def widen(spread2, *factors):
    stacks = []
    for rows in factors:
        hi, lo = split(rows.T)
        stacks.append(jnp.concatenate([hi, lo], axis=1))
    wide = nn(jnp.concatenate(stacks, axis=0), spread2)
    return [wide[i * Q : (i + 1) * Q] for i in range(len(factors))]


def widen_cols(spread_low, *cols):
    rows = jnp.concatenate([*cols, jnp.zeros((HP, 128 - len(cols)), F32)], axis=1).T[0:8]
    wide = exact(nn(thirds(rows), spread_low), 8)
    return [wide[i : i + 1] for i in range(len(cols))]


def silu(x):
    return x * jax.nn.sigmoid(x)


def softplus(x):
    return jnp.maximum(x, 0.0) + jnp.log1p(jnp.exp(-jnp.abs(x)))


def state_factors(dt, run, bef, t0, b):
    t1 = t0 + Q
    tok = iota((1, Q), 1) + t0
    ef = jnp.where((tok < b) | (t0 > b), jnp.exp(bef[:HP]), 0.0)
    er = jnp.where((tok >= b) | (t1 < b), jnp.exp(run[HP:, Q - 1 : Q] - run[HP:]), 0.0)
    tf = jnp.where((tok >= b) | (t1 <= b), jnp.exp(run[:HP, Q - 1 : Q] - run[:HP]), 0.0) * dt[:HP]
    tr = jnp.where((tok < b) | (t0 >= b), jnp.exp(bef[HP:]), 0.0) * dt[HP:]
    return ef, er, tf, tr


def conv_mask(tok, shift, b, off0):
    lost = ((tok < b) & (tok + off0 < shift)) | ((tok >= b) & (tok < b + shift))
    return jnp.where(lost, 0.0, 1.0)


def put_message(ref, state, passed):
    hi, lo = split(passed)
    ref[0:64, :] = state.astype(BF16)
    row = iota((16, state.shape[1]), 0)
    tail = jnp.where(row == 0, hi.astype(F32), jnp.where(row == 1, lo.astype(F32), 0.0))
    ref[64:80, :] = tail.astype(BF16)


def chain(ref):
    total = ref[0, 0:64, :].astype(F32)
    passed = None
    for k in range(1, ref.shape[0]):
        tail = ref[k - 1, 64:80, :].astype(F32)
        here = tail[0:1] + tail[1:2]
        passed = here if passed is None else passed * here
        total = total + passed * ref[k, 0:64, :].astype(F32)
    return total


class Swap:
    def __init__(self, reach, up_ref, down_ref, from_low, from_high, up_send, up_recv, down_send, down_recv):
        self.me, self.core, self.count = lax.axis_index("seq"), lax.axis_index("head"), lax.axis_size("seq")
        self.reach, self.up_ref, self.down_ref, self.from_low, self.from_high = reach, up_ref, down_ref, from_low, from_high
        self.sems = up_send, up_recv, down_send, down_recv

    def up(self, k):
        return pltpu.make_async_remote_copy(
            src_ref=self.up_ref, dst_ref=self.from_low.at[k - 1], send_sem=self.sems[0].at[k - 1],
            recv_sem=self.sems[1].at[k - 1], device_id=(self.me + k, self.core), device_id_type=MESH)

    def down(self, k):
        return pltpu.make_async_remote_copy(
            src_ref=self.down_ref, dst_ref=self.from_high.at[k - 1], send_sem=self.sems[2].at[k - 1],
            recv_sem=self.sems[3].at[k - 1], device_id=(self.me - k, self.core), device_id_type=MESH)

    def greet(self, barrier):
        me, core, count = self.me, self.core, self.count
        for k in range(1, self.reach + 1):
            @pl.when(me + k < count)
            def _():
                pl.semaphore_signal(barrier, inc=1, device_id=(me + k, core), device_id_type=MESH)

            @pl.when(me >= k)
            def _():
                pl.semaphore_signal(barrier, inc=1, device_id=(me - k, core), device_id_type=MESH)
        return jnp.minimum(me, self.reach) + jnp.minimum(count - 1 - me, self.reach)

    def start(self):
        me, count = self.me, self.count
        for k in range(1, self.reach + 1):
            @pl.when(me + k < count)
            def _():
                self.up(k).start()

            @pl.when(me >= k)
            def _():
                self.down(k).start()

            @pl.when(me < k)
            def _():
                self.from_low[k - 1] = jnp.zeros_like(self.from_low[k - 1])

            @pl.when(me + k >= count)
            def _():
                self.from_high[k - 1] = jnp.zeros_like(self.from_high[k - 1])

    def finish(self):
        me, count = self.me, self.count
        for k in range(1, self.reach + 1):
            @pl.when(me + k < count)
            def _():
                self.up(k).wait_send()
                self.down(k).wait_recv()

            @pl.when(me >= k)
            def _():
                self.down(k).wait_send()
                self.up(k).wait_recv()


def chunk_scores(maps, t0, b):
    tr, tc = iota((Q, Q), 0), iota((Q, Q), 1)
    same = (tr + t0 < b) == (tc + t0 < b)
    fwd = nt(maps[:, 64:128], maps[:, 0:64])
    rev = nt(maps[:, 192:256], maps[:, 128:192])
    return jnp.where((tr > tc) & same, fwd, jnp.where((tr < tc) & same, rev, 0.0))


def halves(x):
    left = iota(x.shape, 1) < 64
    zero = jnp.zeros_like(x)
    return jnp.concatenate([jnp.where(left, x, zero), jnp.where(left, zero, x)], axis=0)


class Reduce:
    def __init__(self, bits, pieces, rs_send, rs_recv, ag_send, ag_recv):
        me, core = lax.axis_index("seq"), lax.axis_index("head")
        bit = [lax.rem(me // (1 << k), 2) for k in range(bits)]
        mate = [me + (1 - 2 * bit[k]) * (1 << k) for k in range(bits)]
        self.mates = list(mate)
        self.bits, self.bit, self.mate, self.core, self.pieces = bits, bit, mate, core, pieces
        self.sems = rs_send, rs_recv, ag_send, ag_recv
        self.pos = [0] * len(pieces)
        self.steps = []
        for piece in pieces:
            halvings = halvings_of(piece["work"].shape[0], bits)
            self.steps.append([("rs", s) for s in range(bits)] + [("ag", s) for s in reversed(range(halvings))])

    def geometry(self, p, s):
        rows = self.pieces[p]["work"].shape[0]
        halvings = halvings_of(rows, self.bits)
        off, slot = jnp.int32(0), 0
        for t in range(s):
            if t < halvings:
                rows = rows // 2
                off = off + self.bit[self.pieces[p]["order"][t]] * rows
            slot += rows
        return off, rows, slot, s < halvings

    def remote(self, src, dst, send, recv, k):
        return pltpu.make_async_remote_copy(
            src_ref=src, dst_ref=dst, send_sem=send, recv_sem=recv, device_id=(self.mate[k], self.core),
            device_id_type=MESH)

    def first(self, p):
        return self.bit[self.pieces[p]["order"][0]] * (self.pieces[p]["work"].shape[0] // 2)

    def copy(self, p, step):
        kind, s = step
        piece = self.pieces[p]
        k = piece["order"][s]
        if kind == "rs":
            off, rows, slot, halved = self.geometry(p, s)
            source, off = (piece["work"], off) if s == 0 else (piece["kept"], off - self.first(p))
            if halved:
                rows = rows // 2
                off = off + (1 - self.bit[k]) * rows
            return self.remote(
                source.at[pl.ds(pl.multiple_of(off, 16), rows)], piece["recv"].at[pl.ds(slot, rows)],
                self.sems[0].at[p, s], self.sems[1].at[p, s], k)
        off, rows, _, _ = self.geometry(p, s + 1)
        where = piece["out"].at[pl.ds(pl.multiple_of(off, 16), rows)]
        return self.remote(where, where, self.sems[2].at[p, s], self.sems[3].at[p, s], k)

    def arriving(self, p, s):
        off, rows, _, _ = self.geometry(p, s + 1)
        k = self.pieces[p]["order"][s]
        off = off + (1 - 2 * self.bit[k]) * rows
        where = self.pieces[p]["out"].at[pl.ds(pl.multiple_of(off, 16), rows)]
        return self.remote(where, where, self.sems[2].at[p, s], self.sems[3].at[p, s], k)

    def start(self, p):
        self.copy(p, self.steps[p][0]).start()

    def step(self, p, at):
        kind, s = self.steps[p][at]
        if kind == "rs":
            self.add(p, s, self.copy(p, (kind, s)))
        else:
            self.arriving(p, s).wait_recv()
        if at + 1 < len(self.steps[p]):
            self.copy(p, self.steps[p][at + 1]).start()

    def take(self, name):
        if self.bits != TABLE_BITS:
            return []
        taken = TABLE.get(name, ())
        for p, at in taken:
            assert self.pos[p] == at
            self.pos[p] = at + 1
        return taken

    def at(self, name):
        for p, at in self.take(name):
            self.step(p, at)

    def takes(self, name, count):
        return {k: self.take(name + str(k)) for k in range(count)}

    def hook(self, turn, taken):
        for k, steps in taken.items():
            if steps:
                @pl.when(turn == k)
                def _():
                    for p, at in steps:
                        self.step(p, at)

    def left(self):
        order = list(TABLE["tail"]) if self.bits == TABLE_BITS else []
        rest = [(p, at) for p in range(len(self.pieces)) for at in range(self.pos[p], len(self.steps[p]))]
        return order + sorted((x for x in rest if x not in order), key=lambda x: x[::-1])

    def add(self, p, s, copy):
        piece = self.pieces[p]
        off, rows, slot, halved = self.geometry(p, s)
        if halved:
            copy.wait_recv()
            rows = rows // 2
            off = off + self.bit[piece["order"][s]] * rows
        else:
            copy.wait()
        recv, rel = piece["recv"], off - self.first(p)
        source, at = (piece["work"], off) if s == 0 else (piece["kept"], rel)
        dest, to = (piece["out"], off) if s == self.bits - 1 else (piece["kept"], rel)
        size = next(n for n in (64, 48, 32, 16) if rows % n == 0)

        def one(i, _):
            total = source[pl.ds(pl.multiple_of(at + i * size, 16), size), :].astype(F32)
            total = total + recv[pl.ds(pl.multiple_of(slot + i * size, 16), size), :].astype(F32)
            dest[pl.ds(pl.multiple_of(to + i * size, 16), size), :] = total.astype(BF16)
            return 0

        lax.fori_loop(0, rows // size, one, 0)

    def finish(self, p):
        for kind, s in self.steps[p]:
            if kind == "ag" or self.geometry(p, s)[3]:
                self.copy(p, (kind, s)).wait_send()


def halvings_of(rows, bits):
    made = 0
    while made < bits and (rows >> made) % 32 == 0:
        made += 1
    return made


def piece_names(width, inner):
    return ([f"ggw{g}" for g in range(width // 256)] + [f"gow{g}" for g in range(inner // 256)]
            + [f"gv{g}" for g in range(inner // 256)] + ["gsw"])


def received_rows(rows, bits):
    halvings, total = halvings_of(rows, bits), 0
    for s in range(bits):
        rows = rows // 2 if s < halvings else rows
        total += rows
    return total


def part(i, size):
    return pl.ds(pl.multiple_of(i * size, size), size)


class Refs:
    pass


NAMES_IN = ("lengths", "hid_any", "wg_any", "wv_any", "ws_any", "wo_any", "cot_any",
            "gain", "wstep", "tapv", "taps", "bias", "dlog", "skip", "ggain")
NAMES_OUT = ("block_out", "grad_hidden", "ggw_any", "gow_any", "gvw_any", "gsw_any", "tiny_any")


def layer_kernel(reach, bits, names, *refs):
    r = Refs()
    for name, ref in zip(names, refs):
        setattr(r, name, ref)
    length, width = r.hid.shape
    inner = r.wo.shape[0]
    maps = r.ws.shape[1]
    both = inner + maps
    heads = r.dlog.shape[0]
    nblk, nchunk, per = length // TB, length // Q, TB // Q
    me, core, count = lax.axis_index("seq"), lax.axis_index("head"), lax.axis_size("seq")
    base = me * length

    loads = [pltpu.make_async_copy(src, dst, r.load.at[i]) for i, (src, dst) in enumerate(
        ((r.hid_any, r.hid), (r.wv_any, r.wv), (r.ws_any, r.ws), (r.wg_any, r.wg), (r.wo_any, r.wo),
         (r.cot_any, r.cot)))]
    for load in loads:
        load.start()

    swap1 = Swap(reach, r.msgs.at[0], r.msgs.at[1], r.low1, r.high1, r.up_s.at[0], r.up_r.at[0], r.dn_s.at[0], r.dn_r.at[0])
    swap2 = Swap(reach, r.msgs.at[2], r.msgs.at[3], r.low2, r.high2, r.up_s.at[1], r.up_r.at[1], r.dn_s.at[1], r.dn_r.at[1])
    groups = inner // 256
    names = piece_names(width, inner)
    orders = [ORDERS[i % len(ORDERS)] if bits == TABLE_BITS else tuple(range(bits)) for i in range(len(names))]
    pieces = [
        dict(work=getattr(r, name + "_w"), kept=getattr(r, name + "_k"), recv=getattr(r, name + "_r"),
             out=getattr(r, name + "_o"), order=order)
        for name, order in zip(names, orders)
    ]
    of = {name: i for i, name in enumerate(names)}
    red = Reduce(bits, pieces, r.rs_s, r.rs_r, r.ag_s, r.ag_r)
    barrier = pltpu.get_barrier_semaphore()
    near = swap1.greet(barrier)
    for mate in red.mates:
        pl.semaphore_signal(barrier, inc=1, device_id=(mate, core), device_id_type=MESH)
    pl.semaphore_signal(barrier, inc=1, device_id=(me, 1 - core), device_id_type=MESH)

    def over(src, dst, sems, k):
        return pltpu.make_async_remote_copy(
            src_ref=src, dst_ref=dst, send_sem=sems.at[0, k], recv_sem=sems.at[1, k], device_id=(me, 1 - core),
            device_id_type=MESH)

    def one_sequence(j, carry):
        start, b, off0, after = carry
        end = start + r.lengths[j]
        b = jnp.where((start > base) & (start < base + length), start - base, b)
        off0 = jnp.where((start <= base) & (base < end), base - start, off0)
        after = jnp.where(end == base + length, 0, after)
        return end, b, off0, after

    _, b, off0, after = lax.fori_loop(
        0, r.lengths.shape[0], one_sequence, (jnp.int32(0), jnp.int32(length + 1), jnp.int32(0), jnp.int32(1)))
    before_f = jnp.where(off0 > 0, 1.0, 0.0)
    after_f = after.astype(F32)

    def lanes128(x):
        return jnp.concatenate([x, jnp.zeros((x.shape[0], 128 - x.shape[1]), F32)], axis=1)

    small_cols = jnp.concatenate(
        [lanes128(r.bias[...]), lanes128(r.dlog[...].reshape(1, heads)), lanes128(r.skip[...].reshape(1, heads)),
         jnp.zeros((4, 128), F32)], axis=0).T
    bias = jnp.concatenate([small_cols[:HP, 0:1], small_cols[:HP, 1:2]], axis=0)
    dlog = jnp.concatenate([small_cols[:HP, 2:3], small_cols[:HP, 2:3]], axis=0)
    spread = spread_matrix(inner, inner // heads)
    spread_low = spread.astype(BF16)
    spread2 = jnp.concatenate([spread_low, spread_low], axis=0)
    (skip,) = widen_cols(spread_low, small_cols[:HP, 3:4])
    gain = r.gain[...].reshape(1, width)
    ggain = r.ggain[...].reshape(1, inner)
    r.wst[...] = jnp.zeros_like(r.wst)
    wstep = r.wstep[...].astype(F32)
    for k in range(2):
        r.wst[k * HP : (k + 1) * HP, :] = jnp.concatenate(
            [wstep[:, k, :], jnp.zeros((HP - heads, width), F32)], axis=0).astype(BF16)

    r.tap[:, :inner] = r.tapv[...]
    r.tap[:, inner:] = r.taps[...]
    for blk in range(nblk):
        tok = iota((TB, 128), 0) + blk * TB
        for m in range(1, 4):
            r.valid[m - 1, blk * TB : (blk + 1) * TB, :] = conv_mask(tok, m, b, off0).astype(BF16)

    loads[0].wait()
    loads[1].wait()
    loads[2].wait()

    def normalize(x):
        x = x.astype(F32)
        scale = lax.rsqrt(jnp.mean(x * x, axis=1, keepdims=True) + EPSILON)
        return (x * scale * gain).astype(BF16)

    upto = (iota((Q, Q), 0) <= iota((Q, Q), 1)).astype(BF16)

    def project(blk, _):
        rows = part(blk, TB)
        normed = normalize(r.hid[rows, :])
        r.buf[rows, :] = normed
        r.normt[:, rows] = normed.T
        dest = pl.ds(pl.multiple_of(16 + blk * TB, 16), TB)
        r.joined[dest, :inner] = nn(normed, r.wv[...]).astype(BF16)
        r.joined[dest, inner:] = nn(normed, r.ws[...]).astype(BF16)
        step = nt(r.wst[...], normed)
        dt = softplus(step + bias)
        ld = -jnp.exp(dlog) * dt
        r.step[:, rows] = step
        r.dt[:, rows] = dt
        for q in range(per):
            run = exact(nn(thirds(ld[:, q * Q : (q + 1) * Q]), upto), 2 * HP)
            r.run[:, pl.ds(pl.multiple_of(blk * TB + q * Q, Q), Q)] = run
        return 0

    lax.fori_loop(0, nblk, project, 0)

    pl.semaphore_wait(barrier, near + bits + 1)

    def halo_copy(to):
        return pltpu.make_async_remote_copy(
            src_ref=r.hid.at[pl.ds(length - 16, 16)], dst_ref=r.halo, send_sem=r.edge.at[0], recv_sem=r.edge.at[1],
            device_id=(to, core), device_id_type=MESH)

    @pl.when(me + 1 < count)
    def _():
        halo_copy(me + 1).start()

    @pl.when(me == 0)
    def _():
        r.halo[...] = jnp.zeros_like(r.halo)

    def valid_of(rows, m):
        one = r.valid[m - 1, rows, :].astype(F32)
        return jnp.concatenate([one, one], axis=1)

    def chunk_parts(chunk):
        cols = part(chunk, Q)
        dt, run = r.dt[:, cols], r.run[:, cols]
        ld = -jnp.exp(dlog) * dt
        return dt, ld, run, run - ld

    def summarize(blk, _):
        rows = part(blk, TB)
        for g in range(both // 256):
            cols = slice(g * 256, (g + 1) * 256)
            r.jx[...] = r.joined[pl.ds(pl.multiple_of(blk * TB, 16), TB + 16), cols].astype(F32)
            tap = r.tap[:, cols]
            total = r.jx[16 : 16 + TB, :] * tap[3:4]
            for m in range(1, 4):
                total = total + r.jx[16 - m : 16 - m + TB, :] * valid_of(rows, m) * tap[3 - m : 4 - m]
            sig = jax.nn.sigmoid(total)
            r.act[rows, cols] = (total * sig).astype(BF16)
            r.slope[rows, cols] = (sig * (1.0 + total * (1.0 - sig))).astype(BF16)
        for q in range(per):
            chunk = blk * per + q
            t0 = chunk * Q
            at = part(chunk, Q)
            dt, ld, run, bef = chunk_parts(chunk)
            _, _, tf, tr = state_factors(dt, run, bef, t0, b)
            values = r.act[at, :inner].astype(F32)
            maps_t = r.act[at, inner:].astype(F32).T.astype(BF16)
            tfe, tre = widen(spread2, tf, tr)
            r.inc[chunk, 0:64, :] = nn(maps_t[0:64], (values * tfe).astype(BF16))
            r.inc[chunk, 64:128, :] = nn(maps_t[128:192], (values * tre).astype(BF16))
            gone = jnp.exp(run[:, Q - 1 : Q])
            pf, pr = widen_cols(spread_low, gone[:HP], gone[HP:])
            r.pexp[chunk, 0:1, :] = pf * jnp.where((t0 <= b) & (b < t0 + Q), 0.0, 1.0)
            r.pexp[chunk, 1:2, :] = pr * jnp.where((t0 < b) & (b <= t0 + Q), 0.0, 1.0)
        return 0

    lax.fori_loop(1, nblk, summarize, 0)

    @pl.when(me > 0)
    def _():
        halo_copy(me + 1).wait_recv()

    nh = normalize(r.halo[...])
    r.joined[0:16, :inner] = nn(nh, r.wv[...]).astype(BF16)
    r.joined[0:16, inner:] = nn(nh, r.ws[...]).astype(BF16)
    summarize(jnp.int32(0), 0)
    sumf, prodf = r.inc[0, 0:64, :], r.pexp[0, 0:1, :]
    sumr, prodr = r.inc[nchunk - 1, 64:128, :], r.pexp[nchunk - 1, 1:2, :]
    for c in range(1, nchunk):
        d = nchunk - 1 - c
        pf, pr = r.pexp[c, 0:1, :], r.pexp[d, 1:2, :]
        sumf, prodf = pf * sumf + r.inc[c, 0:64, :], prodf * pf
        sumr, prodr = pr * sumr + r.inc[d, 64:128, :], prodr * pr
    put_message(r.msgs.at[0], sumf, prodf * before_f)
    put_message(r.msgs.at[1], sumr, prodr * after_f)
    swap1.start()

    loads[3].wait()
    tri0, tri1 = iota((Q, Q), 0), iota((Q, Q), 1)
    lower, upper = tri0 > tri1, tri0 < tri1

    def within(blk, _):
        rows = part(blk, TB)
        r.gate[rows, :] = nn(r.buf[rows, :], r.wg[...])
        for q in range(per):
            chunk = blk * per + q
            at = part(chunk, Q)
            t0 = chunk * Q
            dt, ld, run, bef = chunk_parts(chunk)
            ldt = jnp.log(jnp.maximum(dt, 1e-37))
            rowf = ldt[:HP] - run[:HP]
            rowr = ldt[HP:] + bef[HP:]
            cols = jnp.concatenate([bef[:HP], -run[HP:]], axis=0).T
            scores = chunk_scores(r.act[at, inner:], t0, b)
            for j in range(inner // 128):
                lanes = slice(j * 128, (j + 1) * 128)
                weights = []
                for h in (2 * j, 2 * j + 1):
                    e = jnp.where(lower, cols[:, h : h + 1] + rowf[h : h + 1],
                                  cols[:, HP + h : HP + h + 1] + rowr[h : h + 1])
                    weights.append((jnp.exp(jnp.minimum(e, 60.0)) * scores).astype(BF16))
                vp = r.act[at, lanes]
                y = nn(jnp.concatenate(weights, axis=1), halves(vp))
                r.mixed[at, lanes] = y + skip[:, lanes] * vp.astype(F32)
        return 0

    lax.fori_loop(0, nblk, within, 0)
    loads[4].wait()
    loads[5].wait()
    swap1.finish()
    hf = chain(r.low1) * before_f
    hr = chain(r.high1) * after_f
    for c in range(nchunk):
        r.state[c, 0:64, :] = hf.astype(BF16)
        hf = r.pexp[c, 0:1, :] * hf + r.inc[c, 0:64, :]
        d = nchunk - 1 - c
        r.state[d, 64:128, :] = hr.astype(BF16)
        hr = r.pexp[d, 1:2, :] * hr + r.inc[d, 64:128, :]

    def enter(blk, _):
        lane = iota((Q, 128), 1)
        u_all = nt(r.cot[part(blk, TB), :], r.wo[...])
        r.dy[part(blk, TB), :] = u_all
        for q in range(per):
            chunk = blk * per + q
            at = part(chunk, Q)
            dt, ld, run, bef = chunk_parts(chunk)
            ef, er, _, _ = state_factors(dt, run, bef, chunk * Q, b)
            maps_here = r.act[at, inner:]
            state = r.state[chunk]
            efe, ere = widen(spread2, ef, er)
            ys = nn(maps_here[:, 64:128], state[0:64]) * efe + nn(maps_here[:, 192:256], state[64:128]) * ere
            square = jnp.zeros((Q, 1), F32)
            cross = jnp.zeros((Q, 1), F32)
            for j in range(inner // 128):
                lanes = slice(j * 128, (j + 1) * 128)
                y = r.mixed[at, lanes] + ys[:, lanes]
                r.mixed[at, lanes] = y
                gated = y * silu(r.gate[at, lanes])
                square = square + jnp.sum(gated * gated, axis=1, keepdims=True)
                cross = cross + jnp.sum(
                    gated * (u_all[q * Q : (q + 1) * Q, lanes] * ggain[:, lanes]), axis=1, keepdims=True)
            two = jnp.where(lane == 0, square, jnp.where(lane == 1, cross, 0.0))
            r.mine[blk, :, q * Q : (q + 1) * Q] = two.T[0:8]
        over(r.mine.at[blk], r.other.at[blk], r.sum_sem, blk).start()
        return 0

    lax.fori_loop(0, nblk, enter, 0)
    r.small[...] = jnp.zeros_like(r.small)

    def gating(blk, _):
        rows = part(blk, TB)
        over(r.mine.at[blk], r.other.at[blk], r.sum_sem, blk).wait()
        sums = r.mine[blk] + r.other[blk]
        sums = jnp.concatenate([sums, jnp.zeros((120, TB), F32)], axis=0).T
        scale = lax.rsqrt(sums[:, 0:1] / (2 * inner) + EPSILON)
        back = scale * scale * scale * sums[:, 1:2] / (2 * inner)
        for j in range(inner // 128):
            lanes = slice(j * 128, (j + 1) * 128)
            mixed = r.mixed[rows, lanes]
            pre = r.gate[rows, lanes]
            sig = jax.nn.sigmoid(pre)
            gated = mixed * (pre * sig)
            ng = gated * scale
            r.buf[rows, lanes] = (ng * ggain[:, lanes]).astype(BF16)
            g = r.dy[rows, lanes]
            r.small[0:1, lanes] += jnp.sum(g * ng, axis=0, keepdims=True)
            grad_gated = scale * (g * ggain[:, lanes]) - gated * back
            dy = grad_gated * (pre * sig)
            r.small[1:2, lanes] += jnp.sum(dy * r.act[rows, lanes].astype(F32), axis=0, keepdims=True)
            r.dy[rows, lanes] = dy
            r.ggate[rows, lanes] = (grad_gated * mixed * (sig * (1.0 + pre * (1.0 - sig)))).astype(BF16)
        for q in range(per):
            chunk = blk * per + q
            at = part(chunk, Q)
            dt, ld, run, bef = chunk_parts(chunk)
            ef, er, _, _ = state_factors(dt, run, bef, chunk * Q, b)
            maps_t = r.act[at, inner:].astype(F32).T.astype(BF16)
            dy = r.dy[at, :]
            efe, ere = widen(spread2, ef, er)
            r.inc[chunk, 0:64, :] = nn(maps_t[64:128], (dy * efe).astype(BF16))
            r.inc[chunk, 64:128, :] = nn(maps_t[192:256], (dy * ere).astype(BF16))
        return 0

    lax.fori_loop(0, nblk, gating, 0)
    sumf, sumr = r.inc[nchunk - 1, 0:64, :], r.inc[0, 64:128, :]
    for c in range(1, nchunk):
        d = nchunk - 1 - c
        sumf = r.pexp[d, 0:1, :] * sumf + r.inc[d, 0:64, :]
        sumr = r.pexp[c, 1:2, :] * sumr + r.inc[c, 64:128, :]
    put_message(r.msgs.at[2], sumr * after_f, prodr * after_f)
    put_message(r.msgs.at[3], sumf * before_f, prodf * before_f)
    swap2.start()
    for g in range(width // 256):
        pieces[of[f"ggw{g}"]]["work"][...] = nn(r.normt[g * 256 : (g + 1) * 256, :], r.ggate[...]).astype(BF16)
        red.start(of[f"ggw{g}"])
    for g in range(groups):
        pieces[of[f"gow{g}"]]["work"][...] = tn(r.buf[:, g * 256 : (g + 1) * 256], r.cot[...]).astype(BF16)
        red.start(of[f"gow{g}"])

    def project_out(blk, _):
        rows = part(blk, TB)
        r.out_mine[rows, :] = nn(r.buf[rows, :], r.wo[...]).astype(BF16)
        over(r.out_mine.at[rows], r.out_other.at[rows], r.out_sem, blk).start()
        return 0

    lax.fori_loop(0, nblk, project_out, 0)

    sums_low = jnp.concatenate([lower, upper], axis=1).astype(BF16)
    diag = tri0 == tri1
    r.rowbuf[...] = jnp.zeros_like(r.rowbuf)

    taken_within = red.takes("within", nblk)

    def back_within(blk, _):
        for q in range(per):
            chunk = blk * per + q
            at = part(chunk, Q)
            t0 = chunk * Q
            dt, ld, run, bef = chunk_parts(chunk)
            ldt = jnp.log(jnp.maximum(dt, 1e-37))
            cols = jnp.concatenate([ldt[:HP] - run[:HP], ldt[HP:] + bef[HP:]], axis=0).T
            rowf, rowr = bef[:HP], -run[HP:]
            m = r.act[at, inner:]
            entf, readf, entr, readr = m[:, 0:64], m[:, 64:128], m[:, 128:192], m[:, 192:256]
            same = (tri0 + t0 < b) == (tri1 + t0 < b)
            okf, okr = upper & same, lower & same
            scores = jnp.where(okf, nt(entf, readf), jnp.where(okr, nt(entr, readr), 0.0))
            dscore = jnp.zeros((Q, Q), F32)
            for j in range(inner // 128):
                lanes = slice(j * 128, (j + 1) * 128)
                vp = r.act[at, lanes]
                dyp32 = r.dy[at, lanes]
                dyp = dyp32.astype(BF16)
                dw = nt(halves(vp), dyp)
                weights = []
                for i, h in enumerate((2 * j, 2 * j + 1)):
                    e = jnp.where(upper, cols[:, h : h + 1] + rowf[h : h + 1],
                                  cols[:, HP + h : HP + h + 1] + rowr[h : h + 1])
                    x = jnp.exp(jnp.minimum(e, 60.0))
                    weights.append((x * scores).astype(BF16))
                    dwx = dw[i * Q : (i + 1) * Q] * x
                    dscore = dscore + dwx
                    sums = nn((dwx * scores).astype(BF16), sums_low)
                    pf, pr = sums[:, :Q], sums[:, Q:]
                    for place, kept in enumerate((jnp.where(upper, pf, 0.0), jnp.where(lower, pr, 0.0),
                                                  jnp.where(diag, pf, 0.0), jnp.where(diag, pr, 0.0))):
                        r.rowbuf[chunk, place * HP + h : place * HP + h + 1, :] = jnp.sum(kept, axis=0, keepdims=True)
                dv = nn(jnp.concatenate(weights, axis=1), halves(dyp))
                r.mixed[at, lanes] = dv + dyp32 * skip[:, lanes]
            dsf = jnp.where(okf, dscore, 0.0)
            dsr = jnp.where(okr, dscore, 0.0)
            r.mixed[at, inner:] = jnp.concatenate(
                [nn(dsf.astype(BF16), readf), nn(dsf.T.astype(BF16), entf),
                 nn(dsr.astype(BF16), readr), nn(dsr.T.astype(BF16), entr)], axis=1)

        red.hook(blk, taken_within)
        return 0

    lax.fori_loop(0, nblk, back_within, 0)
    swap2.finish()
    df = chain(r.high2)
    dr = chain(r.low2)
    for c in range(nchunk):
        d = nchunk - 1 - c
        r.dstate[d, 0:64, :] = df.astype(BF16)
        df = r.pexp[d, 0:1, :] * df + r.inc[d, 0:64, :]
        r.dstate[c, 64:128, :] = dr.astype(BF16)
        dr = r.pexp[c, 1:2, :] * dr + r.inc[c, 64:128, :]
    r.cg_mine[...] = jnp.zeros_like(r.cg_mine)
    r.hsum[...] = jnp.zeros_like(r.hsum)

    def lent_copy(to):
        return pltpu.make_async_remote_copy(
            src_ref=r.lent_mine, dst_ref=r.lent_other, send_sem=r.edge.at[2], recv_sem=r.edge.at[3],
            device_id=(to, core), device_id_type=MESH)

    lower_low, upper_low = lower.astype(BF16), upper.astype(BF16)

    taken_states = red.takes("states", nblk)

    def back_states(blk, _):
        for q in range(per):
            chunk = blk * per + q
            at = part(chunk, Q)
            dt, ld, run, bef = chunk_parts(chunk)
            ef, er, tf, tr = state_factors(dt, run, bef, chunk * Q, b)
            m = r.act[at, inner:]
            entf, readf, entr, readr = m[:, 0:64], m[:, 64:128], m[:, 128:192], m[:, 192:256]
            state = r.state[chunk]
            grad_state = r.dstate[chunk]
            dy = r.dy[at, :]
            values = r.act[at, :inner].astype(F32)
            efe, ere, tfe, tre = widen(spread2, ef, er, tf, tr)
            dyf, dyr = dy * efe, dy * ere
            dreadf = nt(dyf.astype(BF16), state[0:64])
            dreadr = nt(dyr.astype(BF16), state[64:128])
            qf = nt(spread_low, (nn(readf, state[0:64]) * dyf).astype(BF16))
            qr = nt(spread_low, (nn(readr, state[64:128]) * dyr).astype(BF16))
            dvf = nn(entf, grad_state[0:64]) * tfe
            dvr = nn(entr, grad_state[64:128]) * tre
            wf = nt(spread_low, (values * dvf).astype(BF16))
            wr = nt(spread_low, (values * dvr).astype(BF16))
            dentf = nt((values * tfe).astype(BF16), grad_state[0:64])
            dentr = nt((values * tre).astype(BF16), grad_state[64:128])
            through = state.astype(F32) * grad_state.astype(F32)
            zf = jnp.sum(through[0:64], axis=0, keepdims=True) * r.pexp[chunk, 0:1, :]
            zr = jnp.sum(through[64:128], axis=0, keepdims=True) * r.pexp[chunk, 1:2, :]
            through = jnp.concatenate([zf, zr, jnp.zeros((6, inner), F32)], axis=0)
            through = exact(nt(thirds(through), spread_low), 8)
            through = jnp.concatenate([through, jnp.zeros((120, HP), F32)], axis=0).T
            zf, zr = through[:, 0:1], through[:, 1:2]
            r.mixed[at, :inner] = r.mixed[at, :inner] + dvf + dvr
            r.mixed[at, inner:] = r.mixed[at, inner:] + jnp.concatenate([dentf, dreadf, dentr, dreadr], axis=1)
            late = exact(nn(thirds(jnp.concatenate([qf, wr], axis=0)), lower_low), 2 * HP)
            early = exact(nn(thirds(jnp.concatenate([wf, qr], axis=0)), upper_low), 2 * HP)
            rowsum = r.rowbuf[chunk]
            dld = jnp.concatenate(
                [rowsum[0:HP] + late[:HP] + early[:HP] + zf, rowsum[HP : 2 * HP] + late[HP:] + early[HP:] + zr], axis=0)
            dldt = rowsum[2 * HP : 4 * HP] + jnp.concatenate([wf, wr], axis=0)
            sig = jax.nn.sigmoid(r.step[:, at] + bias)
            ratio = jnp.where(dt < 1e-30, 1.0, sig / jnp.maximum(dt, 1e-30))
            graw = dldt * ratio - jnp.exp(dlog) * sig * dld
            r.gstep[:, at] = graw.astype(BF16)
            r.hsum[:, 0:1] += jnp.sum(graw, axis=1, keepdims=True)
            r.hsum[:, 1:2] += jnp.sum(dld * ld, axis=1, keepdims=True)

        @pl.when(blk == 0)
        def _():
            tok8 = iota((8, 1), 0)
            tap = r.tap[...]
            dconv = r.mixed[0:8, :] * r.slope[0:16, :].astype(F32)[0:8]
            rows = r.joined[0:16, :].astype(F32)[8:16]
            lent = jnp.zeros((8, both), F32)
            for m in range(1, 4):
                first = jnp.concatenate([jnp.zeros((8, both), F32), dconv * conv_mask(tok8, m, b, off0)], axis=0)
                first = first[m : m + 8]
                lent = lent + first * tap[3 - m : 4 - m]
                r.cg_mine[3 - m : 4 - m, :] = jnp.sum(first * rows, axis=0, keepdims=True)
            r.lent_mine[...] = lent

            @pl.when(me > 0)
            def _():
                lent_copy(me - 1).start()

        red.hook(blk, taken_states)
        return 0

    lax.fori_loop(0, nblk, back_states, 0)

    @pl.when(me + 1 < count)
    def _():
        lent_copy(me - 1).wait_recv()

    @pl.when(me + 1 == count)
    def _():
        r.lent_other[...] = jnp.zeros_like(r.lent_other)

    def back_conv(g):
        cols = slice(g * 256, (g + 1) * 256)
        r.ext[...] = jnp.zeros_like(r.ext)

        def one(i, _):
            blk = nblk - 1 - i
            rows = part(blk, TB)
            tap = r.tap[:, cols]
            x = r.joined[pl.ds(pl.multiple_of(16 + blk * TB, 16), TB), cols].astype(F32)
            dconv = r.mixed[rows, cols] * r.slope[rows, cols].astype(F32)
            grad = dconv * tap[3:4]
            r.cg_mine[3:4, cols] += jnp.sum(dconv * x, axis=0, keepdims=True)
            for m in range(1, 4):
                r.ext[m - 1, TB : TB + 8, :] = r.ext[m - 1, 0:8, :]
                r.ext[m - 1, 0:TB, :] = dconv * valid_of(rows, m)
                moved = r.ext[m - 1, m : m + TB, :]
                r.cg_mine[3 - m : 4 - m, cols] += jnp.sum(moved * x, axis=0, keepdims=True)
                grad = grad + moved * tap[3 - m : 4 - m]
            last = jnp.where(blk == nblk - 1, 1.0, 0.0)
            grad = jnp.concatenate([grad[: TB - 8], grad[TB - 8 :] + r.lent_other[:, cols] * last], axis=0)
            if g * 256 < inner:
                r.buf[rows, cols] = grad.astype(BF16)
            else:
                r.gs_mine[rows, :] = grad.astype(BF16)
            return 0

        lax.fori_loop(0, nblk, one, 0)

    back_conv(inner // 256)
    gs_copy = over(r.gs_mine, r.gs_other, r.misc_sem, 0)
    gs_copy.start()
    cg_copy = over(r.cg_mine.at[:, pl.ds(inner, maps)], r.cg_other, r.misc_sem, 1)
    cg_copy.start()
    red.at("maps")

    def finish_maps():
        gs_copy.wait()
        cg_copy.wait()
        r.gs_mine[...] = (r.gs_mine[...].astype(F32) + r.gs_other[...].astype(F32)).astype(BF16)
        half = r.gs_mine[:, pl.ds(pl.multiple_of(core * 128, 128), 128)]
        r.gsw_w[:, 0:128] = nn(r.normt[...], half).astype(BF16)
        gstep = jnp.concatenate([r.gstep[...].astype(F32), jnp.zeros((128 - 2 * HP, length), F32)], axis=0)
        r.gsw_w[:, 128:256] = nt(r.normt[...], gstep.astype(BF16)).astype(BF16)
        red.start(of["gsw"])

    for g in range(groups):
        cols = slice(g * 256, (g + 1) * 256)
        back_conv(g)
        pieces[of[f"gv{g}"]]["work"][...] = nn(r.normt[...], r.buf[:, cols]).astype(BF16)
        red.start(of[f"gv{g}"])
        if g == 0:
            finish_maps()
        red.at("conv" + str(g))

    taken_down = red.takes("down", nblk)

    def down(blk, _):
        rows = part(blk, TB)
        gn = nt(r.ggate[rows, :], r.wg[...]) + nt(r.buf[rows, :], r.wv[...]) + tn(r.gstep[:, rows], r.wst[...])
        r.gn_mine[rows, :] = gn.astype(BF16)
        over(r.gn_mine.at[rows], r.gn_other.at[rows], r.gn_sem, blk).start()
        red.hook(blk, taken_down)
        return 0

    lax.fori_loop(0, nblk, down, 0)
    tiny = r.tiny_w.at[0]
    tiny[...] = jnp.zeros((8, both), F32)
    tiny[0:2, :inner] = r.small[0:2, :]
    head_sums = r.hsum[...].T
    tiny[3:4, 0 : 2 * HP] = head_sums[0:1]
    tiny[3:4, 128 : 128 + 2 * HP] = head_sums[1:2]
    tiny[4:8, :inner] = r.cg_mine[0:4, :inner]
    tiny[4:8, inner:] = r.cg_mine[0:4, inner:] + r.cg_other[0:4, :]

    def out_copy(blk):
        rows = part(blk, TB)
        return (pltpu.make_async_copy(r.out_other.at[rows], r.block_out.at[rows], r.store.at[0, blk]),
                pltpu.make_async_copy(r.gate.at[rows], r.grad_hidden.at[rows], r.store.at[1, blk]))

    taken_end = red.takes("end", nblk)

    def ending(blk, _):
        rows = part(blk, TB)
        over(r.out_mine.at[rows], r.out_other.at[rows], r.out_sem, blk).wait()
        over(r.gn_mine.at[rows], r.gn_other.at[rows], r.gn_sem, blk).wait()
        x = r.hid[rows, :].astype(F32)
        r.out_other[rows, :] = (
            x + (r.out_mine[rows, :].astype(F32) + r.out_other[rows, :].astype(F32))).astype(BF16)
        gn = r.gn_mine[rows, :].astype(F32) + r.gn_other[rows, :].astype(F32) + nt(r.gs_mine[rows, :], r.ws[...])
        scale = lax.rsqrt(jnp.mean(x * x, axis=1, keepdims=True) + EPSILON)
        tiny[2:3, :width] += jnp.sum(gn * x * scale, axis=0, keepdims=True)
        v = gn * gain
        mean = jnp.mean(x * v, axis=1, keepdims=True)
        r.gate[rows, :] = r.cot[rows, :].astype(F32) + scale * v - x * (scale * scale * scale * mean)
        for copy in out_copy(blk):
            copy.start()
        red.hook(blk, taken_end)
        return 0

    lax.fori_loop(0, nblk, ending, 0)

    def tiny_copy(s):
        return pltpu.make_async_remote_copy(
            src_ref=r.tiny_w.at[s], dst_ref=r.tiny_r.at[s], send_sem=r.tiny_sem.at[0, s],
            recv_sem=r.tiny_sem.at[1, s], device_id=(red.mates[s], core), device_id_type=MESH)

    halves_copy = over(r.gsw_o.at[:, pl.ds(0, 128)], r.gsx, r.misc_sem, 2)
    stores = []

    def store(src, dst):
        copy = pltpu.make_async_copy(src, dst, r.store.at[2, len(stores)])
        copy.start()
        stores.append(copy)

    def settle(p):
        red.finish(p)
        name, out = names[p], pieces[p]["out"]
        if name == "gsw":
            halves_copy.start()
            return
        kind, at = name[:-1], pl.ds(int(name[-1]) * 256, 256)
        store(out, r.ggw_any.at[at] if kind == "ggw" else r.gow_any.at[at] if kind == "gow" else r.gvw_any.at[:, at])

    for p in range(len(pieces)):
        if red.pos[p] == len(red.steps[p]):
            settle(p)
    tiny_copy(0).start()
    rest, turns = red.left(), 0
    for i, (p, at) in enumerate(rest):
        red.step(p, at)
        if at == len(red.steps[p]) - 1:
            settle(p)
        while turns < bits and (turns + 1) * len(rest) <= (i + 1) * (bits + 1) or i + 1 == len(rest) and turns < bits:
            tiny_copy(turns).wait()
            r.tiny_w[turns + 1] = r.tiny_w[turns] + r.tiny_r[turns]
            turns += 1
            if turns < bits:
                tiny_copy(turns).start()
    store(r.tiny_w.at[bits], r.tiny_any)
    halves_copy.wait()
    mine_at, other_at = pl.multiple_of(core * 128, 128), pl.multiple_of((1 - core) * 128, 128)
    store(r.gsw_o.at[:, pl.ds(0, 128)], r.gsw_any.at[:, pl.ds(mine_at, 128)])
    store(r.gsx, r.gsw_any.at[:, pl.ds(other_at, 128)])
    store(r.gsw_o.at[:, pl.ds(128, 128)], r.gsw_any.at[:, pl.ds(256, 128)])
    for copy in stores:
        copy.wait()
    for blk in range(nblk):
        for copy in out_copy(blk):
            copy.wait()

    @pl.when(me + 1 < count)
    def _():
        halo_copy(me + 1).wait_send()

    @pl.when(me > 0)
    def _():
        lent_copy(me - 1).wait_send()


TABLE_BITS = 4
ORDERS = (
    (1, 0, 3, 2),
    (0, 1, 3, 2),
    (0, 2, 1, 3),
    (2, 3, 1, 0),
    (1, 0, 2, 3),
    (1, 2, 0, 3),
    (0, 1, 2, 3),
    (2, 1, 0, 3),
    (1, 2, 0, 3),
    (0, 1, 3, 2),
)
TABLE = {
    "within1": (
        (3, 0),
    ),
    "within2": (
        (0, 0), (1, 0), (2, 0),
    ),
    "within3": (
        (4, 0), (5, 0),
    ),
    "states0": (
        (0, 1), (1, 1), (2, 1), (3, 1),
    ),
    "states1": (
        (4, 1), (5, 1),
    ),
    "states2": (
        (2, 2), (3, 2),
    ),
    "states3": (
        (0, 2), (1, 2), (4, 2), (5, 2),
    ),
    "maps": (
        (2, 3), (3, 3),
    ),
    "conv0": (
        (0, 3), (1, 3), (4, 3), (5, 3),
    ),
    "conv1": (
        (2, 4), (3, 4),
    ),
    "conv2": (
        (0, 4), (1, 4), (4, 4), (5, 4),
    ),
    "down0": (
        (2, 5), (3, 5), (6, 0),
    ),
    "down1": (
        (5, 5),
    ),
    "down2": (
        (4, 5), (7, 0), (8, 0),
    ),
    "down3": (
        (0, 5), (1, 5), (6, 1), (9, 0),
    ),
    "end2": (
        (2, 6), (3, 6), (4, 6), (7, 1),
    ),
    "end3": (
        (0, 6),
    ),
    "tail": (
        (5, 6), (6, 2), (8, 1), (1, 6), (9, 1), (6, 3), (7, 2), (9, 2), (8, 2), (6, 4), (7, 3), (3, 7),
        (9, 3), (8, 3), (2, 7), (7, 4), (1, 7), (6, 5), (4, 7), (9, 4), (8, 4), (7, 5), (0, 7), (5, 7),
        (8, 5), (9, 5), (6, 6), (7, 6), (8, 6), (9, 6), (6, 7), (7, 7), (8, 7), (9, 7),
    ),
}


def last_kernel(heads, ggw_ref, gow_ref, gvw_ref, gsw_ref, tiny_ref,
                ngain_ref, ggwo_ref, gvwo_ref, gswo_ref, gsteo_ref, convv_ref, convs_ref, bias_ref, decay_ref,
                skip_ref, ggain_ref, gowo_ref):
    ggwo_ref[...] = ggw_ref[...].astype(F32)
    gvwo_ref[...] = gvw_ref[...].astype(F32)
    maps = gswo_ref.shape[1]
    gswo_ref[...] = gsw_ref[:, :maps].astype(F32)
    step = gsw_ref[:, maps:].astype(F32).T
    gsteo_ref[...] = jnp.stack([step[:heads], step[HP : HP + heads]], axis=1)
    gowo_ref[...] = gow_ref[...].astype(F32)

    @pl.when(pl.program_id(0) == 0)
    def _():
        width, inner = ngain_ref.shape[0], convv_ref.shape[1]
        ngain_ref[...] = tiny_ref[2, :width]
        ggain_ref[...] = tiny_ref[0, :inner]
        convv_ref[...] = tiny_ref[4:8, :inner]
        convs_ref[...] = tiny_ref[4:8, inner:]
        bias_ref[...] = jnp.concatenate([tiny_ref[3:4, 0:heads], tiny_ref[3:4, HP : HP + heads]], axis=0)
        decay_ref[...] = (tiny_ref[3:4, 128 : 128 + heads] + tiny_ref[3:4, 128 + HP : 128 + HP + heads]).reshape(heads)
        spread = spread_matrix(inner, inner // heads)
        total = nt(jnp.broadcast_to(tiny_ref[1:2, :inner], (8, inner)), spread, HIGHEST)
        skip_ref[...] = total[0:1, :heads].reshape(heads)


SMEM_SPEC = pl.BlockSpec(memory_space=pltpu.SMEM)
VMEM_SPEC = pl.BlockSpec(memory_space=pltpu.VMEM)
ANY_SPEC = pl.BlockSpec(memory_space=pl.ANY)


def body(
    hidden_in, norm_gain, gate_proj, value_proj, state_proj, step_proj, conv_value, conv_state,
    step_bias, decay_log, skip_scale, gate_gain, out_proj, lengths, cotangent,
):
    length, width = hidden_in.shape
    inner = gate_proj.shape[1]
    heads = decay_log.shape[0]
    maps = state_proj.shape[1]
    both = inner + maps
    nblk, nchunk = length // TB, length // Q
    count = lax.axis_size("seq")
    bits = count.bit_length() - 1
    assert count == 1 << bits
    reach = min(1 + (LEN_MOST - 2) // length, count - 1)
    npieces = len(piece_names(width, inner))

    def vmem(*dims, dtype=F32):
        return pltpu.VMEM(dims, dtype)

    dma = pltpu.SemaphoreType.DMA
    low = dict(dtype=BF16)
    scratch = dict(
        hid=vmem(length, width, **low), wg=vmem(width, inner, **low), wv=vmem(width, inner, **low),
        ws=vmem(width, maps, **low), wo=vmem(inner, width, **low), cot=vmem(length, width, **low),
        wst=vmem(2 * HP, width, **low), tap=vmem(4, both),
        normt=vmem(width, length, **low), buf=vmem(length, inner, **low), gate=vmem(length, inner),
        joined=vmem(16 + length, both, **low), act=vmem(length, both, **low), step=vmem(2 * HP, length), dt=vmem(2 * HP, length), run=vmem(2 * HP, length),
        inc=vmem(nchunk, 128, inner), pexp=vmem(nchunk, 2, inner), mixed=vmem(length, both),
        state=vmem(nchunk, 128, inner, **low), dstate=vmem(nchunk, 128, inner, **low),
        dy=vmem(length, inner), ggate=vmem(length, inner, **low), gstep=vmem(2 * HP, length, **low),
        msgs=vmem(4, 80, inner, **low),
        low1=vmem(reach, 80, inner, **low), high1=vmem(reach, 80, inner, **low),
        low2=vmem(reach, 80, inner, **low), high2=vmem(reach, 80, inner, **low),
        rowbuf=vmem(nchunk, 4 * HP, Q), jx=vmem(TB + 16, 256), ext=vmem(3, TB + 8, 256),
        valid=vmem(3, length, 128, **low), slope=vmem(length, both, **low), gsx=vmem(width, 128, **low),
        halo=vmem(16, width, **low), mine=vmem(nblk, 8, TB), other=vmem(nblk, 8, TB),
        out_mine=vmem(length, width, **low), out_other=vmem(length, width, **low),
        gn_mine=vmem(length, width, **low), gn_other=vmem(length, width, **low),
        gs_mine=vmem(length, maps, **low), gs_other=vmem(length, maps, **low),
        lent_mine=vmem(8, both), lent_other=vmem(8, both), cg_mine=vmem(8, both), cg_other=vmem(8, maps),
        hsum=vmem(2 * HP, 128), small=vmem(8, inner),
        tiny_w=vmem(bits + 1, 8, both), tiny_r=vmem(bits, 8, both),
    )
    for name in piece_names(width, inner):
        rows, cols = (256, width) if name[:3] in ("ggw", "gow") else (width, 256)
        scratch[name + "_w"] = vmem(rows, cols, **low)
        scratch[name + "_k"] = vmem(rows // 2, cols, **low)
        scratch[name + "_r"] = vmem(received_rows(rows, bits), cols, **low)
        scratch[name + "_o"] = vmem(rows, cols, **low)
    scratch.update(
        load=dma((6,)), store=dma((3, npieces + nblk)), edge=dma((4,)), sum_sem=dma((2, nblk)), out_sem=dma((2, nblk)),
        gn_sem=dma((2, nblk)), misc_sem=dma((2, 3)), tiny_sem=dma((2, bits)),
        up_s=dma((2, reach)), up_r=dma((2, reach)), dn_s=dma((2, reach)), dn_r=dma((2, reach)),
        rs_s=dma((npieces, bits)), rs_r=dma((npieces, bits)), ag_s=dma((npieces, bits)), ag_r=dma((npieces, bits)),
    )

    def shape(*dims, dtype=F32):
        return jax.ShapeDtypeStruct(dims, dtype)

    outs = pl.pallas_call(
        partial(layer_kernel, reach, bits, NAMES_IN + NAMES_OUT + tuple(scratch)),
        in_specs=[SMEM_SPEC] + [ANY_SPEC] * 6 + [VMEM_SPEC] * 8,
        out_specs=[ANY_SPEC] * 7,
        out_shape=[shape(length, width, **low), shape(length, width), shape(width, inner, **low),
                   shape(inner, width, **low), shape(width, inner, **low), shape(width, maps + 128, **low),
                   shape(8, both)],
        scratch_shapes=list(scratch.values()),
        compiler_params=pltpu.CompilerParams(
            collective_id=1, has_side_effects=True, vmem_limit_bytes=VMEM_LIMIT),
    )(lengths, hidden_in, gate_proj, value_proj, state_proj, out_proj, cotangent,
      norm_gain, step_proj.transpose(2, 0, 1), conv_value, conv_state, step_bias, decay_log, skip_scale, gate_gain)
    block_out, grad_hidden, ggw, gow, gvw, gsw, tiny = outs

    rows = 128
    def tall(cols):
        return pl.BlockSpec((rows, cols), lambda i: (i, 0))

    def whole(*dims):
        return pl.BlockSpec(dims, lambda i: (0,) * len(dims))

    assert width % rows == 0 and inner % rows == 0 and inner == width
    final = pl.pallas_call(
        partial(last_kernel, heads),
        grid=(width // rows,),
        in_specs=[tall(inner), tall(width), tall(inner), tall(maps + 128), whole(8, both)],
        out_specs=[whole(width), tall(inner), tall(inner), tall(maps), pl.BlockSpec((heads, 2, rows), lambda i: (0, 0, i)), whole(4, inner),
                   whole(4, maps), whole(2, heads), whole(heads), whole(heads), whole(inner), tall(width)],
        out_shape=[shape(width), shape(width, inner), shape(width, inner), shape(width, maps),
                   shape(heads, 2, width), shape(4, inner), shape(4, maps), shape(2, heads), shape(heads),
                   shape(heads), shape(inner), shape(inner, width)],
        compiler_params=pltpu.CompilerParams(dimension_semantics=("arbitrary",), vmem_limit_bytes=60 * MIB),
    )(ggw, gow, gvw, gsw, tiny)
    ngain, ggw, gvw, gsw, gstepw, convv, convs, bias, decay, skip, ggain, gow = final
    return (block_out, grad_hidden, ngain, ggw, gvw, gsw, gstepw.transpose(1, 2, 0), convv, convs, bias, decay, skip,
            ggain, gow)


def solution(mesh):
    in_specs = (
        P("seq", None),
        P(),
        P(None, "head"),
        P(None, "head"),
        P(),
        P(None, None, "head"),
        P(None, "head"),
        P(),
        P(None, "head"),
        P("head"),
        P("head"),
        P("head"),
        P("head", None),
        P(),
        P("seq", None),
    )
    out_specs = (
        P("seq", None),
        P("seq", None),
        P(),
        P(None, "head"),
        P(None, "head"),
        P(),
        P(None, None, "head"),
        P(None, "head"),
        P(),
        P(None, "head"),
        P("head"),
        P("head"),
        P("head"),
        P("head", None),
    )
    return jax.shard_map(body, mesh=mesh, in_specs=in_specs, out_specs=out_specs, check_vma=False)
```

```python
from functools import partial

import jax
import jax.numpy as jnp
from jax import lax
from jax.experimental import pallas as pl
from jax.experimental.pallas import tpu as pltpu
from jax.sharding import PartitionSpec as P

EPSILON = 1e-05
LEN_MOST = 4096
Q = 128
TB = 256
HP = 16
MIB = 1024 * 1024
VMEM_LIMIT = 63 * MIB + MIB // 2
HIGHEST = lax.Precision.HIGHEST
F32 = jnp.float32
BF16 = jnp.bfloat16
MESH = pl.DeviceIdType.MESH


def nn(a, b, precision=None):
    return jnp.dot(a, b, preferred_element_type=F32, precision=precision)


def nt(a, b, precision=None):
    return lax.dot_general(a, b, (((1,), (1,)), ((), ())), preferred_element_type=F32, precision=precision)


def tn(a, b, precision=None):
    return lax.dot_general(a, b, (((0,), (0,)), ((), ())), preferred_element_type=F32, precision=precision)


def iota(shape, axis):
    return lax.broadcasted_iota(jnp.int32, shape, axis)


def spread_matrix(width, hdim):
    return (iota((HP, width), 1) // hdim == iota((HP, width), 0)).astype(F32)


def split(x):
    hi = x.astype(BF16)
    return hi, (x - hi.astype(F32)).astype(BF16)


def thirds(x):
    hi = x.astype(BF16)
    rest = x - hi.astype(F32)
    mid = rest.astype(BF16)
    return jnp.concatenate([hi, mid, (rest - mid.astype(F32)).astype(BF16)], axis=0)


def exact(product, rows):
    return product[:rows] + product[rows : 2 * rows] + product[2 * rows :]


def widen(spread2, *factors):
    stacks = []
    for rows in factors:
        hi, lo = split(rows.T)
        stacks.append(jnp.concatenate([hi, lo], axis=1))
    wide = nn(jnp.concatenate(stacks, axis=0), spread2)
    return [wide[i * Q : (i + 1) * Q] for i in range(len(factors))]


def widen_cols(spread_low, *cols):
    rows = jnp.concatenate([*cols, jnp.zeros((HP, 128 - len(cols)), F32)], axis=1).T[0:8]
    wide = exact(nn(thirds(rows), spread_low), 8)
    return [wide[i : i + 1] for i in range(len(cols))]


def silu(x):
    return x * jax.nn.sigmoid(x)


def softplus(x):
    return jnp.maximum(x, 0.0) + jnp.log1p(jnp.exp(-jnp.abs(x)))


def state_factors(dt, run, bef, t0, b):
    t1 = t0 + Q
    tok = iota((1, Q), 1) + t0
    ef = jnp.where((tok < b) | (t0 > b), jnp.exp(bef[:HP]), 0.0)
    er = jnp.where((tok >= b) | (t1 < b), jnp.exp(run[HP:, Q - 1 : Q] - run[HP:]), 0.0)
    tf = jnp.where((tok >= b) | (t1 <= b), jnp.exp(run[:HP, Q - 1 : Q] - run[:HP]), 0.0) * dt[:HP]
    tr = jnp.where((tok < b) | (t0 >= b), jnp.exp(bef[HP:]), 0.0) * dt[HP:]
    return ef, er, tf, tr


def conv_mask(tok, shift, b, off0):
    lost = ((tok < b) & (tok + off0 < shift)) | ((tok >= b) & (tok < b + shift))
    return jnp.where(lost, 0.0, 1.0)


def put_message(ref, state, passed):
    hi, lo = split(passed)
    ref[0:64, :] = state.astype(BF16)
    row = iota((16, state.shape[1]), 0)
    tail = jnp.where(row == 0, hi.astype(F32), jnp.where(row == 1, lo.astype(F32), 0.0))
    ref[64:80, :] = tail.astype(BF16)


def chain(ref):
    total = ref[0, 0:64, :].astype(F32)
    passed = None
    for k in range(1, ref.shape[0]):
        tail = ref[k - 1, 64:80, :].astype(F32)
        here = tail[0:1] + tail[1:2]
        passed = here if passed is None else passed * here
        total = total + passed * ref[k, 0:64, :].astype(F32)
    return total


class Swap:
    def __init__(self, reach, up_ref, down_ref, from_low, from_high, up_send, up_recv, down_send, down_recv):
        self.me, self.core, self.count = lax.axis_index("seq"), lax.axis_index("head"), lax.axis_size("seq")
        self.reach, self.up_ref, self.down_ref, self.from_low, self.from_high = reach, up_ref, down_ref, from_low, from_high
        self.sems = up_send, up_recv, down_send, down_recv

    def up(self, k):
        return pltpu.make_async_remote_copy(
            src_ref=self.up_ref, dst_ref=self.from_low.at[k - 1], send_sem=self.sems[0].at[k - 1],
            recv_sem=self.sems[1].at[k - 1], device_id=(self.me + k, self.core), device_id_type=MESH)

    def down(self, k):
        return pltpu.make_async_remote_copy(
            src_ref=self.down_ref, dst_ref=self.from_high.at[k - 1], send_sem=self.sems[2].at[k - 1],
            recv_sem=self.sems[3].at[k - 1], device_id=(self.me - k, self.core), device_id_type=MESH)

    def greet(self, barrier):
        me, core, count = self.me, self.core, self.count
        for k in range(1, self.reach + 1):
            @pl.when(me + k < count)
            def _():
                pl.semaphore_signal(barrier, inc=1, device_id=(me + k, core), device_id_type=MESH)

            @pl.when(me >= k)
            def _():
                pl.semaphore_signal(barrier, inc=1, device_id=(me - k, core), device_id_type=MESH)
        return jnp.minimum(me, self.reach) + jnp.minimum(count - 1 - me, self.reach)

    def start(self):
        me, count = self.me, self.count
        for k in range(1, self.reach + 1):
            @pl.when(me + k < count)
            def _():
                self.up(k).start()

            @pl.when(me >= k)
            def _():
                self.down(k).start()

            @pl.when(me < k)
            def _():
                self.from_low[k - 1] = jnp.zeros_like(self.from_low[k - 1])

            @pl.when(me + k >= count)
            def _():
                self.from_high[k - 1] = jnp.zeros_like(self.from_high[k - 1])

    def finish(self):
        me, count = self.me, self.count
        for k in range(1, self.reach + 1):
            @pl.when(me + k < count)
            def _():
                self.up(k).wait_send()
                self.down(k).wait_recv()

            @pl.when(me >= k)
            def _():
                self.down(k).wait_send()
                self.up(k).wait_recv()


def chunk_scores(maps, t0, b):
    tr, tc = iota((Q, Q), 0), iota((Q, Q), 1)
    same = (tr + t0 < b) == (tc + t0 < b)
    fwd = nt(maps[:, 64:128], maps[:, 0:64])
    rev = nt(maps[:, 192:256], maps[:, 128:192])
    return jnp.where((tr > tc) & same, fwd, jnp.where((tr < tc) & same, rev, 0.0))


def halves(x):
    left = iota(x.shape, 1) < 64
    zero = jnp.zeros_like(x)
    return jnp.concatenate([jnp.where(left, x, zero), jnp.where(left, zero, x)], axis=0)


class Reduce:
    def __init__(self, bits, pieces, rs_send, rs_recv, ag_send, ag_recv):
        me, core = lax.axis_index("seq"), lax.axis_index("head")
        bit = [lax.rem(me // (1 << k), 2) for k in range(bits)]
        mate = [me + (1 - 2 * bit[k]) * (1 << k) for k in range(bits)]
        self.mates = list(mate)
        self.bits, self.bit, self.mate, self.core, self.pieces = bits, bit, mate, core, pieces
        self.sems = rs_send, rs_recv, ag_send, ag_recv
        self.pos = [0] * len(pieces)
        self.steps = []
        for piece in pieces:
            halvings = halvings_of(piece["work"].shape[0], bits)
            self.steps.append([("rs", s) for s in range(bits)] + [("ag", s) for s in reversed(range(halvings))])

    def geometry(self, p, s):
        rows = self.pieces[p]["work"].shape[0]
        halvings = halvings_of(rows, self.bits)
        off, slot = jnp.int32(0), 0
        for t in range(s):
            if t < halvings:
                rows = rows // 2
                off = off + self.bit[self.pieces[p]["order"][t]] * rows
            slot += rows
        return off, rows, slot, s < halvings

    def remote(self, src, dst, send, recv, k):
        return pltpu.make_async_remote_copy(
            src_ref=src, dst_ref=dst, send_sem=send, recv_sem=recv, device_id=(self.mate[k], self.core),
            device_id_type=MESH)

    def first(self, p):
        return self.bit[self.pieces[p]["order"][0]] * (self.pieces[p]["work"].shape[0] // 2)

    def copy(self, p, step):
        kind, s = step
        piece = self.pieces[p]
        k = piece["order"][s]
        if kind == "rs":
            off, rows, slot, halved = self.geometry(p, s)
            source, off = (piece["work"], off) if s == 0 else (piece["kept"], off - self.first(p))
            if halved:
                rows = rows // 2
                off = off + (1 - self.bit[k]) * rows
            return self.remote(
                source.at[pl.ds(pl.multiple_of(off, 16), rows)], piece["recv"].at[pl.ds(slot, rows)],
                self.sems[0].at[p, s], self.sems[1].at[p, s], k)
        off, rows, _, _ = self.geometry(p, s + 1)
        where = piece["out"].at[pl.ds(pl.multiple_of(off, 16), rows)]
        return self.remote(where, where, self.sems[2].at[p, s], self.sems[3].at[p, s], k)

    def arriving(self, p, s):
        off, rows, _, _ = self.geometry(p, s + 1)
        k = self.pieces[p]["order"][s]
        off = off + (1 - 2 * self.bit[k]) * rows
        where = self.pieces[p]["out"].at[pl.ds(pl.multiple_of(off, 16), rows)]
        return self.remote(where, where, self.sems[2].at[p, s], self.sems[3].at[p, s], k)

    def start(self, p):
        self.copy(p, self.steps[p][0]).start()

    def step(self, p, at):
        kind, s = self.steps[p][at]
        if kind == "rs":
            self.add(p, s, self.copy(p, (kind, s)))
        else:
            self.arriving(p, s).wait_recv()
        if at + 1 < len(self.steps[p]):
            self.copy(p, self.steps[p][at + 1]).start()

    def take(self, name):
        if self.bits != TABLE_BITS:
            return []
        taken = TABLE.get(name, ())
        for p, at in taken:
            assert self.pos[p] == at
            self.pos[p] = at + 1
        return taken

    def at(self, name):
        for p, at in self.take(name):
            self.step(p, at)

    def takes(self, name, count):
        return {k: self.take(name + str(k)) for k in range(count)}

    def hook(self, turn, taken, per=1, q=0):
        for k, steps in taken.items():
            if steps and k % per == q:
                @pl.when(turn == k // per)
                def _():
                    for p, at in steps:
                        self.step(p, at)

    def left(self):
        order = list(TABLE["tail"]) if self.bits == TABLE_BITS else []
        rest = [(p, at) for p in range(len(self.pieces)) for at in range(self.pos[p], len(self.steps[p]))]
        return order + sorted((x for x in rest if x not in order), key=lambda x: x[::-1])

    def add(self, p, s, copy):
        piece = self.pieces[p]
        off, rows, slot, halved = self.geometry(p, s)
        if halved:
            copy.wait_recv()
            rows = rows // 2
            off = off + self.bit[piece["order"][s]] * rows
        else:
            copy.wait()
        recv, rel = piece["recv"], off - self.first(p)
        source, at = (piece["work"], off) if s == 0 else (piece["kept"], rel)
        dest, to = (piece["out"], off) if s == self.bits - 1 else (piece["kept"], rel)
        size = next(n for n in (64, 48, 32, 16) if rows % n == 0)

        def one(i, _):
            total = source[pl.ds(pl.multiple_of(at + i * size, 16), size), :].astype(F32)
            total = total + recv[pl.ds(pl.multiple_of(slot + i * size, 16), size), :].astype(F32)
            dest[pl.ds(pl.multiple_of(to + i * size, 16), size), :] = total.astype(BF16)
            return 0

        lax.fori_loop(0, rows // size, one, 0)

    def finish(self, p):
        for kind, s in self.steps[p]:
            if kind == "ag" or self.geometry(p, s)[3]:
                self.copy(p, (kind, s)).wait_send()


def halvings_of(rows, bits):
    made = 0
    while made < bits and (rows >> made) % 32 == 0:
        made += 1
    return made


def piece_names(width, inner):
    return ([f"ggw{g}" for g in range(width // 256)] + [f"gow{g}" for g in range(inner // 256)]
            + [f"gv{g}" for g in range(inner // 256)] + ["gsw"])


def received_rows(rows, bits):
    halvings, total = halvings_of(rows, bits), 0
    for s in range(bits):
        rows = rows // 2 if s < halvings else rows
        total += rows
    return total


def part(i, size):
    return pl.ds(pl.multiple_of(i * size, size), size)


class Refs:
    pass


NAMES_IN = ("lengths", "hid_any", "wg_any", "wv_any", "ws_any", "wo_any", "cot_any",
            "gain", "wstep", "tapv", "taps", "bias", "dlog", "skip", "ggain")
NAMES_OUT = ("block_out", "grad_hidden", "ggw_any", "gow_any", "gvw_any", "gsw_any", "tiny_any")


def layer_kernel(reach, bits, names, *refs):
    r = Refs()
    for name, ref in zip(names, refs):
        setattr(r, name, ref)
    length, width = r.hid.shape
    inner = r.wo.shape[0]
    maps = r.ws.shape[1]
    both = inner + maps
    heads = r.dlog.shape[0]
    nblk, nchunk, per = length // TB, length // Q, TB // Q
    me, core, count = lax.axis_index("seq"), lax.axis_index("head"), lax.axis_size("seq")
    base = me * length

    loads = [pltpu.make_async_copy(src, dst, r.load.at[i]) for i, (src, dst) in enumerate(
        ((r.hid_any, r.hid), (r.wv_any, r.wv), (r.ws_any, r.ws), (r.wg_any, r.wg), (r.wo_any, r.wo),
         (r.cot_any, r.cot)))]
    for load in loads:
        load.start()

    swap1 = Swap(reach, r.msgs.at[0], r.msgs.at[1], r.low1, r.high1, r.up_s.at[0], r.up_r.at[0], r.dn_s.at[0], r.dn_r.at[0])
    swap2 = Swap(reach, r.msgs.at[2], r.msgs.at[3], r.low2, r.high2, r.up_s.at[1], r.up_r.at[1], r.dn_s.at[1], r.dn_r.at[1])
    groups = inner // 256
    names = piece_names(width, inner)
    orders = [ORDERS[i % len(ORDERS)] if bits == TABLE_BITS else tuple(range(bits)) for i in range(len(names))]
    pieces = [
        dict(work=getattr(r, name + "_w"), kept=getattr(r, name + "_k"), recv=getattr(r, name + "_r"),
             out=getattr(r, name + "_o"), order=order)
        for name, order in zip(names, orders)
    ]
    of = {name: i for i, name in enumerate(names)}
    red = Reduce(bits, pieces, r.rs_s, r.rs_r, r.ag_s, r.ag_r)
    barrier = pltpu.get_barrier_semaphore()
    near = swap1.greet(barrier)
    for mate in red.mates:
        pl.semaphore_signal(barrier, inc=1, device_id=(mate, core), device_id_type=MESH)
    pl.semaphore_signal(barrier, inc=1, device_id=(me, 1 - core), device_id_type=MESH)

    def over(src, dst, sems, k):
        return pltpu.make_async_remote_copy(
            src_ref=src, dst_ref=dst, send_sem=sems.at[0, k], recv_sem=sems.at[1, k], device_id=(me, 1 - core),
            device_id_type=MESH)

    def one_sequence(j, carry):
        start, b, off0, after = carry
        end = start + r.lengths[j]
        b = jnp.where((start > base) & (start < base + length), start - base, b)
        off0 = jnp.where((start <= base) & (base < end), base - start, off0)
        after = jnp.where(end == base + length, 0, after)
        return end, b, off0, after

    _, b, off0, after = lax.fori_loop(
        0, r.lengths.shape[0], one_sequence, (jnp.int32(0), jnp.int32(length + 1), jnp.int32(0), jnp.int32(1)))
    before_f = jnp.where(off0 > 0, 1.0, 0.0)
    after_f = after.astype(F32)

    def lanes128(x):
        return jnp.concatenate([x, jnp.zeros((x.shape[0], 128 - x.shape[1]), F32)], axis=1)

    small_cols = jnp.concatenate(
        [lanes128(r.bias[...]), lanes128(r.dlog[...].reshape(1, heads)), lanes128(r.skip[...].reshape(1, heads)),
         jnp.zeros((4, 128), F32)], axis=0).T
    bias = jnp.concatenate([small_cols[:HP, 0:1], small_cols[:HP, 1:2]], axis=0)
    dlog = jnp.concatenate([small_cols[:HP, 2:3], small_cols[:HP, 2:3]], axis=0)
    spread = spread_matrix(inner, inner // heads)
    spread_low = spread.astype(BF16)
    spread2 = jnp.concatenate([spread_low, spread_low], axis=0)
    (skip,) = widen_cols(spread_low, small_cols[:HP, 3:4])
    gain = r.gain[...].reshape(1, width)
    ggain = r.ggain[...].reshape(1, inner)
    r.wst[...] = jnp.zeros_like(r.wst)
    wstep = r.wstep[...].astype(F32)
    for k in range(2):
        r.wst[k * HP : (k + 1) * HP, :] = jnp.concatenate(
            [wstep[:, k, :], jnp.zeros((HP - heads, width), F32)], axis=0).astype(BF16)

    r.tap[:, :inner] = r.tapv[...]
    r.tap[:, inner:] = r.taps[...]
    for blk in range(nblk):
        tok = iota((TB, 128), 0) + blk * TB
        for m in range(1, 4):
            r.valid[m - 1, blk * TB : (blk + 1) * TB, :] = conv_mask(tok, m, b, off0).astype(BF16)

    loads[0].wait()
    loads[1].wait()
    loads[2].wait()

    def normalize(x):
        x = x.astype(F32)
        scale = lax.rsqrt(jnp.mean(x * x, axis=1, keepdims=True) + EPSILON)
        return (x * scale * gain).astype(BF16)

    upto = (iota((Q, Q), 0) <= iota((Q, Q), 1)).astype(BF16)

    def project(blk, _):
        rows = part(blk, TB)
        normed = normalize(r.hid[rows, :])
        r.buf[rows, :] = normed
        r.normt[:, rows] = normed.T
        dest = pl.ds(pl.multiple_of(16 + blk * TB, 16), TB)
        r.joined[dest, :inner] = nn(normed, r.wv[...]).astype(BF16)
        r.joined[dest, inner:] = nn(normed, r.ws[...]).astype(BF16)
        step = nt(r.wst[...], normed)
        dt = softplus(step + bias)
        ld = -jnp.exp(dlog) * dt
        r.step[:, rows] = step
        r.dt[:, rows] = dt
        for q in range(per):
            run = exact(nn(thirds(ld[:, q * Q : (q + 1) * Q]), upto), 2 * HP)
            r.run[:, pl.ds(pl.multiple_of(blk * TB + q * Q, Q), Q)] = run
        return 0

    lax.fori_loop(0, nblk, project, 0)

    pl.semaphore_wait(barrier, near + bits + 1)

    def halo_copy(to):
        return pltpu.make_async_remote_copy(
            src_ref=r.hid.at[pl.ds(length - 16, 16)], dst_ref=r.halo, send_sem=r.edge.at[0], recv_sem=r.edge.at[1],
            device_id=(to, core), device_id_type=MESH)

    @pl.when(me + 1 < count)
    def _():
        halo_copy(me + 1).start()

    @pl.when(me == 0)
    def _():
        r.halo[...] = jnp.zeros_like(r.halo)

    def valid_of(rows, m):
        one = r.valid[m - 1, rows, :].astype(F32)
        return jnp.concatenate([one, one], axis=1)

    def chunk_parts(chunk):
        cols = part(chunk, Q)
        dt, run = r.dt[:, cols], r.run[:, cols]
        ld = -jnp.exp(dlog) * dt
        return dt, ld, run, run - ld

    def summarize(blk, _):
        rows = part(blk, TB)
        for g in range(both // 256):
            cols = slice(g * 256, (g + 1) * 256)
            r.jx[...] = r.joined[pl.ds(pl.multiple_of(blk * TB, 16), TB + 16), cols].astype(F32)
            tap = r.tap[:, cols]
            total = r.jx[16 : 16 + TB, :] * tap[3:4]
            for m in range(1, 4):
                total = total + r.jx[16 - m : 16 - m + TB, :] * valid_of(rows, m) * tap[3 - m : 4 - m]
            sig = jax.nn.sigmoid(total)
            r.act[rows, cols] = (total * sig).astype(BF16)
            r.slope[rows, cols] = (sig * (1.0 + total * (1.0 - sig))).astype(BF16)
        for q in range(per):
            chunk = blk * per + q
            t0 = chunk * Q
            at = part(chunk, Q)
            dt, ld, run, bef = chunk_parts(chunk)
            _, _, tf, tr = state_factors(dt, run, bef, t0, b)
            values = r.act[at, :inner].astype(F32)
            maps_t = r.act[at, inner:].astype(F32).T.astype(BF16)
            tfe, tre = widen(spread2, tf, tr)
            r.inc[chunk, 0:64, :] = nn(maps_t[0:64], (values * tfe).astype(BF16))
            r.inc[chunk, 64:128, :] = nn(maps_t[128:192], (values * tre).astype(BF16))
            gone = jnp.exp(run[:, Q - 1 : Q])
            pf, pr = widen_cols(spread_low, gone[:HP], gone[HP:])
            r.pexp[chunk, 0:1, :] = pf * jnp.where((t0 <= b) & (b < t0 + Q), 0.0, 1.0)
            r.pexp[chunk, 1:2, :] = pr * jnp.where((t0 < b) & (b <= t0 + Q), 0.0, 1.0)
        return 0

    lax.fori_loop(1, nblk, summarize, 0)

    @pl.when(me > 0)
    def _():
        halo_copy(me + 1).wait_recv()

    nh = normalize(r.halo[...])
    r.joined[0:16, :inner] = nn(nh, r.wv[...]).astype(BF16)
    r.joined[0:16, inner:] = nn(nh, r.ws[...]).astype(BF16)
    summarize(jnp.int32(0), 0)
    sumf, prodf = r.inc[0, 0:64, :], r.pexp[0, 0:1, :]
    sumr, prodr = r.inc[nchunk - 1, 64:128, :], r.pexp[nchunk - 1, 1:2, :]
    for c in range(1, nchunk):
        d = nchunk - 1 - c
        pf, pr = r.pexp[c, 0:1, :], r.pexp[d, 1:2, :]
        sumf, prodf = pf * sumf + r.inc[c, 0:64, :], prodf * pf
        sumr, prodr = pr * sumr + r.inc[d, 64:128, :], prodr * pr
    put_message(r.msgs.at[0], sumf, prodf * before_f)
    put_message(r.msgs.at[1], sumr, prodr * after_f)
    swap1.start()

    loads[3].wait()
    loads[4].wait()
    loads[5].wait()
    tri0, tri1 = iota((Q, Q), 0), iota((Q, Q), 1)
    lower, upper = tri0 > tri1, tri0 < tri1

    def within(blk, _):
        rows = part(blk, TB)
        r.gate[rows, :] = nn(r.buf[rows, :], r.wg[...])
        r.dy[rows, :] = nt(r.cot[rows, :], r.wo[...])
        for q in range(per):
            chunk = blk * per + q
            at = part(chunk, Q)
            t0 = chunk * Q
            dt, ld, run, bef = chunk_parts(chunk)
            ldt = jnp.log(jnp.maximum(dt, 1e-37))
            rowf = ldt[:HP] - run[:HP]
            rowr = ldt[HP:] + bef[HP:]
            cols = jnp.concatenate([bef[:HP], -run[HP:]], axis=0).T
            scores = chunk_scores(r.act[at, inner:], t0, b)
            for j in range(inner // 128):
                lanes = slice(j * 128, (j + 1) * 128)
                weights = []
                for h in (2 * j, 2 * j + 1):
                    e = jnp.where(lower, cols[:, h : h + 1] + rowf[h : h + 1],
                                  cols[:, HP + h : HP + h + 1] + rowr[h : h + 1])
                    weights.append((jnp.exp(jnp.minimum(e, 60.0)) * scores).astype(BF16))
                vp = r.act[at, lanes]
                y = nn(jnp.concatenate(weights, axis=1), halves(vp))
                r.mixed[at, lanes] = y + skip[:, lanes] * vp.astype(F32)
        return 0

    lax.fori_loop(0, nblk, within, 0)
    swap1.finish()
    hf = chain(r.low1) * before_f
    hr = chain(r.high1) * after_f
    for c in range(nchunk):
        r.state[c, 0:64, :] = hf.astype(BF16)
        hf = r.pexp[c, 0:1, :] * hf + r.inc[c, 0:64, :]
        d = nchunk - 1 - c
        r.state[d, 64:128, :] = hr.astype(BF16)
        hr = r.pexp[d, 1:2, :] * hr + r.inc[d, 64:128, :]

    def enter(blk, _):
        lane = iota((Q, 128), 1)
        u_all = r.dy[part(blk, TB), :]
        for q in range(per):
            chunk = blk * per + q
            at = part(chunk, Q)
            dt, ld, run, bef = chunk_parts(chunk)
            ef, er, _, _ = state_factors(dt, run, bef, chunk * Q, b)
            maps_here = r.act[at, inner:]
            state = r.state[chunk]
            efe, ere = widen(spread2, ef, er)
            ys = nn(maps_here[:, 64:128], state[0:64]) * efe + nn(maps_here[:, 192:256], state[64:128]) * ere
            square = jnp.zeros((Q, 128), F32)
            cross = jnp.zeros((Q, 128), F32)
            for j in range(inner // 128):
                lanes = slice(j * 128, (j + 1) * 128)
                y = r.mixed[at, lanes] + ys[:, lanes]
                r.mixed[at, lanes] = y
                gated = y * silu(r.gate[at, lanes])
                square = square + gated * gated
                cross = cross + gated * (u_all[q * Q : (q + 1) * Q, lanes] * ggain[:, lanes])
            square = jnp.sum(square, axis=1, keepdims=True)
            cross = jnp.sum(cross, axis=1, keepdims=True)
            two = jnp.where(lane == 0, square, jnp.where(lane == 1, cross, 0.0))
            r.mine[blk, :, q * Q : (q + 1) * Q] = two.T[0:8]
        over(r.mine.at[blk], r.other.at[blk], r.sum_sem, blk).start()
        return 0

    lax.fori_loop(0, nblk, enter, 0)
    r.small[...] = jnp.zeros_like(r.small)

    def gating(blk, _):
        rows = part(blk, TB)
        over(r.mine.at[blk], r.other.at[blk], r.sum_sem, blk).wait()
        sums = r.mine[blk] + r.other[blk]
        sums = jnp.concatenate([sums, jnp.zeros((120, TB), F32)], axis=0).T
        scale = lax.rsqrt(sums[:, 0:1] / (2 * inner) + EPSILON)
        back = scale * scale * scale * sums[:, 1:2] / (2 * inner)
        for j in range(inner // 128):
            lanes = slice(j * 128, (j + 1) * 128)
            mixed = r.mixed[rows, lanes]
            pre = r.gate[rows, lanes]
            sig = jax.nn.sigmoid(pre)
            gated = mixed * (pre * sig)
            ng = gated * scale
            r.buf[rows, lanes] = (ng * ggain[:, lanes]).astype(BF16)
            g = r.dy[rows, lanes]
            r.small[0:1, lanes] += jnp.sum(g * ng, axis=0, keepdims=True)
            grad_gated = scale * (g * ggain[:, lanes]) - gated * back
            dy = grad_gated * (pre * sig)
            r.small[1:2, lanes] += jnp.sum(dy * r.act[rows, lanes].astype(F32), axis=0, keepdims=True)
            r.dy[rows, lanes] = dy
            r.ggate[rows, lanes] = (grad_gated * mixed * (sig * (1.0 + pre * (1.0 - sig)))).astype(BF16)
        for q in range(per):
            chunk = blk * per + q
            at = part(chunk, Q)
            dt, ld, run, bef = chunk_parts(chunk)
            ef, er, _, _ = state_factors(dt, run, bef, chunk * Q, b)
            maps_t = r.act[at, inner:].astype(F32).T.astype(BF16)
            dy = r.dy[at, :]
            efe, ere = widen(spread2, ef, er)
            r.inc[chunk, 0:64, :] = nn(maps_t[64:128], (dy * efe).astype(BF16))
            r.inc[chunk, 64:128, :] = nn(maps_t[192:256], (dy * ere).astype(BF16))
        return 0

    lax.fori_loop(0, nblk, gating, 0)
    sumf, sumr = r.inc[nchunk - 1, 0:64, :], r.inc[0, 64:128, :]
    for c in range(1, nchunk):
        d = nchunk - 1 - c
        sumf = r.pexp[d, 0:1, :] * sumf + r.inc[d, 0:64, :]
        sumr = r.pexp[c, 1:2, :] * sumr + r.inc[c, 64:128, :]
    put_message(r.msgs.at[2], sumr * after_f, prodr * after_f)
    put_message(r.msgs.at[3], sumf * before_f, prodf * before_f)
    swap2.start()
    for g in range(width // 256):
        pieces[of[f"ggw{g}"]]["work"][...] = nn(r.normt[g * 256 : (g + 1) * 256, :], r.ggate[...]).astype(BF16)
        red.start(of[f"ggw{g}"])
    for g in range(groups):
        pieces[of[f"gow{g}"]]["work"][...] = tn(r.buf[:, g * 256 : (g + 1) * 256], r.cot[...]).astype(BF16)
        red.start(of[f"gow{g}"])

    def project_out(blk, _):
        rows = part(blk, TB)
        r.out_mine[rows, :] = nn(r.buf[rows, :], r.wo[...]).astype(BF16)
        over(r.out_mine.at[rows], r.out_other.at[rows], r.out_sem, blk).start()
        return 0

    lax.fori_loop(0, nblk, project_out, 0)

    sums_low = jnp.concatenate([lower, upper], axis=1).astype(BF16)
    diag = tri0 == tri1
    r.rowbuf[...] = jnp.zeros_like(r.rowbuf)

    taken_within = red.takes("within", nchunk)

    def back_within(blk, _):
        for q in range(per):
            chunk = blk * per + q
            at = part(chunk, Q)
            t0 = chunk * Q
            dt, ld, run, bef = chunk_parts(chunk)
            ldt = jnp.log(jnp.maximum(dt, 1e-37))
            cols = jnp.concatenate([ldt[:HP] - run[:HP], ldt[HP:] + bef[HP:]], axis=0).T
            rowf, rowr = bef[:HP], -run[HP:]
            m = r.act[at, inner:]
            entf, readf, entr, readr = m[:, 0:64], m[:, 64:128], m[:, 128:192], m[:, 192:256]
            same = (tri0 + t0 < b) == (tri1 + t0 < b)
            okf, okr = upper & same, lower & same
            scores = jnp.where(okf, nt(entf, readf), jnp.where(okr, nt(entr, readr), 0.0))
            dscore = jnp.zeros((Q, Q), F32)
            for j in range(inner // 128):
                lanes = slice(j * 128, (j + 1) * 128)
                vp = r.act[at, lanes]
                dyp32 = r.dy[at, lanes]
                dyp = dyp32.astype(BF16)
                dw = nt(halves(vp), dyp)
                weights = []
                for i, h in enumerate((2 * j, 2 * j + 1)):
                    e = jnp.where(upper, cols[:, h : h + 1] + rowf[h : h + 1],
                                  cols[:, HP + h : HP + h + 1] + rowr[h : h + 1])
                    x = jnp.exp(jnp.minimum(e, 60.0))
                    weights.append((x * scores).astype(BF16))
                    dwx = dw[i * Q : (i + 1) * Q] * x
                    dscore = dscore + dwx
                    sums = nn((dwx * scores).astype(BF16), sums_low)
                    pf, pr = sums[:, :Q], sums[:, Q:]
                    for place, kept in enumerate((jnp.where(upper, pf, 0.0), jnp.where(lower, pr, 0.0),
                                                  jnp.where(diag, pf, 0.0), jnp.where(diag, pr, 0.0))):
                        r.rowbuf[chunk, place * HP + h : place * HP + h + 1, :] = jnp.sum(kept, axis=0, keepdims=True)
                dv = nn(jnp.concatenate(weights, axis=1), halves(dyp))
                r.mixed[at, lanes] = dv + dyp32 * skip[:, lanes]
            dsf = jnp.where(okf, dscore, 0.0)
            dsr = jnp.where(okr, dscore, 0.0)
            r.mixed[at, inner:] = jnp.concatenate(
                [nn(dsf.astype(BF16), readf), nn(dsf.T.astype(BF16), entf),
                 nn(dsr.astype(BF16), readr), nn(dsr.T.astype(BF16), entr)], axis=1)
            red.hook(blk, taken_within, per, q)
        return 0

    lax.fori_loop(0, nblk, back_within, 0)
    swap2.finish()
    df = chain(r.high2)
    dr = chain(r.low2)
    for c in range(nchunk):
        d = nchunk - 1 - c
        r.dstate[d, 0:64, :] = df.astype(BF16)
        df = r.pexp[d, 0:1, :] * df + r.inc[d, 0:64, :]
        r.dstate[c, 64:128, :] = dr.astype(BF16)
        dr = r.pexp[c, 1:2, :] * dr + r.inc[c, 64:128, :]
    r.cg_mine[...] = jnp.zeros_like(r.cg_mine)
    r.hsum[...] = jnp.zeros_like(r.hsum)

    def lent_copy(to):
        return pltpu.make_async_remote_copy(
            src_ref=r.lent_mine, dst_ref=r.lent_other, send_sem=r.edge.at[2], recv_sem=r.edge.at[3],
            device_id=(to, core), device_id_type=MESH)

    lower_low, upper_low = lower.astype(BF16), upper.astype(BF16)

    taken_states = red.takes("states", nchunk)

    def back_states(blk, _):
        for q in range(per):
            chunk = blk * per + q
            at = part(chunk, Q)
            dt, ld, run, bef = chunk_parts(chunk)
            ef, er, tf, tr = state_factors(dt, run, bef, chunk * Q, b)
            m = r.act[at, inner:]
            entf, readf, entr, readr = m[:, 0:64], m[:, 64:128], m[:, 128:192], m[:, 192:256]
            state = r.state[chunk]
            grad_state = r.dstate[chunk]
            dy = r.dy[at, :]
            values = r.act[at, :inner].astype(F32)
            efe, ere, tfe, tre = widen(spread2, ef, er, tf, tr)
            dyf, dyr = dy * efe, dy * ere
            dreadf = nt(dyf.astype(BF16), state[0:64])
            dreadr = nt(dyr.astype(BF16), state[64:128])
            qf = nt(spread_low, (nn(readf, state[0:64]) * dyf).astype(BF16))
            qr = nt(spread_low, (nn(readr, state[64:128]) * dyr).astype(BF16))
            dvf = nn(entf, grad_state[0:64]) * tfe
            dvr = nn(entr, grad_state[64:128]) * tre
            wf = nt(spread_low, (values * dvf).astype(BF16))
            wr = nt(spread_low, (values * dvr).astype(BF16))
            dentf = nt((values * tfe).astype(BF16), grad_state[0:64])
            dentr = nt((values * tre).astype(BF16), grad_state[64:128])
            through = state.astype(F32) * grad_state.astype(F32)
            zf = jnp.sum(through[0:64], axis=0, keepdims=True) * r.pexp[chunk, 0:1, :]
            zr = jnp.sum(through[64:128], axis=0, keepdims=True) * r.pexp[chunk, 1:2, :]
            through = jnp.concatenate([zf, zr, jnp.zeros((6, inner), F32)], axis=0)
            through = exact(nt(thirds(through), spread_low), 8)
            through = jnp.concatenate([through, jnp.zeros((120, HP), F32)], axis=0).T
            zf, zr = through[:, 0:1], through[:, 1:2]
            r.mixed[at, :inner] = r.mixed[at, :inner] + dvf + dvr
            r.mixed[at, inner:] = r.mixed[at, inner:] + jnp.concatenate([dentf, dreadf, dentr, dreadr], axis=1)
            late = exact(nn(thirds(jnp.concatenate([qf, wr], axis=0)), lower_low), 2 * HP)
            early = exact(nn(thirds(jnp.concatenate([wf, qr], axis=0)), upper_low), 2 * HP)
            rowsum = r.rowbuf[chunk]
            dld = jnp.concatenate(
                [rowsum[0:HP] + late[:HP] + early[:HP] + zf, rowsum[HP : 2 * HP] + late[HP:] + early[HP:] + zr], axis=0)
            dldt = rowsum[2 * HP : 4 * HP] + jnp.concatenate([wf, wr], axis=0)
            sig = jax.nn.sigmoid(r.step[:, at] + bias)
            ratio = jnp.where(dt < 1e-30, 1.0, sig / jnp.maximum(dt, 1e-30))
            graw = dldt * ratio - jnp.exp(dlog) * sig * dld
            r.gstep[:, at] = graw.astype(BF16)
            r.hsum[:, 0:1] += jnp.sum(graw, axis=1, keepdims=True)
            r.hsum[:, 1:2] += jnp.sum(dld * ld, axis=1, keepdims=True)
            red.hook(blk, taken_states, per, q)

        @pl.when(blk == 0)
        def _():
            tok8 = iota((8, 1), 0)
            tap = r.tap[...]
            dconv = r.mixed[0:8, :] * r.slope[0:16, :].astype(F32)[0:8]
            rows = r.joined[0:16, :].astype(F32)[8:16]
            lent = jnp.zeros((8, both), F32)
            for m in range(1, 4):
                first = jnp.concatenate([jnp.zeros((8, both), F32), dconv * conv_mask(tok8, m, b, off0)], axis=0)
                first = first[m : m + 8]
                lent = lent + first * tap[3 - m : 4 - m]
                r.cg_mine[3 - m : 4 - m, :] = jnp.sum(first * rows, axis=0, keepdims=True)
            r.lent_mine[...] = lent

            @pl.when(me > 0)
            def _():
                lent_copy(me - 1).start()

        return 0

    lax.fori_loop(0, nblk, back_states, 0)

    @pl.when(me + 1 < count)
    def _():
        lent_copy(me - 1).wait_recv()

    @pl.when(me + 1 == count)
    def _():
        r.lent_other[...] = jnp.zeros_like(r.lent_other)

    def back_conv(g):
        cols = slice(g * 256, (g + 1) * 256)
        r.ext[...] = jnp.zeros_like(r.ext)
        taken = red.takes(f"conv{g}_", nblk)

        def one(i, _):
            blk = nblk - 1 - i
            rows = part(blk, TB)
            tap = r.tap[:, cols]
            x = r.joined[pl.ds(pl.multiple_of(16 + blk * TB, 16), TB), cols].astype(F32)
            dconv = r.mixed[rows, cols] * r.slope[rows, cols].astype(F32)
            grad = dconv * tap[3:4]
            r.cg_mine[3:4, cols] += jnp.sum(dconv * x, axis=0, keepdims=True)
            for m in range(1, 4):
                r.ext[m - 1, TB : TB + 8, :] = r.ext[m - 1, 0:8, :]
                r.ext[m - 1, 0:TB, :] = dconv * valid_of(rows, m)
                moved = r.ext[m - 1, m : m + TB, :]
                r.cg_mine[3 - m : 4 - m, cols] += jnp.sum(moved * x, axis=0, keepdims=True)
                grad = grad + moved * tap[3 - m : 4 - m]
            last = jnp.where(blk == nblk - 1, 1.0, 0.0)
            grad = jnp.concatenate([grad[: TB - 8], grad[TB - 8 :] + r.lent_other[:, cols] * last], axis=0)
            if g * 256 < inner:
                r.buf[rows, cols] = grad.astype(BF16)
            else:
                r.gs_mine[rows, :] = grad.astype(BF16)
            red.hook(i, taken)
            return 0

        lax.fori_loop(0, nblk, one, 0)

    back_conv(inner // 256)
    gs_copy = over(r.gs_mine, r.gs_other, r.misc_sem, 0)
    gs_copy.start()
    cg_copy = over(r.cg_mine.at[:, pl.ds(inner, maps)], r.cg_other, r.misc_sem, 1)
    cg_copy.start()
    def finish_maps():
        gs_copy.wait()
        cg_copy.wait()
        r.gs_mine[...] = (r.gs_mine[...].astype(F32) + r.gs_other[...].astype(F32)).astype(BF16)
        half = r.gs_mine[:, pl.ds(pl.multiple_of(core * 128, 128), 128)]
        r.gsw_w[:, 0:128] = nn(r.normt[...], half).astype(BF16)
        gstep = jnp.concatenate([r.gstep[...].astype(F32), jnp.zeros((128 - 2 * HP, length), F32)], axis=0)
        r.gsw_w[:, 128:256] = nt(r.normt[...], gstep.astype(BF16)).astype(BF16)
        red.start(of["gsw"])

    for g in range(groups):
        cols = slice(g * 256, (g + 1) * 256)
        back_conv(g)
        pieces[of[f"gv{g}"]]["work"][...] = nn(r.normt[...], r.buf[:, cols]).astype(BF16)
        red.start(of[f"gv{g}"])
        if g == 0:
            finish_maps()

    taken_down = red.takes("down", nblk)

    def down(blk, _):
        rows = part(blk, TB)
        gn = nt(r.ggate[rows, :], r.wg[...]) + nt(r.buf[rows, :], r.wv[...]) + tn(r.gstep[:, rows], r.wst[...])
        r.gn_mine[rows, :] = gn.astype(BF16)
        over(r.gn_mine.at[rows], r.gn_other.at[rows], r.gn_sem, blk).start()
        red.hook(blk, taken_down)
        return 0

    lax.fori_loop(0, nblk, down, 0)
    tiny = r.tiny_w.at[0]
    tiny[...] = jnp.zeros((8, both), F32)
    tiny[0:2, :inner] = r.small[0:2, :]
    head_sums = r.hsum[...].T
    tiny[3:4, 0 : 2 * HP] = head_sums[0:1]
    tiny[3:4, 128 : 128 + 2 * HP] = head_sums[1:2]
    tiny[4:8, :inner] = r.cg_mine[0:4, :inner]
    tiny[4:8, inner:] = r.cg_mine[0:4, inner:] + r.cg_other[0:4, :]

    def out_copy(blk):
        rows = part(blk, TB)
        return (pltpu.make_async_copy(r.out_other.at[rows], r.block_out.at[rows], r.store.at[0, blk]),
                pltpu.make_async_copy(r.gate.at[rows], r.grad_hidden.at[rows], r.store.at[1, blk]))

    taken_end = red.takes("end", nblk)

    def ending(blk, _):
        rows = part(blk, TB)
        over(r.out_mine.at[rows], r.out_other.at[rows], r.out_sem, blk).wait()
        over(r.gn_mine.at[rows], r.gn_other.at[rows], r.gn_sem, blk).wait()
        x = r.hid[rows, :].astype(F32)
        r.out_other[rows, :] = (
            x + (r.out_mine[rows, :].astype(F32) + r.out_other[rows, :].astype(F32))).astype(BF16)
        gn = r.gn_mine[rows, :].astype(F32) + r.gn_other[rows, :].astype(F32) + nt(r.gs_mine[rows, :], r.ws[...])
        scale = lax.rsqrt(jnp.mean(x * x, axis=1, keepdims=True) + EPSILON)
        tiny[2:3, :width] += jnp.sum(gn * x * scale, axis=0, keepdims=True)
        v = gn * gain
        mean = jnp.mean(x * v, axis=1, keepdims=True)
        r.gate[rows, :] = r.cot[rows, :].astype(F32) + scale * v - x * (scale * scale * scale * mean)
        for copy in out_copy(blk):
            copy.start()
        red.hook(blk, taken_end)
        return 0

    lax.fori_loop(0, nblk, ending, 0)

    def tiny_copy(s):
        return pltpu.make_async_remote_copy(
            src_ref=r.tiny_w.at[s], dst_ref=r.tiny_r.at[s], send_sem=r.tiny_sem.at[0, s],
            recv_sem=r.tiny_sem.at[1, s], device_id=(red.mates[s], core), device_id_type=MESH)

    halves_copy = over(r.gsw_o.at[:, pl.ds(0, 128)], r.gsx, r.misc_sem, 2)
    stores = []

    def store(src, dst):
        copy = pltpu.make_async_copy(src, dst, r.store.at[2, len(stores)])
        copy.start()
        stores.append(copy)

    def settle(p):
        red.finish(p)
        name, out = names[p], pieces[p]["out"]
        if name == "gsw":
            halves_copy.start()
            return
        kind, at = name[:-1], pl.ds(int(name[-1]) * 256, 256)
        store(out, r.ggw_any.at[at] if kind == "ggw" else r.gow_any.at[at] if kind == "gow" else r.gvw_any.at[:, at])

    for p in range(len(pieces)):
        if red.pos[p] == len(red.steps[p]):
            settle(p)
    tiny_copy(0).start()
    rest, turns = red.left(), 0
    for i, (p, at) in enumerate(rest):
        red.step(p, at)
        if at == len(red.steps[p]) - 1:
            settle(p)
        while turns < bits and (turns + 1) * len(rest) <= (i + 1) * (bits + 1) or i + 1 == len(rest) and turns < bits:
            tiny_copy(turns).wait()
            r.tiny_w[turns + 1] = r.tiny_w[turns] + r.tiny_r[turns]
            turns += 1
            if turns < bits:
                tiny_copy(turns).start()
    store(r.tiny_w.at[bits], r.tiny_any)
    halves_copy.wait()
    mine_at, other_at = pl.multiple_of(core * 128, 128), pl.multiple_of((1 - core) * 128, 128)
    store(r.gsw_o.at[:, pl.ds(0, 128)], r.gsw_any.at[:, pl.ds(mine_at, 128)])
    store(r.gsx, r.gsw_any.at[:, pl.ds(other_at, 128)])
    store(r.gsw_o.at[:, pl.ds(128, 128)], r.gsw_any.at[:, pl.ds(256, 128)])
    for copy in stores:
        copy.wait()
    for blk in range(nblk):
        for copy in out_copy(blk):
            copy.wait()

    @pl.when(me + 1 < count)
    def _():
        halo_copy(me + 1).wait_send()

    @pl.when(me > 0)
    def _():
        lent_copy(me - 1).wait_send()


TABLE_BITS = 4
ORDERS = (
    (0, 1, 2, 3),
    (0, 1, 2, 3),
    (3, 1, 0, 2),
    (1, 2, 3, 0),
    (2, 0, 1, 3),
    (1, 0, 3, 2),
    (2, 0, 1, 3),
    (1, 2, 0, 3),
    (2, 0, 1, 3),
    (0, 1, 3, 2),
)
TABLE = {
    "within3": (
        (0, 0),
    ),
    "within4": (
        (1, 0), (3, 0), (2, 0), (4, 0), (5, 0),
    ),
    "within7": (
        (0, 1), (3, 1),
    ),
    "states0": (
        (4, 1), (5, 1), (1, 1), (2, 1),
    ),
    "states1": (
        (0, 2), (3, 2),
    ),
    "states2": (
        (2, 2), (4, 2),
    ),
    "states3": (
        (1, 2), (3, 3), (5, 2),
    ),
    "states4": (
        (0, 3), (2, 3), (4, 3),
    ),
    "states5": (
        (3, 4), (1, 3), (5, 3),
    ),
    "states7": (
        (2, 4), (0, 4), (4, 4),
    ),
    "conv3_1": (
        (5, 4),
    ),
    "conv3_2": (
        (1, 4),
    ),
    "conv0_0": (
        (3, 5),
    ),
    "conv0_1": (
        (2, 5), (4, 5), (0, 5),
    ),
    "conv1_0": (
        (5, 5), (1, 5),
    ),
    "conv1_2": (
        (4, 6),
    ),
    "conv1_3": (
        (3, 6),
    ),
    "conv2_1": (
        (0, 6), (2, 6),
    ),
    "down1": (
        (1, 6), (5, 6), (6, 0),
    ),
    "down3": (
        (9, 0),
    ),
    "tail": (
        (4, 7), (3, 7), (0, 7), (7, 0), (6, 1), (2, 7), (8, 0), (1, 7), (9, 1), (7, 1), (6, 2), (5, 7),
        (8, 1), (7, 2), (9, 2), (6, 3), (8, 2), (7, 3), (9, 3), (6, 4), (8, 3), (7, 4), (9, 4), (6, 5),
        (7, 5), (8, 4), (9, 5), (6, 6), (8, 5), (7, 6), (9, 6), (8, 6), (6, 7), (7, 7), (9, 7), (8, 7),
    ),
}


def last_kernel(heads, ggw_ref, gow_ref, gvw_ref, gsw_ref, tiny_ref, out_ref, gh_ref,
                ngain_ref, ggwo_ref, gvwo_ref, gswo_ref, gsteo_ref, convv_ref, convs_ref, bias_ref, decay_ref,
                skip_ref, ggain_ref, gowo_ref, outo_ref, gho_ref):
    outo_ref[...] = out_ref[...]
    gho_ref[...] = gh_ref[...]
    ggwo_ref[...] = ggw_ref[...].astype(F32)
    gvwo_ref[...] = gvw_ref[...].astype(F32)
    maps = gswo_ref.shape[1]
    gswo_ref[...] = gsw_ref[:, :maps].astype(F32)
    step = gsw_ref[:, maps:].astype(F32).T
    gsteo_ref[...] = jnp.stack([step[:heads], step[HP : HP + heads]], axis=1)
    gowo_ref[...] = gow_ref[...].astype(F32)

    @pl.when(pl.program_id(0) == 0)
    def _():
        width, inner = ngain_ref.shape[0], convv_ref.shape[1]
        ngain_ref[...] = tiny_ref[2, :width]
        ggain_ref[...] = tiny_ref[0, :inner]
        convv_ref[...] = tiny_ref[4:8, :inner]
        convs_ref[...] = tiny_ref[4:8, inner:]
        bias_ref[...] = jnp.concatenate([tiny_ref[3:4, 0:heads], tiny_ref[3:4, HP : HP + heads]], axis=0)
        decay_ref[...] = (tiny_ref[3:4, 128 : 128 + heads] + tiny_ref[3:4, 128 + HP : 128 + HP + heads]).reshape(heads)
        spread = spread_matrix(inner, inner // heads)
        total = nt(jnp.broadcast_to(tiny_ref[1:2, :inner], (8, inner)), spread, HIGHEST)
        skip_ref[...] = total[0:1, :heads].reshape(heads)


SMEM_SPEC = pl.BlockSpec(memory_space=pltpu.SMEM)
VMEM_SPEC = pl.BlockSpec(memory_space=pltpu.VMEM)
ANY_SPEC = pl.BlockSpec(memory_space=pl.ANY)


def body(
    hidden_in, norm_gain, gate_proj, value_proj, state_proj, step_proj, conv_value, conv_state,
    step_bias, decay_log, skip_scale, gate_gain, out_proj, lengths, cotangent,
):
    length, width = hidden_in.shape
    inner = gate_proj.shape[1]
    heads = decay_log.shape[0]
    maps = state_proj.shape[1]
    both = inner + maps
    nblk, nchunk = length // TB, length // Q
    count = lax.axis_size("seq")
    bits = count.bit_length() - 1
    assert count == 1 << bits
    reach = min(1 + (LEN_MOST - 2) // length, count - 1)
    npieces = len(piece_names(width, inner))

    def vmem(*dims, dtype=F32):
        return pltpu.VMEM(dims, dtype)

    dma = pltpu.SemaphoreType.DMA
    low = dict(dtype=BF16)
    scratch = dict(
        hid=vmem(length, width, **low), wg=vmem(width, inner, **low), wv=vmem(width, inner, **low),
        ws=vmem(width, maps, **low), wo=vmem(inner, width, **low), cot=vmem(length, width, **low),
        wst=vmem(2 * HP, width, **low), tap=vmem(4, both),
        normt=vmem(width, length, **low), buf=vmem(length, inner, **low), gate=vmem(length, inner),
        joined=vmem(16 + length, both, **low), act=vmem(length, both, **low), step=vmem(2 * HP, length), dt=vmem(2 * HP, length), run=vmem(2 * HP, length),
        inc=vmem(nchunk, 128, inner), pexp=vmem(nchunk, 2, inner), mixed=vmem(length, both),
        state=vmem(nchunk, 128, inner, **low), dstate=vmem(nchunk, 128, inner, **low),
        dy=vmem(length, inner), ggate=vmem(length, inner, **low), gstep=vmem(2 * HP, length, **low),
        msgs=vmem(4, 80, inner, **low),
        low1=vmem(reach, 80, inner, **low), high1=vmem(reach, 80, inner, **low),
        low2=vmem(reach, 80, inner, **low), high2=vmem(reach, 80, inner, **low),
        rowbuf=vmem(nchunk, 4 * HP, Q), jx=vmem(TB + 16, 256), ext=vmem(3, TB + 8, 256),
        valid=vmem(3, length, 128, **low), slope=vmem(length, both, **low), gsx=vmem(width, 128, **low),
        halo=vmem(16, width, **low), mine=vmem(nblk, 8, TB), other=vmem(nblk, 8, TB),
        out_mine=vmem(length, width, **low), out_other=vmem(length, width, **low),
        gn_mine=vmem(length, width, **low), gn_other=vmem(length, width, **low),
        gs_mine=vmem(length, maps, **low), gs_other=vmem(length, maps, **low),
        lent_mine=vmem(8, both), lent_other=vmem(8, both), cg_mine=vmem(8, both), cg_other=vmem(8, maps),
        hsum=vmem(2 * HP, 128), small=vmem(8, inner),
        tiny_w=vmem(bits + 1, 8, both), tiny_r=vmem(bits, 8, both),
    )
    for name in piece_names(width, inner):
        rows, cols = (256, width) if name[:3] in ("ggw", "gow") else (width, 256)
        scratch[name + "_w"] = vmem(rows, cols, **low)
        scratch[name + "_k"] = vmem(rows // 2, cols, **low)
        scratch[name + "_r"] = vmem(received_rows(rows, bits), cols, **low)
        scratch[name + "_o"] = vmem(rows, cols, **low)
    scratch.update(
        load=dma((6,)), store=dma((3, npieces + nblk)), edge=dma((4,)), sum_sem=dma((2, nblk)), out_sem=dma((2, nblk)),
        gn_sem=dma((2, nblk)), misc_sem=dma((2, 3)), tiny_sem=dma((2, bits)),
        up_s=dma((2, reach)), up_r=dma((2, reach)), dn_s=dma((2, reach)), dn_r=dma((2, reach)),
        rs_s=dma((npieces, bits)), rs_r=dma((npieces, bits)), ag_s=dma((npieces, bits)), ag_r=dma((npieces, bits)),
    )

    def shape(*dims, dtype=F32):
        return jax.ShapeDtypeStruct(dims, dtype)

    outs = pl.pallas_call(
        partial(layer_kernel, reach, bits, NAMES_IN + NAMES_OUT + tuple(scratch)),
        in_specs=[SMEM_SPEC] + [ANY_SPEC] * 6 + [VMEM_SPEC] * 8,
        out_specs=[ANY_SPEC] * 7,
        out_shape=[shape(length, width, **low), shape(length, width), shape(width, inner, **low),
                   shape(inner, width, **low), shape(width, inner, **low), shape(width, maps + 128, **low),
                   shape(8, both)],
        scratch_shapes=list(scratch.values()),
        compiler_params=pltpu.CompilerParams(
            collective_id=1, has_side_effects=True, vmem_limit_bytes=VMEM_LIMIT),
    )(lengths, hidden_in, gate_proj, value_proj, state_proj, out_proj, cotangent,
      norm_gain, step_proj.transpose(2, 0, 1), conv_value, conv_state, step_bias, decay_log, skip_scale, gate_gain)
    block_out, grad_hidden, ggw, gow, gvw, gsw, tiny = outs

    rows = 384
    def tall(cols):
        return pl.BlockSpec((rows, cols), lambda i: (i, 0))

    def whole(*dims):
        return pl.BlockSpec(dims, lambda i: (0,) * len(dims))

    steps = width // rows
    tokens = pl.BlockSpec((length // steps, width), lambda i: (i, 0))
    assert width % rows == 0 and length % steps == 0 and inner % rows == 0 and inner == width
    final = pl.pallas_call(
        partial(last_kernel, heads),
        grid=(width // rows,),
        in_specs=[tall(inner), tall(width), tall(inner), tall(maps + 128), whole(8, both), tokens, tokens],
        out_specs=[whole(width), tall(inner), tall(inner), tall(maps), pl.BlockSpec((heads, 2, rows), lambda i: (0, 0, i)), whole(4, inner),
                   whole(4, maps), whole(2, heads), whole(heads), whole(heads), whole(inner), tall(width), tokens, tokens],
        out_shape=[shape(width), shape(width, inner), shape(width, inner), shape(width, maps),
                   shape(heads, 2, width), shape(4, inner), shape(4, maps), shape(2, heads), shape(heads),
                   shape(heads), shape(inner), shape(inner, width), shape(length, width, **low), shape(length, width)],
        compiler_params=pltpu.CompilerParams(dimension_semantics=("arbitrary",), vmem_limit_bytes=60 * MIB),
    )(ggw, gow, gvw, gsw, tiny, block_out, grad_hidden)
    ngain, ggw, gvw, gsw, gstepw, convv, convs, bias, decay, skip, ggain, gow, block_out, grad_hidden = final
    return (block_out, grad_hidden, ngain, ggw, gvw, gsw, gstepw.transpose(1, 2, 0), convv, convs, bias, decay, skip,
            ggain, gow)


def solution(mesh):
    in_specs = (
        P("seq", None),
        P(),
        P(None, "head"),
        P(None, "head"),
        P(),
        P(None, None, "head"),
        P(None, "head"),
        P(),
        P(None, "head"),
        P("head"),
        P("head"),
        P("head"),
        P("head", None),
        P(),
        P("seq", None),
    )
    out_specs = (
        P("seq", None),
        P("seq", None),
        P(),
        P(None, "head"),
        P(None, "head"),
        P(),
        P(None, None, "head"),
        P(None, "head"),
        P(),
        P(None, "head"),
        P("head"),
        P("head"),
        P("head"),
        P("head", None),
    )
    return jax.shard_map(body, mesh=mesh, in_specs=in_specs, out_specs=out_specs, check_vma=False)
```
